32 devices in a mesh: dp: 8 (over z, y), tensor: 4 (over x, core).
Axes of the slice: x: 2, y: 2, z: 4, core: 2. Of those that a mesh axis runs over, the one named last changes fastest.
Arguments:
- frames: bfloat16 [64, 13, 13, 512], P('dp', None, None, 'tensor'), may hold values from -10 to 10
- item_mask: int32 [64], P('dp'), may hold values 0 or 1
- weights: float32 [2, 4608, 512], P(None, 'dp', 'tensor'), may hold values from -0.09375 to 0.09375
- biases: float32 [2, 512], replicated, may hold values from -0.4 to 0.4
- cotangent: bfloat16 [64, 13, 13, 512], P('dp', None, None, 'tensor'), may hold values from -8 to 8
- weight_first: float32 [2, 4608, 512], P(None, 'dp', 'tensor'), may hold values from -0.0018412241 to 0.0018412241
- weight_second: float32 [2, 4608, 512], P(None, 'dp', 'tensor'), may hold values from 1.0594082e-07 to 1.6950531e-06
- bias_first: float32 [2, 512], replicated, may hold values from -0.0018412241 to 0.0018412241
- bias_second: float32 [2, 512], replicated, may hold values from 1.0594082e-07 to 1.6950531e-06
Outputs:
- act4: bfloat16 [64, 13, 13, 512], P('dp', None, None, 'tensor')
- act5: bfloat16 [64, 13, 13, 512], P('dp', None, None, 'tensor')
- input_grad: float32 [64, 13, 13, 512], P('dp', None, None, 'tensor')
- grad_norm: float32 [], replicated
- new_weights: float32 [2, 4608, 512], P(None, 'dp', 'tensor')
- new_weight_first: float32 [2, 4608, 512], P(None, 'dp', 'tensor')
- new_weight_second: float32 [2, 4608, 512], P(None, 'dp', 'tensor')
- new_biases: float32 [2, 512], replicated
- new_bias_first: float32 [2, 512], replicated
- new_bias_second: float32 [2, 512], replicated
The draws below stay inside these ranges and needn't reach their ends.
All inputs are finite; a program needn't handle non-finite values. No bound on the sum of `item_mask` on one device may be relied on, other than what follows from the above.
Results may differ from the reference program's by a relative error of at most 0.0086.
Values may be sent and summed in bfloat16 or wider, within the bound.
A program may use at most 128 MiB of HBM per device.

```python
import math
import jax
import jax.numpy as jnp
from jax import lax

C = 512
H = 13
W = 13
ITEMS_DEV = 8
STEP = 5
ITEMS = 64
KIN = 4608


def draw_frames(key, part):
    key = jax.random.fold_in(key, 11)
    ramp = jnp.arange(C, dtype=jnp.float32) / (C - 1)
    values = jnp.clip(jax.random.normal(key, (ITEMS, H, W, C), jnp.float32), -4.0, 4.0)
    return (values * (1.0 + 1.5 * ramp)).astype(jnp.bfloat16)


def draw_cotangent(key, part):
    key = jax.random.fold_in(key, 23)
    ramp = jnp.arange(C, dtype=jnp.float32) / (C - 1)
    values = jnp.clip(jax.random.normal(key, (ITEMS, H, W, C), jnp.float32), -4.0, 4.0)
    return (values * (1.0 + 0.8 * ramp)).astype(jnp.bfloat16)


def with_ends(result, own_key, least, largest):
    place = [jax.random.randint(jax.random.fold_in(own_key, axis), (), 0, length) for axis, length in enumerate(result.shape)]
    widest = result.shape.index(max(result.shape))
    neighbour = place[:widest] + [(place[widest] + 1) % result.shape[widest]] + place[widest + 1:]
    return result.at[tuple(place)].set(least).at[tuple(neighbour)].set(largest)


def levels(stream_key, dims, split, smallest, largest):
    loudness, own = 1.0, jax.random.fold_in(stream_key, 6)
    for dim, blocks in split:
        heights = jnp.exp(jax.random.uniform(jax.random.fold_in(own, dim), (blocks,), jnp.float32, smallest / len(split), largest / len(split)))
        loudness = loudness * jnp.repeat(heights, dims[dim] // blocks).reshape([-1 if axis == dim else 1 for axis in range(len(dims))])
    return loudness


def bell_draw(rng, extent, deviation, bound, shards=(), held_as=jnp.bfloat16):
    gain = levels(rng, extent, shards, -0.22, 0.18) if shards else 1.0
    values = jax.random.normal(rng, extent, jnp.float32) * deviation * gain
    return jnp.minimum(jnp.maximum(values, -bound), bound).astype(held_as)


def setup_inputs(seed: int = 0) -> dict:
    splits = jax.random.split(jax.random.key(seed), 10)
    frames = draw_frames(jax.random.fold_in(splits[9], 71), 0)
    item_mask = with_ends((jax.random.randint(splits[1], (ITEMS,), 0, 4) < 3).astype(jnp.int32), jax.random.fold_in(splits[1], 1), 0, 1)
    weights = bell_draw(splits[2], (2, KIN, C), (9 * C) ** -0.5, 0.09375, ((1, 8), (2, 4)), jnp.float32)
    biases = bell_draw(splits[3], (2, C), 0.1, 0.4, (), jnp.float32)
    cotangent = draw_cotangent(jax.random.fold_in(splits[9], 71), 0)
    weight_first = bell_draw(splits[5], (2, KIN, C), ((18 * C * C + 2 * C) ** -0.5), 0.0018412241, ((1, 8), (2, 4)), jnp.float32)
    weight_second = jnp.clip(jnp.exp(math.log(1.6950531289694482e-06) - 2.7725887 * jax.random.uniform(splits[6], (2, KIN, C), jnp.float32) ** levels(splits[6], (2, KIN, C), ((1, 8), (2, 4)), -0.2, 0.2)), 1.0594082056059051e-07, 1.6950531289694482e-06)
    bias_first = bell_draw(splits[7], (2, C), ((18 * C * C + 2 * C) ** -0.5), 0.0018412241, (), jnp.float32)
    bias_second = jnp.clip(jnp.exp(jax.random.uniform(splits[8], (2, C), jnp.float32, math.log(1.0594082056059051e-07), math.log(1.6950531289694482e-06))), 1.0594082056059051e-07, 1.6950531289694482e-06)
    return {"frames": frames, "item_mask": item_mask, "weights": weights, "biases": biases, "cotangent": cotangent, "weight_first": weight_first, "weight_second": weight_second, "bias_first": bias_first, "bias_second": bias_second}


@jax.custom_vjp
def low(v):
    return lax.optimization_barrier(v.astype(jnp.bfloat16)).astype(jnp.float32)

@jax.custom_vjp
def low_back(v):
    return v

def low_keep(v):
    return (low(v), None)

def low_pass(kept, grad):
    return (grad,)

def back_keep(v):
    return (v, None)

def back_low(kept, grad):
    return (low(grad),)
low.defvjp(low_keep, low_pass)
low_back.defvjp(back_keep, back_low)
CLIP_NORM = 1.0
BETA_ONE = 0.5
BETA_TWO = 0.5
RATE = 0.01
BIAS_RATE = 0.03
DECAY = 0.1
EPSILON = 1e-08

def to_kernel(weight_rows):
    in_chan = weight_rows.shape[0] // 9
    return jnp.transpose(weight_rows.reshape(in_chan, 3, 3, weight_rows.shape[1]), (1, 2, 0, 3))

def convolve(inputs, weight_rows):
    return lax.conv_general_dilated(inputs, to_kernel(weight_rows), (1, 1), ((1, 1), (1, 1)), dimension_numbers=('NHWC', 'HWIO', 'NHWC'), precision=lax.Precision.HIGHEST)

def forward(frames, weights, biases, mask_float):
    rounded = low(weights)
    pre_four = low_back(convolve(frames, rounded[0]) + biases[0])
    act_four = low(jax.nn.gelu(pre_four))
    pre_five = low_back(convolve(act_four, rounded[1]) + biases[1])
    act_five = low(mask_float * jax.nn.gelu(pre_five))
    return (act_four, act_five)

def adam_update(param, grad, first, second, rate, decay):
    first_new = BETA_ONE * first + (1.0 - BETA_ONE) * grad
    second_new = BETA_TWO * second + (1.0 - BETA_TWO) * grad * grad
    corrected = first_new / (1.0 - BETA_ONE ** STEP)
    scaled = jnp.sqrt(second_new / (1.0 - BETA_TWO ** STEP)) + EPSILON
    return (param - rate * (corrected / scaled + decay * param), first_new, second_new)

def reference(frames, item_mask, weights, biases, cotangent, weight_first, weight_second, bias_first, bias_second):
    groups = frames.shape[0] // ITEMS_DEV
    frame_blocks = frames.reshape(groups, ITEMS_DEV, H, W, C)
    cot_blocks = cotangent.reshape(groups, ITEMS_DEV, H, W, C)
    mask_blocks = item_mask.reshape(groups, ITEMS_DEV)

    def block_step(totals, item_block):
        frame_block, cot_block, mask_block = item_block
        mask_float = mask_block.astype(jnp.float32)[:, None, None, None]

        def local_forward(frame_vals, weight_vals, bias_vals):
            return forward(frame_vals, weight_vals, bias_vals, mask_float)
        outs_pair, pullback = jax.vjp(local_forward, frame_block.astype(jnp.float32), weights, biases)
        grad_frames, grad_weights, grad_biases = pullback((jnp.zeros_like(outs_pair[0]), cot_block.astype(jnp.float32)))
        new_totals = (totals[0] + grad_weights, totals[1] + grad_biases)
        return (new_totals, (outs_pair[0].astype(jnp.bfloat16), outs_pair[1].astype(jnp.bfloat16), grad_frames))
    start_totals = (jnp.zeros(weights.shape, jnp.float32), jnp.zeros(biases.shape, jnp.float32))
    totals, stacked = lax.scan(block_step, start_totals, (frame_blocks, cot_blocks, mask_blocks))
    grad_weights, grad_biases = totals
    act_four = stacked[0].reshape(frames.shape)
    act_five = stacked[1].reshape(frames.shape)
    input_grad = stacked[2].reshape(frames.shape)
    squares = jnp.sum(grad_weights * grad_weights) + jnp.sum(grad_biases * grad_biases)
    grad_norm = jnp.sqrt(squares)
    factor = jnp.minimum(1.0, CLIP_NORM / (grad_norm + 1e-06))
    new_weights, weight_m, weight_v = adam_update(weights, grad_weights * factor, weight_first, weight_second, RATE, DECAY)
    new_biases, bias_m, bias_v = adam_update(biases, grad_biases * factor, bias_first, bias_second, BIAS_RATE, 0.0)
    return (act_four, act_five, input_grad, grad_norm, new_weights, weight_m, weight_v, new_biases, bias_m, bias_v)
```

```python
import functools
import math

import jax
import jax.numpy as jnp
from jax import lax
from jax.experimental import pallas as pl
from jax.experimental.pallas import tpu as pltpu
from jax.sharding import PartitionSpec as P

STEP = 5
CLIP_NORM = 1.0
BETA_ONE = 0.5
BETA_TWO = 0.5
RATE = 0.01
BIAS_RATE = 0.03
DECAY = 0.1
EPSILON = 1e-08

MESH = pl.DeviceIdType.MESH
BF16 = jnp.bfloat16
F32 = jnp.float32
ROOT = math.sqrt(2.0 / math.pi)
CUBE = 0.044715
TAPS = 9
LANES = 128
PAD = 16
HALVES = 2
WIDE = 256


def gelu_parts(value):
    square = value * value
    th = jnp.tanh(ROOT * value * (1.0 + CUBE * square))
    half = 0.5 * (1.0 + th)
    slope = half + 0.5 * value * (1.0 - th * th) * (ROOT * (1.0 + 3.0 * CUBE * square))
    return value * half, slope


def flip_bits(index, mask):
    bit = 1
    while bit <= mask:
        if mask & bit:
            index = index + bit - 2 * bit * lax.rem(lax.div(index, bit), 2)
        bit *= 2
    return index


class Sizes:
    def __init__(self, mesh, frames_shape, weights_shape):
        self.dp = mesh.shape["dp"]
        self.tensor = mesh.shape["tensor"]
        self.items, self.height, self.width, self.out = frames_shape
        self.chan = self.out * self.tensor
        self.rows = weights_shape[1]
        self.own_in = self.rows // TAPS
        self.cols = TAPS * self.out
        self.major = self.dp // 2
        self.pairs = self.tensor // 2
        self.slots = self.dp // self.tensor
        self.spots = self.height * self.width
        self.span = -(-self.spots // 16) * 16
        self.wire = BF16 if self.own_in % 16 == 0 else F32
        self.group = self.items // HALVES


def body(
    sz,
    frames_ref,
    mask_ref,
    weights_ref,
    biases_ref,
    cot_ref,
    act4_out,
    act5_out,
    igrad_out,
    grads_out,
    stats_out,
    w_in,
    cot,
    w_all,
    frames,
    acts,
    spread,
    edges,
    slope4,
    act5,
    shifted,
    deltas,
    part_send,
    part_recv,
    part_own,
    cross_send,
    cross_recv,
    igrad,
    kgrad,
    near_send,
    near_recv,
    far_send,
    far_recv,
    shard,
    rows_out,
    bias_sum,
    stats_dp,
    stats_t,
    local_sem,
    out_sem,
    wz_send,
    wz_recv,
    wy_send,
    wy_recv,
    ax_send,
    ax_recv,
    as_send,
    as_recv,
    af_send,
    af_recv,
    rs_send,
    rs_recv,
    rx_send,
    rx_recv,
    gy_send,
    gy_recv,
    gz_send,
    gz_recv,
    sd_send,
    sd_recv,
    st_send,
    st_recv,
):
    d = lax.axis_index("dp")
    t = lax.axis_index("tensor")
    major, minor = lax.div(d, 2), lax.rem(d, 2)
    near = (2 * major + 1 - minor, t)
    pair, side = lax.div(t, 2), lax.rem(t, 2)
    sibling = (d, 2 * pair + 1 - side)

    def far_slot(k):
        return 2 * flip_bits(major, k) + minor

    def far(k):
        return (far_slot(k), t)

    def cross_rank(k):
        return 2 * lax.rem(pair + k, sz.pairs) + side

    def cross_from(k):
        return 2 * lax.rem(pair + sz.pairs - k, sz.pairs) + side

    def remote(src, dst, send, recv, device):
        return pltpu.make_async_remote_copy(
            src_ref=src, dst_ref=dst, send_sem=send, recv_sem=recv, device_id=device, device_id_type=MESH
        )

    far_steps = range(1, sz.major)
    cross_steps = range(1, sz.pairs)
    group = sz.group

    load_w = [pltpu.make_async_copy(weights_ref.at[l], w_in.at[l], local_sem.at[l]) for l in (0, 1)]
    load_frames = pltpu.make_async_copy(frames_ref, frames.at[t], local_sem.at[2])
    load_cot = pltpu.make_async_copy(cot_ref, cot, local_sem.at[3])
    load_w[0].start()
    load_frames.start()
    load_w[1].start()
    load_cot.start()

    barrier = pltpu.get_barrier_semaphore()
    for k in range(1, sz.dp):
        pl.semaphore_signal(barrier, inc=1, device_id=(lax.rem(d + k, sz.dp), t), device_id_type=MESH)
    for k in range(1, sz.tensor):
        pl.semaphore_signal(barrier, inc=1, device_id=(d, lax.rem(t + k, sz.tensor)), device_id_type=MESH)

    rest = sz.span + PAD
    for edge in (slice(0, PAD), slice(rest, rest + PAD)):
        spread[:, edge, :] = jnp.zeros((group, PAD, sz.cols), F32)
        shifted[:, edge, :] = jnp.zeros((3, PAD, sz.out), F32)
    spot = lax.broadcasted_iota(jnp.int32, (sz.span, sz.out), 0)
    column = lax.rem(spot, sz.width)
    edges[0] = (column > 0).astype(F32)
    edges[1] = (column < sz.width - 1).astype(F32)
    edges[2] = (spot < sz.spots).astype(F32)
    bias_sum[...] = jnp.zeros_like(bias_sum)

    def weight_sends(l):
        out = [remote(w_all.at[l, d], w_all.at[l, d], wz_send.at[l, k], wz_recv.at[l, k], far(k)) for k in far_steps]
        out.append(remote(w_all.at[l, d], w_all.at[l, d], wy_send.at[l, 0], wy_recv.at[l, 0], near))
        return out

    def weight_forward(l, k):
        slot = far_slot(k)
        return remote(w_all.at[l, slot], w_all.at[l, slot], wy_send.at[l, k], wy_recv.at[l, k], near)

    def weight_from_far(l, k):
        slot = far_slot(k)
        remote(w_all.at[l, slot], w_all.at[l, slot], wz_send.at[l, k], wz_recv.at[l, k], far(k)).wait_recv()

    def weight_from_near(l, k):
        slot = 2 * flip_bits(major, k) + 1 - minor
        remote(w_all.at[l, slot], w_all.at[l, slot], wy_send.at[l, k], wy_recv.at[l, k], near).wait_recv()

    def round_weights(l):
        load_w[l].wait()
        for tap in range(TAPS):
            w_all[l, d, :, tap * sz.out : (tap + 1) * sz.out] = w_in[
                l, pl.ds(tap, sz.own_in, stride=TAPS), :
            ].astype(sz.wire)

    pl.semaphore_wait(barrier, sz.dp + sz.tensor - 2)

    round_weights(0)
    sends = weight_sends(0)
    for copy in sends:
        copy.start()

    def piece(maps, rank, h):
        return maps.at[rank, pl.ds(h * group, group)]

    def gather_sends(g, maps, h):
        own = piece(maps, t, h)
        out = [remote(own, own, ax_send.at[g, h, k], ax_recv.at[g, h, k], (d, cross_rank(k))) for k in cross_steps]
        out.append(remote(own, own, as_send.at[g, h], as_recv.at[g, h], sibling))
        return out

    def gather_forward(g, maps, h, k):
        block = piece(maps, cross_from(k), h)
        return remote(block, block, af_send.at[g, h, k], af_recv.at[g, h, k], sibling)

    def gather_from_cross(g, maps, h, k):
        block = piece(maps, cross_from(k), h)
        remote(block, block, ax_send.at[g, h, k], ax_recv.at[g, h, k], sibling).wait_recv()

    def gather_from_sibling(g, maps, h):
        block = piece(maps, sibling[1], h)
        remote(block, block, as_send.at[g, h], as_recv.at[g, h], sibling).wait_recv()
        for k in cross_steps:
            rank = 2 * lax.rem(pair + sz.pairs - k, sz.pairs) + 1 - side
            block = piece(maps, rank, h)
            remote(block, block, af_send.at[g, h, k], af_recv.at[g, h, k], sibling).wait_recv()

    def gather_all(g, maps):
        for h in range(HALVES):
            for k in cross_steps:
                gather_from_cross(g, maps, h, k)
                gather_forward(g, maps, h, k).start()
        for h in range(HALVES):
            gather_from_sibling(g, maps, h)

    def gather_sent(g, maps):
        for h in range(HALVES):
            for copy in gather_sends(g, maps, h):
                copy.wait_send()
            for k in cross_steps:
                gather_forward(g, maps, h, k).wait_send()

    load_frames.wait()
    for h in range(HALVES):
        for copy in gather_sends(0, frames, h):
            copy.start()
    round_weights(1)
    gather_all(0, frames)

    for k in far_steps:
        weight_from_far(0, k)
        weight_forward(0, k).start()
    sends = weight_sends(1)
    for copy in sends:
        copy.start()
    for k in range(sz.major):
        weight_from_near(0, k)

    def convolve(l, maps, finish, after):
        @pl.loop(0, HALVES)
        def _(h):
            left = jnp.concatenate(
                [maps[q, pl.ds(h * group, group)].reshape(group * sz.span, sz.out) for q in range(sz.tensor)], axis=1
            )
            for start in range(0, sz.cols, WIDE):
                stop = min(start + WIDE, sz.cols)
                right = w_all[l, :, :, start:stop].reshape(sz.chan, stop - start).astype(BF16)
                product = jnp.dot(left, right, preferred_element_type=F32)
                spread[:, PAD:rest, start:stop] = product.reshape(group, sz.span, stop - start)

            @pl.loop(0, group)
            def _(m):
                sums = []
                for b in range(3):
                    total = None
                    for a in range(3):
                        first = PAD + sz.width * (a - 1) + b - 1
                        tap = 3 * a + b
                        term = spread[m, pl.ds(first, sz.span), tap * sz.out : (tap + 1) * sz.out]
                        total = term if total is None else total + term
                    sums.append(total)
                finish(h * group + m, sums[1] + sums[0] * edges[0] + sums[2] * edges[1])

            after(h)

    def own_bias(l):
        return biases_ref[l : l + 1, pl.ds(pl.multiple_of(t * sz.out, sz.out), sz.out)]

    def finish_four(n, value):
        act, slope = gelu_parts(value + own_bias(0))
        acts[t, n] = (act * edges[2]).astype(BF16)
        slope4[n] = slope * edges[2]

    def after_four(h):
        for copy in gather_sends(1, acts, h):
            copy.start()

    convolve(0, frames, finish_four, after_four)
    save_act4 = pltpu.make_async_copy(acts.at[t], act4_out, out_sem.at[0])
    save_act4.start()

    for k in far_steps:
        weight_from_far(1, k)
        weight_forward(1, k).start()
    gather_all(1, acts)
    for k in range(sz.major):
        weight_from_near(1, k)

    def spread_delta(l, n, delta):
        bias_sum[l, :, :] += jnp.sum(delta.reshape(sz.span // 8, 8, sz.out), axis=0)
        shifted[0, PAD:rest, :] = delta * edges[0]
        shifted[1, PAD:rest, :] = delta
        shifted[2, PAD:rest, :] = delta * edges[1]
        for a in range(3):
            for b in range(3):
                first = PAD - sz.width * (a - 1) - (b - 1)
                tap = 3 * a + b
                deltas[n, :, tap * sz.out : (tap + 1) * sz.out] = shifted[b, pl.ds(first, sz.span), :].astype(BF16)

    load_cot.wait()

    def finish_five(n, value):
        act, slope = gelu_parts(value + own_bias(1))
        keep = mask_ref[n].astype(F32)
        act5[n] = (act * keep).astype(BF16)
        delta = (cot[n].astype(F32) * keep * slope).astype(BF16).astype(F32)
        spread_delta(1, n, delta)

    convolve(1, acts, finish_five, lambda h: None)
    save_act5 = pltpu.make_async_copy(act5, act5_out, out_sem.at[1])
    save_act5.start()

    def part_copy(l, h):
        own = part_send.at[l, :, pl.ds(h * group, group)]
        there = part_recv.at[l, :, pl.ds(h * group, group)]
        return remote(own, there, rs_send.at[l, h], rs_recv.at[l, h], sibling)

    def cross_copy(l, h, k):
        return remote(
            cross_send.at[l, k, pl.ds(h * group, group)],
            cross_recv.at[l, k, pl.ds(h * group, group)],
            rx_send.at[l, h, k],
            rx_recv.at[l, h, k],
            (d, cross_rank(k)),
        )

    def back_products(l):
        def weights_for(which):
            blocks = [
                w_all[l, pl.ds((2 * j + which) * sz.slots, sz.slots)].reshape(sz.out, sz.cols) for j in range(sz.pairs)
            ]
            return jnp.concatenate(blocks, axis=0).astype(BF16)

        def products(h, right):
            left = deltas[pl.ds(h * group, group)].reshape(group * sz.span, sz.cols)
            out = lax.dot_general(left, right, (((1,), (1,)), ((), ())), preferred_element_type=F32)
            return [out[:, j * sz.out : (j + 1) * sz.out].reshape(group, sz.span, sz.out) for j in range(sz.pairs)]

        @pl.loop(0, HALVES)
        def _(h):
            for j, block in enumerate(products(h, weights_for(1 - side))):
                part_send[l, j, pl.ds(h * group, group)] = block.astype(BF16)
            part_copy(l, h).start()

        @pl.loop(0, HALVES)
        def _(h):
            for j, block in enumerate(products(h, weights_for(side))):
                part_own[j, pl.ds(h * group, group)] = block

        for h in range(HALVES):
            part_copy(l, h).wait_recv()
            items = pl.ds(h * group, group)
            for k in cross_steps:
                j = lax.rem(pair + k, sz.pairs)
                cross_send[l, k, items] = (part_own[j, items] + part_recv[l, j, items].astype(F32)).astype(BF16)
                cross_copy(l, h, k).start()

    def back_total(l, n):
        total = part_own[pair, n] + part_recv[l, pair, n].astype(F32)
        for k in cross_steps:
            total += cross_recv[l, k, n].astype(F32)
        return total

    def near_copy(l, k):
        return remote(near_send.at[l, k], near_recv.at[l, k], gy_send.at[l, k], gy_recv.at[l, k], near)

    def far_copy(l, k):
        return remote(far_send.at[l, k], far_recv.at[l, k], gz_send.at[l, k], gz_recv.at[l, k], far(k))

    grad_order = [*reversed(far_steps), 0]

    def weight_grads(l, maps):
        left = jnp.concatenate([maps[q].reshape(sz.items * sz.span, sz.out) for q in range(sz.tensor)], axis=1)
        for start in range(0, sz.cols, WIDE):
            stop = min(start + WIDE, sz.cols)
            right = deltas[:, :, start:stop].reshape(sz.items * sz.span, stop - start)
            product = lax.dot_general(left, right, (((0,), (0,)), ((), ())), preferred_element_type=F32)
            kgrad[l, :, :, start:stop] = product.reshape(sz.dp, sz.own_in, stop - start)
        for k in grad_order:
            near_send[l, k] = kgrad[l, 2 * flip_bits(major, k) + 1 - minor].astype(sz.wire)
            near_copy(l, k).start()

    def grads_to_far(l):
        for k in grad_order:
            near_copy(l, k).wait_recv()
            if k:
                far_send[l, k] = (kgrad[l, far_slot(k)] + near_recv[l, k].astype(F32)).astype(sz.wire)
                far_copy(l, k).start()

    def grads_done(l):
        total = kgrad[l, d] + near_recv[l, 0].astype(F32)
        for k in far_steps:
            far_copy(l, k).wait_recv()
            total += far_recv[l, k].astype(F32)
        shard[...] = total
        squares = jnp.sum((total * total).reshape(sz.own_in // 8, 8, sz.cols), axis=0)
        for tap in range(TAPS):
            rows_out[l, pl.ds(tap, sz.own_in, stride=TAPS), :] = shard[:, tap * sz.out : (tap + 1) * sz.out]
        return sum(squares[:, tap * sz.out : (tap + 1) * sz.out] for tap in range(TAPS))

    back_products(1)
    weight_grads(1, acts)

    for h in range(HALVES):
        for k in cross_steps:
            cross_copy(1, h, k).wait_recv()

        @pl.loop(h * group, (h + 1) * group)
        def _(n):
            delta = (back_total(1, n) * slope4[n]).astype(BF16).astype(F32)
            spread_delta(0, n, delta)

    weight_grads(0, frames)
    grads_to_far(1)
    back_products(0)
    grads_to_far(0)

    for h in range(HALVES):
        for k in cross_steps:
            cross_copy(0, h, k).wait_recv()

        @pl.loop(h * group, (h + 1) * group)
        def _(n):
            igrad[n] = back_total(0, n)

    save_igrad = pltpu.make_async_copy(igrad, igrad_out, out_sem.at[2])
    save_igrad.start()

    squares = grads_done(1)
    save_grads = [pltpu.make_async_copy(rows_out.at[l], grads_out.at[l], out_sem.at[3 + l]) for l in (0, 1)]
    save_grads[1].start()
    squares += grads_done(0)
    save_grads[0].start()

    stats_dp[d, 0:1, :] = jnp.sum(squares, axis=0, keepdims=True)
    for l in (0, 1):
        stats_dp[d, l + 1 : l + 2, :] = jnp.sum(bias_sum[l], axis=0, keepdims=True)
    stats_dp[d, 3:8, :] = jnp.zeros((5, sz.out), F32)

    def stats_over_dp(k, slot):
        return remote(
            stats_dp.at[slot], stats_dp.at[slot], sd_send.at[k], sd_recv.at[k], (lax.rem(d + k, sz.dp), t)
        )

    def stats_over_tensor(k, slot):
        return remote(
            stats_t.at[slot], stats_t.at[slot], st_send.at[k], st_recv.at[k], (d, lax.rem(t + k, sz.tensor))
        )

    for k in range(1, sz.dp):
        stats_over_dp(k, d).start()
    for k in range(1, sz.dp):
        stats_over_dp(k, lax.rem(d + sz.dp - k, sz.dp)).wait_recv()
    total = stats_dp[0]
    for slot in range(1, sz.dp):
        total += stats_dp[slot]
    stats_t[t] = total
    for k in range(1, sz.tensor):
        stats_over_tensor(k, t).start()
    for k in range(1, sz.tensor):
        stats_over_tensor(k, lax.rem(t + sz.tensor - k, sz.tensor)).wait_recv()
    save_stats = pltpu.make_async_copy(stats_t, stats_out, out_sem.at[5])
    save_stats.start()

    for l in (0, 1):
        for copy in weight_sends(l):
            copy.wait_send()
        for k in far_steps:
            weight_forward(l, k).wait_send()
            far_copy(l, k).wait_send()
        for k in range(sz.major):
            near_copy(l, k).wait_send()
        for h in range(HALVES):
            part_copy(l, h).wait_send()
            for k in cross_steps:
                cross_copy(l, h, k).wait_send()
    gather_sent(0, frames)
    gather_sent(1, acts)
    for k in range(1, sz.dp):
        stats_over_dp(k, d).wait_send()
    for k in range(1, sz.tensor):
        stats_over_tensor(k, t).wait_send()
    for copy in (save_act4, save_act5, save_igrad, *save_grads, save_stats):
        copy.wait()


def train_step(sz, frames, item_mask, weights, biases, cotangent):
    sem = pltpu.SemaphoreType.DMA
    vmem = pltpu.VMEM
    maps = (sz.items, sz.span, sz.out)
    shapes = [
        vmem((2, sz.rows, sz.out), F32),
        vmem(maps, BF16),
        vmem((2, sz.dp, sz.own_in, sz.cols), sz.wire),
        vmem((sz.tensor, *maps), BF16),
        vmem((sz.tensor, *maps), BF16),
        vmem((sz.group, sz.span + 2 * PAD, sz.cols), F32),
        vmem((3, sz.span, sz.out), F32),
        vmem(maps, F32),
        vmem(maps, BF16),
        vmem((3, sz.span + 2 * PAD, sz.out), F32),
        vmem((sz.items, sz.span, sz.cols), BF16),
        vmem((2, sz.pairs, *maps), BF16),
        vmem((2, sz.pairs, *maps), BF16),
        vmem((sz.pairs, *maps), F32),
        vmem((2, sz.pairs, *maps), BF16),
        vmem((2, sz.pairs, *maps), BF16),
        vmem(maps, F32),
        vmem((2, sz.dp, sz.own_in, sz.cols), F32),
        vmem((2, sz.major, sz.own_in, sz.cols), sz.wire),
        vmem((2, sz.major, sz.own_in, sz.cols), sz.wire),
        vmem((2, sz.major, sz.own_in, sz.cols), sz.wire),
        vmem((2, sz.major, sz.own_in, sz.cols), sz.wire),
        vmem((sz.own_in, sz.cols), F32),
        vmem((2, sz.rows, sz.out), F32),
        vmem((2, 8, sz.out), F32),
        vmem((sz.dp, 8, sz.out), F32),
        vmem((sz.tensor, 8, sz.out), F32),
        sem((4,)),
        sem((6,)),
        sem((2, sz.major)),
        sem((2, sz.major)),
        sem((2, sz.major)),
        sem((2, sz.major)),
        sem((2, HALVES, sz.pairs)),
        sem((2, HALVES, sz.pairs)),
        sem((2, HALVES)),
        sem((2, HALVES)),
        sem((2, HALVES, sz.pairs)),
        sem((2, HALVES, sz.pairs)),
        sem((2, HALVES)),
        sem((2, HALVES)),
        sem((2, HALVES, sz.pairs)),
        sem((2, HALVES, sz.pairs)),
        sem((2, sz.major)),
        sem((2, sz.major)),
        sem((2, sz.major)),
        sem((2, sz.major)),
        sem((sz.dp,)),
        sem((sz.dp,)),
        sem((sz.tensor,)),
        sem((sz.tensor,)),
    ]
    anywhere = pl.BlockSpec(memory_space=pl.ANY)
    macs = 6 * sz.items * sz.spots * TAPS * sz.chan * sz.out
    return pl.pallas_call(
        functools.partial(body, sz),
        out_shape=[
            jax.ShapeDtypeStruct(maps, BF16),
            jax.ShapeDtypeStruct(maps, BF16),
            jax.ShapeDtypeStruct(maps, F32),
            jax.ShapeDtypeStruct((2, sz.rows, sz.out), F32),
            jax.ShapeDtypeStruct((sz.tensor, 8, sz.out), F32),
        ],
        in_specs=[
            anywhere,
            pl.BlockSpec(memory_space=pltpu.SMEM),
            anywhere,
            pl.BlockSpec(memory_space=pltpu.VMEM),
            anywhere,
        ],
        out_specs=[anywhere] * 5,
        scratch_shapes=shapes,
        compiler_params=pltpu.CompilerParams(
            collective_id=0, has_side_effects=True, vmem_limit_bytes=58 * 1024 * 1024
        ),
        cost_estimate=pl.CostEstimate(flops=2 * macs, bytes_accessed=6_000_000, transcendentals=0),
        name="train_step",
    )(frames, item_mask, weights, biases, cotangent)


def adam_update(param, grad, first, second, rate, decay):
    first_new = BETA_ONE * first + (1.0 - BETA_ONE) * grad
    second_new = BETA_TWO * second + (1.0 - BETA_TWO) * grad * grad
    corrected = first_new / (1.0 - BETA_ONE**STEP)
    scaled = jnp.sqrt(second_new / (1.0 - BETA_TWO**STEP)) + EPSILON
    return (param - rate * (corrected / scaled + decay * param), first_new, second_new)


def on_device(
    mesh,
    frames,
    item_mask,
    weights,
    biases,
    cotangent,
    weight_first,
    weight_second,
    bias_first,
    bias_second,
):
    sz = Sizes(mesh, frames.shape, weights.shape)

    def flat(maps):
        rows = maps.reshape(sz.items, sz.spots, sz.out)
        return jnp.pad(rows, ((0, 0), (0, sz.span - sz.spots), (0, 0)))

    def square(rows):
        return rows[:, : sz.spots].reshape(sz.items, sz.height, sz.width, sz.out)

    act_four, act_five, input_grad, grad_shard, stats = train_step(
        sz, flat(frames), item_mask, weights, biases, flat(cotangent)
    )
    bias_grad = jnp.moveaxis(stats[:, 1:3, :], 1, 0).reshape(2, sz.chan)
    grad_norm = jnp.sqrt(jnp.sum(stats[:, 0, :]) + jnp.sum(bias_grad * bias_grad))
    factor = jnp.minimum(1.0, CLIP_NORM / (grad_norm + 1e-06))
    new_weights, weight_m, weight_v = adam_update(
        weights, grad_shard * factor, weight_first, weight_second, RATE, DECAY
    )
    new_biases, bias_m, bias_v = adam_update(
        biases, bias_grad * factor, bias_first, bias_second, BIAS_RATE, 0.0
    )
    return (
        square(act_four),
        square(act_five),
        square(input_grad),
        grad_norm,
        new_weights,
        weight_m,
        weight_v,
        new_biases,
        bias_m,
        bias_v,
    )


def solution(mesh):
    split = P("dp", None, None, "tensor")
    rows = P(None, "dp", "tensor")
    in_specs = (split, P("dp"), rows, P(), split, rows, rows, P(), P())
    out_specs = (split, split, split, P(), rows, rows, rows, P(), P(), P())
    return jax.shard_map(
        functools.partial(on_device, mesh), mesh=mesh, in_specs=in_specs, out_specs=out_specs, check_vma=False
    )
```

```python
import functools
import math

import jax
import jax.numpy as jnp
from jax import lax
from jax.experimental import pallas as pl
from jax.experimental.pallas import tpu as pltpu
from jax.sharding import PartitionSpec as P

STEP = 5
CLIP_NORM = 1.0
BETA_ONE = 0.5
BETA_TWO = 0.5
RATE = 0.01
BIAS_RATE = 0.03
DECAY = 0.1
EPSILON = 1e-08

MESH = pl.DeviceIdType.MESH
BF16 = jnp.bfloat16
F32 = jnp.float32
ROOT = math.sqrt(2.0 / math.pi)
CUBE = 0.044715
TAPS = 9
WIDE = 256


def gelu_parts(value):
    square = value * value
    th = jnp.tanh(ROOT * value * (1.0 + CUBE * square))
    half = 0.5 * (1.0 + th)
    slope = half + 0.5 * value * (1.0 - th * th) * (ROOT * (1.0 + 3.0 * CUBE * square))
    return value * half, slope


def flip_bits(index, mask):
    bit = 1
    while bit <= mask:
        if mask & bit:
            index = index + bit - 2 * bit * lax.rem(lax.div(index, bit), 2)
        bit *= 2
    return index


def adam_update(param, grad, first, second, rate, decay):
    first_new = BETA_ONE * first + (1.0 - BETA_ONE) * grad
    second_new = BETA_TWO * second + (1.0 - BETA_TWO) * grad * grad
    corrected = first_new / (1.0 - BETA_ONE**STEP)
    scaled = jnp.sqrt(second_new / (1.0 - BETA_TWO**STEP)) + EPSILON
    return (param - rate * (corrected / scaled + decay * param), first_new, second_new)


class Sizes:
    def __init__(self, mesh, frames_shape, weights_shape):
        self.dp = mesh.shape["dp"]
        self.tensor = mesh.shape["tensor"]
        self.items, self.height, self.width, self.out = frames_shape
        self.chan = self.out * self.tensor
        self.rows = weights_shape[1]
        self.own_in = self.rows // TAPS
        self.cols = TAPS * self.out
        self.major = self.dp // 2
        self.pairs = self.tensor // 2
        self.slots = self.dp // self.tensor
        self.spots = self.height * self.width
        self.real = self.spots * self.items
        self.span = -(-self.real // 16) * 16
        self.halo = (self.width + 1) * self.items
        self.pieces = next(n for n in (5, 4, 3, 2, 1) if self.span // 16 % n == 0)
        self.piece = self.span // self.pieces
        self.groups = ((0, self.pieces // 2), (self.pieces // 2, self.pieces))
        self.wire = BF16 if self.own_in % 16 == 0 else F32
        self.relay = self.major == 4
        self.far_order = (2, 1, 3) if self.relay else tuple(range(1, self.major))


def body(
    sz,
    frames_ref,
    mask_ref,
    weights_ref,
    biases_ref,
    cot_ref,
    act4_out,
    act5_out,
    igrad_out,
    grads_out,
    stats_out,
    w_in,
    stage,
    cot,
    biases,
    mask,
    keep,
    w_all,
    frames,
    acts,
    spread,
    edges,
    slope4,
    act5,
    shifted,
    deltas,
    part_send,
    part_recv,
    part_own,
    cross_send,
    cross_recv,
    igrad,
    kgrad,
    near_send,
    near_recv,
    far_send,
    far_recv,
    shard,
    rows_out,
    bias_sum,
    stats_dp,
    stats_t,
    local_sem,
    out_sem,
    wz_send,
    wz_recv,
    wf_send,
    wy_send,
    wy_recv,
    ax_send,
    ax_recv,
    as_send,
    as_recv,
    af_send,
    af_recv,
    rs_send,
    rs_recv,
    rx_send,
    rx_recv,
    gy_send,
    gy_recv,
    gz_send,
    gz_recv,
    sd_send,
    sd_recv,
    st_send,
    st_recv,
):
    d = lax.axis_index("dp")
    t = lax.axis_index("tensor")
    major, minor = lax.div(d, 2), lax.rem(d, 2)
    near = (2 * major + 1 - minor, t)
    pair, side = lax.div(t, 2), lax.rem(t, 2)
    sibling = (d, 2 * pair + 1 - side)
    middle = jnp.logical_and(major > 0, major < sz.major - 1)

    def far_slot(k):
        return 2 * flip_bits(major, k) + minor

    def near_slot(k):
        return 2 * flip_bits(major, k) + 1 - minor

    def far(k):
        return (far_slot(k), t)

    def cross_rank(k):
        return 2 * lax.rem(pair + k, sz.pairs) + side

    def cross_from(k):
        return 2 * lax.rem(pair + sz.pairs - k, sz.pairs) + side

    def remote(src, dst, send, recv, device):
        return pltpu.make_async_remote_copy(
            src_ref=src, dst_ref=dst, send_sem=send, recv_sem=recv, device_id=device, device_id_type=MESH
        )

    def same(block, send, recv, device):
        return remote(block, block, send, recv, device)

    far_steps = range(1, sz.major)
    cross_steps = range(1, sz.pairs)
    all_pieces = range(sz.pieces)

    def rows_of(p):
        return pl.ds(pl.multiple_of(p * sz.piece, 16), sz.piece)

    load_w = [pltpu.make_async_copy(weights_ref.at[l], w_in.at[l], local_sem.at[l]) for l in (0, 1)]
    load_frames = pltpu.make_async_copy(frames_ref, stage.at[0], local_sem.at[2])
    load_cot = pltpu.make_async_copy(cot_ref, stage.at[1], local_sem.at[3])
    load_biases = pltpu.make_async_copy(biases_ref, biases, local_sem.at[4])
    load_mask = pltpu.make_async_copy(mask_ref, mask, local_sem.at[5])
    for copy in (load_w[0], load_frames, load_w[1], load_cot, load_biases, load_mask):
        copy.start()

    barrier = pltpu.get_barrier_semaphore()
    for k in range(1, sz.dp):
        pl.semaphore_signal(barrier, inc=1, device_id=(lax.rem(d + k, sz.dp), t), device_id_type=MESH)
    for k in range(1, sz.tensor):
        pl.semaphore_signal(barrier, inc=1, device_id=(d, lax.rem(t + k, sz.tensor)), device_id_type=MESH)

    def weight_sends(l):
        block = w_all.at[l, d]
        direct = {k: same(block, wz_send.at[l, k], wz_recv.at[l, k], far(k)) for k in sz.far_order}
        return direct, same(block, wy_send.at[l, 0], wy_recv.at[l, 0], near)

    def weight_relay(l):
        return same(w_all.at[l, far_slot(2)], wf_send.at[l], wz_recv.at[l, 3], far(1))

    def weight_forward(l, k):
        return same(w_all.at[l, far_slot(k)], wy_send.at[l, k], wy_recv.at[l, k], near)

    def send_weights(l):
        direct, over = weight_sends(l)
        over.start()
        for k, copy in direct.items():
            if sz.relay and k == 3:
                pl.when(middle)(copy.start)
            else:
                copy.start()

    def weights_sent(l):
        direct, over = weight_sends(l)
        over.wait_send()
        for k, copy in direct.items():
            weight_forward(l, k).wait_send()
            if sz.relay and k == 3:

                @pl.when(middle)
                def _():
                    copy.wait_send()
                    weight_relay(l).wait_send()

            else:
                copy.wait_send()

    def forward_weights(l, k):
        same(w_all.at[l, far_slot(k)], wz_send.at[l, k], wz_recv.at[l, k], far(k)).wait_recv()
        if sz.relay and k == 2:
            pl.when(middle)(weight_relay(l).start)
        weight_forward(l, k).start()

    def weights_here(l):
        for k in range(sz.major):
            same(w_all.at[l, near_slot(k)], wy_send.at[l, k], wy_recv.at[l, k], near).wait_recv()

    def round_weights(l):
        load_w[l].wait()
        for tap in range(TAPS):
            w_all[l, d, :, tap * sz.out : (tap + 1) * sz.out] = w_in[
                l, pl.ds(tap, sz.own_in, stride=TAPS), :
            ].astype(sz.wire)

    def gather_sends(g, maps, p, rows):
        own = maps.at[t, rows]
        out = [same(own, ax_send.at[g, p, k], ax_recv.at[g, p, k], (d, cross_rank(k))) for k in cross_steps]
        out.append(same(own, as_send.at[g, p], as_recv.at[g, p], sibling))
        return out

    def gather_forward(g, maps, p, rows, k):
        return same(maps.at[cross_from(k), rows], af_send.at[g, p, k], af_recv.at[g, p, k], sibling)

    def gather_pass_on(g, maps, p, rows):
        for k in cross_steps:
            same(maps.at[cross_from(k), rows], ax_send.at[g, p, k], ax_recv.at[g, p, k], sibling).wait_recv()
            gather_forward(g, maps, p, rows, k).start()

    def gather_here(g, maps, p, rows):
        same(maps.at[sibling[1], rows], as_send.at[g, p], as_recv.at[g, p], sibling).wait_recv()
        for k in cross_steps:
            rank = 2 * lax.rem(pair + sz.pairs - k, sz.pairs) + 1 - side
            same(maps.at[rank, rows], af_send.at[g, p, k], af_recv.at[g, p, k], sibling).wait_recv()

    def gather_sent(g, maps, p, rows):
        for copy in gather_sends(g, maps, p, rows):
            copy.wait_send()
        for k in cross_steps:
            gather_forward(g, maps, p, rows, k).wait_send()

    whole = pl.ds(0, sz.span)

    def product(l, maps, group):
        rows = slice(group[0] * sz.piece, group[1] * sz.piece)
        left = jnp.concatenate([maps[q, rows] for q in range(sz.tensor)], axis=1)
        for start in range(0, sz.cols, WIDE):
            stop = min(start + WIDE, sz.cols)
            right = w_all[l, :, :, start:stop].reshape(sz.chan, stop - start).astype(BF16)
            spread[sz.halo + rows.start : sz.halo + rows.stop, start:stop] = jnp.dot(
                left, right, preferred_element_type=F32
            )

    def own_bias(l):
        return biases[l : l + 1, pl.ds(pl.multiple_of(t * sz.out, sz.out), sz.out)]

    def shifted_sum(p):
        sums = []
        for b in range(3):
            total = None
            for a in range(3):
                shift = sz.items * (sz.width * (a - 1) + b - 1)
                tap = 3 * a + b
                rows = pl.ds(pl.multiple_of(p * sz.piece + sz.halo + shift, 8), sz.piece)
                term = spread[rows, tap * sz.out : (tap + 1) * sz.out]
                total = term if total is None else total + term
            sums.append(total)
        return sums[1] + sums[0] * edges[0, rows_of(p)] + sums[2] * edges[1, rows_of(p)]

    def note_delta(l, p, delta):
        bias_sum[l] += jnp.sum(delta.reshape(sz.piece // 8, 8, sz.out), axis=0)
        rows = pl.ds(pl.multiple_of(p * sz.piece + sz.halo, 8), sz.piece)
        shifted[0, rows] = delta * edges[0, rows_of(p)]
        shifted[1, rows] = delta
        shifted[2, rows] = delta * edges[1, rows_of(p)]

    def spread_delta():
        @pl.loop(0, sz.pieces)
        def _(p):
            for a in range(3):
                for b in range(3):
                    shift = sz.items * (sz.width * (a - 1) + b - 1)
                    tap = 3 * a + b
                    rows = pl.ds(pl.multiple_of(p * sz.piece + sz.halo - shift, 8), sz.piece)
                    deltas[rows_of(p), tap * sz.out : (tap + 1) * sz.out] = shifted[b, rows].astype(BF16)

    def finish_four(first, last):
        @pl.loop(first, last)
        def _(p):
            act, slope = gelu_parts(shifted_sum(p) + own_bias(0))
            acts[t, rows_of(p)] = (act * edges[2, rows_of(p)]).astype(BF16)
            slope4[rows_of(p)] = slope * edges[2, rows_of(p)]
            for copy in gather_sends(1, acts, p, rows_of(p)):
                copy.start()

    def by_item(value):
        return (value.reshape(sz.piece // sz.items, sz.items, sz.out) * keep[...]).reshape(sz.piece, sz.out)

    def finish_five(first, last):
        @pl.loop(first, last)
        def _(p):
            act, slope = gelu_parts(shifted_sum(p) + own_bias(1))
            act5[rows_of(p)] = by_item(act).astype(BF16)
            delta = (by_item(cot[rows_of(p)].astype(F32)) * slope).astype(BF16).astype(F32)
            note_delta(1, p, delta)

    def part_copy(l, p):
        rows = rows_of(p)
        return remote(
            part_send.at[l, :, rows], part_recv.at[l, :, rows], rs_send.at[l, p], rs_recv.at[l, p], sibling
        )

    def cross_copy(l, p, k):
        rows = rows_of(p)
        return remote(
            cross_send.at[l, k, rows],
            cross_recv.at[l, k, rows],
            rx_send.at[l, p, k],
            rx_recv.at[l, p, k],
            (d, cross_rank(k)),
        )

    def back_product(l, group, which):
        blocks = [
            w_all[l, pl.ds((2 * j + which) * sz.slots, sz.slots)].reshape(sz.out, sz.cols) for j in range(sz.pairs)
        ]
        right = jnp.concatenate(blocks, axis=0).astype(BF16)
        left = deltas[group[0] * sz.piece : group[1] * sz.piece]
        out = lax.dot_general(left, right, (((1,), (1,)), ((), ())), preferred_element_type=F32)
        return [out[:, j * sz.out : (j + 1) * sz.out] for j in range(sz.pairs)]

    def back_to_sibling(l, group):
        rows = slice(group[0] * sz.piece, group[1] * sz.piece)
        for j, block in enumerate(back_product(l, group, 1 - side)):
            part_send[l, j, rows] = block.astype(BF16)
        for p in range(*group):
            part_copy(l, p).start()

    def back_own(l, group):
        rows = slice(group[0] * sz.piece, group[1] * sz.piece)
        for j, block in enumerate(back_product(l, group, side)):
            part_own[j, rows] = block

    def back_across(l, group):
        @pl.loop(*group)
        def _(p):
            part_copy(l, p).wait_recv()
            for k in cross_steps:
                j = lax.rem(pair + k, sz.pairs)
                total = part_own[j, rows_of(p)] + part_recv[l, j, rows_of(p)].astype(F32)
                cross_send[l, k, rows_of(p)] = total.astype(BF16)
                cross_copy(l, p, k).start()

    def back_products(l):
        one, two = sz.groups
        back_to_sibling(l, one)
        back_own(l, one)
        back_to_sibling(l, two)
        back_across(l, one)
        back_own(l, two)
        back_across(l, two)

    def back_total(l, p):
        total = part_own[pair, rows_of(p)] + part_recv[l, pair, rows_of(p)].astype(F32)
        for k in cross_steps:
            cross_copy(l, p, k).wait_recv()
            total += cross_recv[l, k, rows_of(p)].astype(F32)
        return total

    def near_copy(l, k):
        return remote(near_send.at[l, k], near_recv.at[l, k], gy_send.at[l, k], gy_recv.at[l, k], near)

    def far_copy(l, k):
        return remote(far_send.at[l, k], far_recv.at[l, k], gz_send.at[l, k], gz_recv.at[l, k], far(k))

    half = sz.tensor // 2
    far_half = [k for k in far_steps if k >= sz.major // 2]
    near_half = [k for k in far_steps if k < sz.major // 2]

    def grads_half(l, maps, other):
        own = lax.div(major, sz.major // 2)
        first = (1 - own if other else own) * half
        left = jnp.concatenate([maps[first + q] for q in range(half)], axis=1)
        into = pl.ds(first * sz.slots, half * sz.slots)
        for start in range(0, sz.cols, WIDE):
            stop = min(start + WIDE, sz.cols)
            product = lax.dot_general(left, deltas[:, start:stop], (((0,), (0,)), ((), ())), preferred_element_type=F32)
            kgrad[l, into, :, start:stop] = product.reshape(half * sz.slots, sz.own_in, stop - start)
        for k in far_half if other else [*near_half, 0]:
            near_send[l, k] = kgrad[l, near_slot(k)].astype(sz.wire)
            near_copy(l, k).start()

    def grads_far(l, k):
        near_copy(l, k).wait_recv()
        far_send[l, k] = (kgrad[l, far_slot(k)] + near_recv[l, k].astype(F32)).astype(sz.wire)
        far_copy(l, k).start()

    def grads_done(l):
        near_copy(l, 0).wait_recv()
        for k in far_steps:
            far_copy(l, k).wait_recv()
        total = kgrad[l, d] + near_recv[l, 0].astype(F32)
        for k in far_steps:
            total += far_recv[l, k].astype(F32)
        shard[...] = total
        squares = jnp.sum((total * total).reshape(sz.own_in // 8, 8, sz.cols), axis=0)
        for tap in range(TAPS):
            rows_out[l, pl.ds(tap, sz.own_in, stride=TAPS), :] = shard[:, tap * sz.out : (tap + 1) * sz.out]
        return sum(squares[:, tap * sz.out : (tap + 1) * sz.out] for tap in range(TAPS))

    rest = sz.halo + sz.span
    for first in (0, rest):
        spread[first : first + sz.halo, :] = jnp.zeros((sz.halo, sz.cols), F32)
        shifted[:, first : first + sz.halo, :] = jnp.zeros((3, sz.halo, sz.out), F32)

    @pl.loop(0, sz.pieces)
    def _(p):
        spot = lax.div(p * sz.piece + lax.broadcasted_iota(jnp.int32, (sz.piece, sz.out), 0), sz.items)
        column = lax.rem(spot, sz.width)
        edges[0, rows_of(p)] = (column > 0).astype(F32)
        edges[1, rows_of(p)] = (column < sz.width - 1).astype(F32)
        edges[2, rows_of(p)] = (spot < sz.spots).astype(F32)

    bias_sum[...] = jnp.zeros_like(bias_sum)
    tail = sz.span - 16
    cot[tail:] = jnp.zeros((16, sz.out), BF16)
    frames[t, tail:] = jnp.zeros((16, sz.out), BF16)

    round_weights(0)
    pl.semaphore_wait(barrier, sz.dp + sz.tensor - 2)
    send_weights(0)
    load_frames.wait()
    frames[t, 0 : sz.real] = stage[0]
    for copy in gather_sends(0, frames, 0, whole):
        copy.start()
    round_weights(1)
    send_weights(1)

    load_cot.wait()
    cot[0 : sz.real] = stage[1]
    load_biases.wait()
    load_mask.wait()
    item = lax.broadcasted_iota(jnp.int32, (sz.items, sz.out), 0)
    kept = jnp.zeros((sz.items, sz.out), F32)
    for n in range(sz.items):
        kept = jnp.where(item == n, mask[n].astype(F32), kept)
    keep[...] = kept

    gather_pass_on(0, frames, 0, whole)
    for k in far_steps:
        forward_weights(0, k)
    gather_here(0, frames, 0, whole)
    weights_here(0)

    one, two = sz.groups
    product(0, frames, one)
    finish_four(0, one[1] - 1)
    product(0, frames, two)
    finish_four(one[1] - 1, sz.pieces)

    for k in far_steps:
        forward_weights(1, k)
    stage[0] = acts[t, 0 : sz.real]
    save_act4 = pltpu.make_async_copy(stage.at[0], act4_out, out_sem.at[0])
    save_act4.start()

    for p in all_pieces:
        gather_pass_on(1, acts, p, rows_of(p))
    for p in all_pieces:
        gather_here(1, acts, p, rows_of(p))
    weights_here(1)
    product(1, acts, one)
    finish_five(0, one[1] - 1)
    product(1, acts, two)
    finish_five(one[1] - 1, sz.pieces)
    spread_delta()

    grads_half(1, acts, True)
    back_products(1)
    grads_half(1, acts, False)
    stage[1] = act5[0 : sz.real]
    save_act5 = pltpu.make_async_copy(stage.at[1], act5_out, out_sem.at[1])
    save_act5.start()
    for k in far_half:
        grads_far(1, k)

    @pl.loop(0, sz.pieces)
    def _(p):
        note_delta(0, p, (back_total(1, p) * slope4[rows_of(p)]).astype(BF16).astype(F32))

    spread_delta()
    grads_half(0, frames, True)
    for k in near_half:
        grads_far(1, k)
    grads_half(0, frames, False)
    back_products(0)
    for k in far_half:
        grads_far(0, k)
    squares = grads_done(1)
    save_grads = [pltpu.make_async_copy(rows_out.at[l], grads_out.at[l], out_sem.at[3 + l]) for l in (0, 1)]
    save_grads[1].start()
    for k in near_half:
        grads_far(0, k)

    @pl.loop(0, sz.pieces)
    def _(p):
        igrad[rows_of(p)] = back_total(0, p)

    save_igrad = pltpu.make_async_copy(igrad.at[0 : sz.real], igrad_out, out_sem.at[2])
    save_igrad.start()

    squares += grads_done(0)
    save_grads[0].start()

    stats_dp[d, 0:1, :] = jnp.sum(squares, axis=0, keepdims=True)
    for l in (0, 1):
        stats_dp[d, l + 1 : l + 2, :] = jnp.sum(bias_sum[l], axis=0, keepdims=True)
    stats_dp[d, 3:8, :] = jnp.zeros((5, sz.out), F32)

    def stats_over_dp(k, slot):
        return same(stats_dp.at[slot], sd_send.at[k], sd_recv.at[k], (lax.rem(d + k, sz.dp), t))

    def stats_over_tensor(k, slot):
        return same(stats_t.at[slot], st_send.at[k], st_recv.at[k], (d, lax.rem(t + k, sz.tensor)))

    for k in range(1, sz.dp):
        stats_over_dp(k, d).start()
    for k in range(1, sz.dp):
        stats_over_dp(k, lax.rem(d + sz.dp - k, sz.dp)).wait_recv()
    total = stats_dp[0]
    for slot in range(1, sz.dp):
        total += stats_dp[slot]
    stats_t[t] = total
    for k in range(1, sz.tensor):
        stats_over_tensor(k, t).start()
    for k in range(1, sz.tensor):
        stats_over_tensor(k, lax.rem(t + sz.tensor - k, sz.tensor)).wait_recv()
    save_stats = pltpu.make_async_copy(stats_t, stats_out, out_sem.at[5])
    save_stats.start()

    for l in (0, 1):
        weights_sent(l)
        for k in far_steps:
            far_copy(l, k).wait_send()
        for k in range(sz.major):
            near_copy(l, k).wait_send()

        @pl.loop(0, sz.pieces)
        def _(p):
            part_copy(l, p).wait_send()
            for k in cross_steps:
                cross_copy(l, p, k).wait_send()

    gather_sent(0, frames, 0, whole)

    @pl.loop(0, sz.pieces)
    def _(p):
        gather_sent(1, acts, p, rows_of(p))

    for k in range(1, sz.dp):
        stats_over_dp(k, d).wait_send()
    for k in range(1, sz.tensor):
        stats_over_tensor(k, t).wait_send()
    for copy in (save_act4, save_act5, save_igrad, *save_grads, save_stats):
        copy.wait()


def train_step(sz, frames, item_mask, weights, biases, cotangent):
    sem = pltpu.SemaphoreType.DMA
    vmem = pltpu.VMEM
    maps = (sz.span, sz.out)
    block = (sz.own_in, sz.cols)
    shapes = [
        vmem((2, sz.rows, sz.out), F32),
        vmem((2, sz.real, sz.out), BF16),
        vmem(maps, BF16),
        vmem((2, sz.chan), F32),
        pltpu.SMEM((sz.items,), jnp.int32),
        vmem((sz.items, sz.out), F32),
        vmem((2, sz.dp, *block), sz.wire),
        vmem((sz.tensor, *maps), BF16),
        vmem((sz.tensor, *maps), BF16),
        vmem((sz.span + 2 * sz.halo, sz.cols), F32),
        vmem((3, *maps), F32),
        vmem(maps, F32),
        vmem(maps, BF16),
        vmem((3, sz.span + 2 * sz.halo, sz.out), F32),
        vmem((sz.span, sz.cols), BF16),
        vmem((2, sz.pairs, *maps), BF16),
        vmem((2, sz.pairs, *maps), BF16),
        vmem((sz.pairs, *maps), F32),
        vmem((2, sz.pairs, *maps), BF16),
        vmem((2, sz.pairs, *maps), BF16),
        vmem(maps, F32),
        vmem((2, sz.dp, *block), F32),
        vmem((2, sz.major, *block), sz.wire),
        vmem((2, sz.major, *block), sz.wire),
        vmem((2, sz.major, *block), sz.wire),
        vmem((2, sz.major, *block), sz.wire),
        vmem(block, F32),
        vmem((2, sz.rows, sz.out), F32),
        vmem((2, 8, sz.out), F32),
        vmem((sz.dp, 8, sz.out), F32),
        vmem((sz.tensor, 8, sz.out), F32),
        sem((6,)),
        sem((6,)),
        sem((2, sz.major)),
        sem((2, sz.major)),
        sem((2,)),
        sem((2, sz.major)),
        sem((2, sz.major)),
        sem((2, sz.pieces, sz.pairs)),
        sem((2, sz.pieces, sz.pairs)),
        sem((2, sz.pieces)),
        sem((2, sz.pieces)),
        sem((2, sz.pieces, sz.pairs)),
        sem((2, sz.pieces, sz.pairs)),
        sem((2, sz.pieces)),
        sem((2, sz.pieces)),
        sem((2, sz.pieces, sz.pairs)),
        sem((2, sz.pieces, sz.pairs)),
        sem((2, sz.major)),
        sem((2, sz.major)),
        sem((2, sz.major)),
        sem((2, sz.major)),
        sem((sz.dp,)),
        sem((sz.dp,)),
        sem((sz.tensor,)),
        sem((sz.tensor,)),
    ]
    anywhere = pl.BlockSpec(memory_space=pl.ANY)
    macs = 6 * sz.real * TAPS * sz.chan * sz.out
    rows = (sz.real, sz.out)
    return pl.pallas_call(
        functools.partial(body, sz),
        out_shape=[
            jax.ShapeDtypeStruct(rows, BF16),
            jax.ShapeDtypeStruct(rows, BF16),
            jax.ShapeDtypeStruct(rows, F32),
            jax.ShapeDtypeStruct((2, sz.rows, sz.out), F32),
            jax.ShapeDtypeStruct((sz.tensor, 8, sz.out), F32),
        ],
        in_specs=[anywhere] * 5,
        out_specs=[anywhere] * 5,
        scratch_shapes=shapes,
        compiler_params=pltpu.CompilerParams(
            collective_id=0, has_side_effects=True, vmem_limit_bytes=60 * 1024 * 1024
        ),
        cost_estimate=pl.CostEstimate(flops=2 * macs, bytes_accessed=6_000_000, transcendentals=0),
        name="train_step",
    )(frames, item_mask, weights, biases, cotangent)


def finish_body(
    sz,
    act4_ref,
    act5_ref,
    igrad_ref,
    grads_ref,
    stats_ref,
    weights_ref,
    first_ref,
    second_ref,
    biases,
    bias_first,
    bias_second,
    act4_out,
    act5_out,
    igrad_out,
    norm_out,
    weights_out,
    first_out,
    second_out,
    biases_out,
    bias_first_out,
    bias_second_out,
    stats,
    maps,
    igrad,
    olds,
    news,
    in_sem,
    out_sem,
    move_sem,
):
    sources = (weights_ref, grads_ref, first_ref, second_ref)
    targets = (weights_out, first_out, second_out)
    loads = [
        [pltpu.make_async_copy(ref.at[l], olds.at[l, i], in_sem.at[l, i]) for i, ref in enumerate(sources)]
        for l in (0, 1)
    ]
    stores = [
        [pltpu.make_async_copy(news.at[l, i], ref.at[l], out_sem.at[l, i]) for i, ref in enumerate(targets)]
        for l in (0, 1)
    ]
    moves = (
        (act4_ref, maps.at[0], act4_out),
        (act5_ref, maps.at[1], act5_out),
        (igrad_ref, igrad, igrad_out),
    )
    moves_in = [pltpu.make_async_copy(src, held, move_sem.at[0, i]) for i, (src, held, _) in enumerate(moves)]
    moves_out = [pltpu.make_async_copy(held, dst, move_sem.at[1, i]) for i, (_, held, dst) in enumerate(moves)]
    load_stats = pltpu.make_async_copy(stats_ref, stats, move_sem.at[0, 3])
    for copy in (load_stats, *loads[0], *moves_in, *loads[1]):
        copy.start()
    load_stats.wait()
    bias_grad = jnp.concatenate([stats[q, 1:3, :] for q in range(sz.tensor)], axis=1)
    squares = jnp.sum(stats[:, 0, :], axis=(0, 1), keepdims=True) + jnp.sum(
        bias_grad * bias_grad, axis=(0, 1), keepdims=True
    )
    grad_norm = jnp.sqrt(squares)
    factor = jnp.minimum(1.0, CLIP_NORM / (grad_norm + 1e-06))
    norm_out[...] = grad_norm
    biases_out[...], bias_first_out[...], bias_second_out[...] = adam_update(
        biases[...], bias_grad * factor, bias_first[...], bias_second[...], BIAS_RATE, 0.0
    )
    for l in (0, 1):
        for copy in loads[l]:
            copy.wait()
        news[l, 0], news[l, 1], news[l, 2] = adam_update(
            olds[l, 0], olds[l, 1] * factor, olds[l, 2], olds[l, 3], RATE, DECAY
        )
        for copy in stores[l]:
            copy.start()
        if l == 0:
            for here, there in zip(moves_in, moves_out):
                here.wait()
                there.start()
    for copy in (*stores[0], *stores[1], *moves_out):
        copy.wait()


def finish(sz, act4, act5, igrad, grads, stats, weights, first, second, biases, bias_first, bias_second):
    anywhere = pl.BlockSpec(memory_space=pl.ANY)
    inside = pl.BlockSpec(memory_space=pltpu.VMEM)
    outside = pl.BlockSpec(memory_space=pltpu.HBM)
    like = lambda x: jax.ShapeDtypeStruct(x.shape, x.dtype)
    sem = pltpu.SemaphoreType.DMA
    return pl.pallas_call(
        functools.partial(finish_body, sz),
        out_shape=[
            like(act4),
            like(act5),
            like(igrad),
            jax.ShapeDtypeStruct((1, 1), F32),
            like(weights),
            like(first),
            like(second),
            like(biases),
            like(bias_first),
            like(bias_second),
        ],
        in_specs=[outside] * 5 + [anywhere] * 3 + [inside] * 3,
        out_specs=[outside] * 3 + [inside] + [outside] * 3 + [inside] * 3,
        scratch_shapes=[
            pltpu.VMEM((sz.tensor, 8, sz.out), F32),
            pltpu.VMEM((2, sz.real, sz.out), BF16),
            pltpu.VMEM((sz.real, sz.out), F32),
            pltpu.VMEM((2, 4, sz.rows, sz.out), F32),
            pltpu.VMEM((2, 3, sz.rows, sz.out), F32),
            sem((2, 4)),
            sem((2, 3)),
            sem((2, 4)),
        ],
        compiler_params=pltpu.CompilerParams(vmem_limit_bytes=60 * 1024 * 1024),
        cost_estimate=pl.CostEstimate(flops=5_000_000, bytes_accessed=7_000_000, transcendentals=0),
        name="clip_and_adamw",
    )(act4, act5, igrad, grads, stats, weights, first, second, biases, bias_first, bias_second)


def on_device(
    mesh,
    frames,
    item_mask,
    weights,
    biases,
    cotangent,
    weight_first,
    weight_second,
    bias_first,
    bias_second,
):
    sz = Sizes(mesh, frames.shape, weights.shape)

    def flat(maps):
        return jnp.transpose(maps, (1, 2, 0, 3)).reshape(sz.real, sz.out)

    def square(rows):
        return jnp.transpose(rows.reshape(sz.height, sz.width, sz.items, sz.out), (2, 0, 1, 3))

    made = train_step(sz, flat(frames), item_mask, weights, biases, flat(cotangent))
    act_four, act_five, input_grad, grad_norm, *rest = finish(
        sz, *made, weights, weight_first, weight_second, biases, bias_first, bias_second
    )
    return (square(act_four), square(act_five), square(input_grad), grad_norm.reshape(()), *rest)


def solution(mesh):
    split = P("dp", None, None, "tensor")
    rows = P(None, "dp", "tensor")
    in_specs = (split, P("dp"), rows, P(), split, rows, rows, P(), P())
    out_specs = (split, split, split, P(), rows, rows, rows, P(), P(), P())
    return jax.shard_map(
        functools.partial(on_device, mesh), mesh=mesh, in_specs=in_specs, out_specs=out_specs, check_vma=False
    )
```

```python
import functools
import math

import jax
import jax.numpy as jnp
from jax import lax
from jax.experimental import pallas as pl
from jax.experimental.pallas import tpu as pltpu
from jax.sharding import PartitionSpec as P

STEP = 5
CLIP_NORM = 1.0
BETA_ONE = 0.5
BETA_TWO = 0.5
RATE = 0.01
BIAS_RATE = 0.03
DECAY = 0.1
EPSILON = 1e-08

MESH = pl.DeviceIdType.MESH
BF16 = jnp.bfloat16
F32 = jnp.float32
ROOT = math.sqrt(2.0 / math.pi)
CUBE = 0.044715
TAPS = 9
WIDE = 256


def gelu_parts(value):
    square = value * value
    th = jnp.tanh(ROOT * value * (1.0 + CUBE * square))
    half = 0.5 * (1.0 + th)
    slope = half + 0.5 * value * (1.0 - th * th) * (ROOT * (1.0 + 3.0 * CUBE * square))
    return value * half, slope


def flip_bits(index, mask):
    bit = 1
    while bit <= mask:
        if mask & bit:
            index = index + bit - 2 * bit * lax.rem(lax.div(index, bit), 2)
        bit *= 2
    return index


def adam_update(param, grad, first, second, rate, decay):
    first_new = BETA_ONE * first + (1.0 - BETA_ONE) * grad
    second_new = BETA_TWO * second + (1.0 - BETA_TWO) * grad * grad
    corrected = first_new * (1.0 / (1.0 - BETA_ONE**STEP))
    scaled = jnp.sqrt(second_new * (1.0 / (1.0 - BETA_TWO**STEP))) + EPSILON
    return (param - rate * (corrected / scaled + decay * param), first_new, second_new)


class Sizes:
    def __init__(self, mesh, frames_shape, weights_shape):
        self.dp = mesh.shape["dp"]
        self.tensor = mesh.shape["tensor"]
        self.items, self.height, self.width, self.out = frames_shape
        self.chan = self.out * self.tensor
        self.rows = weights_shape[1]
        self.own_in = self.rows // TAPS
        self.cols = TAPS * self.out
        self.major = self.dp // 2
        self.pairs = self.tensor // 2
        self.slots = self.dp // self.tensor
        self.spots = self.height * self.width
        self.real = self.spots * self.items
        self.span = -(-self.real // 16) * 16
        self.halo = (self.width + 1) * self.items
        self.pieces = next(n for n in (5, 4, 3, 2, 1) if self.span // 16 % n == 0)
        self.piece = self.span // self.pieces
        self.groups = ((0, self.pieces // 2), (self.pieces // 2, self.pieces))
        self.wire = BF16 if self.own_in % 16 == 0 else F32
        cut = (TAPS + 1) // 2 * self.out
        self.parts = ((0, cut), (cut, self.cols))
        self.devices = self.dp * self.tensor


def body(
    sz,
    frames_ref,
    mask_ref,
    weights_ref,
    biases_ref,
    cot_ref,
    act4_out,
    act5_out,
    igrad_out,
    grads_out,
    stats_out,
    w_in,
    stage,
    cot,
    biases,
    mask,
    keep,
    w_all,
    frames,
    acts,
    spread,
    edges,
    slope4,
    act5,
    shifted,
    deltas,
    part_send,
    part_recv,
    part_own,
    cross_send,
    cross_recv,
    igrad,
    kgrad,
    near_send,
    near_recv,
    far_send,
    far_recv,
    shard,
    rows_out,
    bias_sum,
    stats_all,
    stats_t,
    local_sem,
    out_sem,
    wu_send,
    wd_send,
    wz_recv,
    wy_send,
    wy_recv,
    ax_send,
    ax_recv,
    as_send,
    as_recv,
    af_send,
    af_recv,
    rs_send,
    rs_recv,
    rx_send,
    rx_recv,
    gy_send,
    gy_recv,
    gz_send,
    gz_recv,
    st_send,
    st_recv,
):
    d = lax.axis_index("dp")
    t = lax.axis_index("tensor")
    major, minor = lax.div(d, 2), lax.rem(d, 2)
    near = (2 * major + 1 - minor, t)
    pair, side = lax.div(t, 2), lax.rem(t, 2)
    sibling = (d, 2 * pair + 1 - side)

    def far_slot(k):
        return 2 * flip_bits(major, k) + minor

    def near_slot(k):
        return 2 * flip_bits(major, k) + 1 - minor

    def far(k):
        return (far_slot(k), t)

    def cross_rank(k):
        return 2 * lax.rem(pair + k, sz.pairs) + side

    def cross_from(k):
        return 2 * lax.rem(pair + sz.pairs - k, sz.pairs) + side

    def remote(src, dst, send, recv, device):
        return pltpu.make_async_remote_copy(
            src_ref=src, dst_ref=dst, send_sem=send, recv_sem=recv, device_id=device, device_id_type=MESH
        )

    def same(block, send, recv, device):
        return remote(block, block, send, recv, device)

    all_pieces = range(sz.pieces)

    def rows_of(p):
        return pl.ds(pl.multiple_of(p * sz.piece, 16), sz.piece)

    far_steps = range(1, sz.major)
    cross_steps = range(1, sz.pairs)
    above, below = major + 1 < sz.major, major > 0
    up, down = (2 * (major + 1) + minor, t), (2 * (major - 1) + minor, t)

    barrier = pltpu.get_barrier_semaphore()

    def greet(device):
        pl.semaphore_signal(barrier, inc=1, device_id=device, device_id_type=MESH)

    pl.when(above)(lambda: greet(up))
    pl.when(below)(lambda: greet(down))
    greet(near)
    for k in cross_steps:
        greet((d, cross_rank(k)))
    greet(sibling)

    load_w = [pltpu.make_async_copy(weights_ref.at[l], w_in.at[l], local_sem.at[l]) for l in (0, 1)]
    load_frames = pltpu.make_async_copy(frames_ref, stage.at[0], local_sem.at[2])
    load_cot = pltpu.make_async_copy(cot_ref, stage.at[1], local_sem.at[3])
    load_biases = pltpu.make_async_copy(biases_ref, biases, local_sem.at[4])
    load_mask = pltpu.make_async_copy(mask_ref, mask, local_sem.at[5])
    for copy in (load_w[0], load_frames, load_w[1], load_cot, load_biases, load_mask):
        copy.start()

    def weight_block(l, part, slot):
        first, last = sz.parts[part]
        return w_all.at[l, slot, :, first:last]

    def weight_up(l, part, source):
        return same(
            weight_block(l, part, 2 * source + minor), wu_send.at[l, part, source], wz_recv.at[l, part, source], up
        )

    def weight_down(l, part, source):
        return same(
            weight_block(l, part, 2 * source + minor), wd_send.at[l, part, source], wz_recv.at[l, part, source], down
        )

    def weight_over(l, part, source):
        return same(
            weight_block(l, part, 2 * source + minor), wy_send.at[l, part, source], wy_recv.at[l, part, source], near
        )

    def weights_out(l, part):
        pl.when(above)(weight_up(l, part, major).start)
        pl.when(below)(weight_down(l, part, major).start)

    def weights_on(l, part):
        @pl.loop(1, sz.major)
        def _(step):
            @pl.when(major - step >= 0)
            def _():
                source = major - step
                weight_up(l, part, source).wait_recv()
                pl.when(above)(weight_up(l, part, source).start)
                weight_over(l, part, source).start()

            @pl.when(major + step < sz.major)
            def _():
                source = major + step
                weight_down(l, part, source).wait_recv()
                pl.when(below)(weight_down(l, part, source).start)
                weight_over(l, part, source).start()

    def weights_here(l, part):
        @pl.loop(0, sz.major)
        def _(source):
            same(
                weight_block(l, part, 2 * source + 1 - minor),
                wy_send.at[l, part, source],
                wy_recv.at[l, part, source],
                near,
            ).wait_recv()

    def weights_sent(l, part):
        @pl.loop(0, sz.major)
        def _(source):
            weight_over(l, part, source).wait_send()

            @pl.when(jnp.logical_and(source <= major, above))
            def _():
                weight_up(l, part, source).wait_send()

            @pl.when(jnp.logical_and(source >= major, below))
            def _():
                weight_down(l, part, source).wait_send()

    def round_weights(l):
        load_w[l].wait()
        for tap in range(TAPS):
            w_all[l, d, :, tap * sz.out : (tap + 1) * sz.out] = w_in[
                l, pl.ds(tap, sz.own_in, stride=TAPS), :
            ].astype(sz.wire)

    def gather_sends(g, maps, p, rows):
        own = maps.at[t, rows]
        out = [same(own, ax_send.at[g, p, k], ax_recv.at[g, p, k], (d, cross_rank(k))) for k in cross_steps]
        out.append(same(own, as_send.at[g, p], as_recv.at[g, p], sibling))
        return out

    def gather_forward(g, maps, p, rows, k):
        return same(maps.at[cross_from(k), rows], af_send.at[g, p, k], af_recv.at[g, p, k], sibling)

    def gather_pass_on(g, maps, p, rows):
        for k in cross_steps:
            same(maps.at[cross_from(k), rows], ax_send.at[g, p, k], ax_recv.at[g, p, k], sibling).wait_recv()
            gather_forward(g, maps, p, rows, k).start()

    def gather_here(g, maps, p, rows):
        same(maps.at[sibling[1], rows], as_send.at[g, p], as_recv.at[g, p], sibling).wait_recv()
        for k in cross_steps:
            rank = 2 * lax.rem(pair + sz.pairs - k, sz.pairs) + 1 - side
            same(maps.at[rank, rows], af_send.at[g, p, k], af_recv.at[g, p, k], sibling).wait_recv()

    def gather_sent(g, maps, p, rows):
        for copy in gather_sends(g, maps, p, rows):
            copy.wait_send()
        for k in cross_steps:
            gather_forward(g, maps, p, rows, k).wait_send()

    whole = pl.ds(0, sz.span)

    def product(l, part, maps, group):
        rows = slice(group[0] * sz.piece, group[1] * sz.piece)
        left = jnp.concatenate([maps[q, rows] for q in range(sz.tensor)], axis=1)
        first, last = sz.parts[part]
        for start in range(first, last, WIDE):
            stop = min(start + WIDE, last)
            right = w_all[l, :, :, start:stop].reshape(sz.chan, stop - start).astype(BF16)
            spread[sz.halo + rows.start : sz.halo + rows.stop, start:stop] = jnp.dot(
                left, right, preferred_element_type=F32
            )

    def own_bias(l):
        return biases[l : l + 1, pl.ds(pl.multiple_of(t * sz.out, sz.out), sz.out)]

    def shifted_sum(p):
        sums = []
        for b in range(3):
            total = None
            for a in range(3):
                shift = sz.items * (sz.width * (a - 1) + b - 1)
                tap = 3 * a + b
                rows = pl.ds(pl.multiple_of(p * sz.piece + sz.halo + shift, 8), sz.piece)
                term = spread[rows, tap * sz.out : (tap + 1) * sz.out]
                total = term if total is None else total + term
            sums.append(total)
        return sums[1] + sums[0] * edges[0, rows_of(p)] + sums[2] * edges[1, rows_of(p)]

    def note_delta(l, p, delta):
        bias_sum[l] += jnp.sum(delta.reshape(sz.piece // 8, 8, sz.out), axis=0)
        rows = pl.ds(pl.multiple_of(p * sz.piece + sz.halo, 8), sz.piece)
        shifted[0, rows] = delta * edges[0, rows_of(p)]
        shifted[1, rows] = delta
        shifted[2, rows] = delta * edges[1, rows_of(p)]

    def spread_delta():
        @pl.loop(0, sz.pieces)
        def _(p):
            for a in range(3):
                for b in range(3):
                    shift = sz.items * (sz.width * (a - 1) + b - 1)
                    tap = 3 * a + b
                    rows = pl.ds(pl.multiple_of(p * sz.piece + sz.halo - shift, 8), sz.piece)
                    deltas[rows_of(p), tap * sz.out : (tap + 1) * sz.out] = shifted[b, rows].astype(BF16)

    def finish_four(first, last):
        @pl.loop(first, last)
        def _(p):
            act, slope = gelu_parts(shifted_sum(p) + own_bias(0))
            acts[t, rows_of(p)] = (act * edges[2, rows_of(p)]).astype(BF16)
            slope4[rows_of(p)] = slope * edges[2, rows_of(p)]
            for copy in gather_sends(1, acts, p, rows_of(p)):
                copy.start()

    def by_item(value):
        return (value.reshape(sz.piece // sz.items, sz.items, sz.out) * keep[...]).reshape(sz.piece, sz.out)

    def finish_five(first, last):
        @pl.loop(first, last)
        def _(p):
            act, slope = gelu_parts(shifted_sum(p) + own_bias(1))
            act5[rows_of(p)] = by_item(act).astype(BF16)
            delta = (by_item(cot[rows_of(p)].astype(F32)) * slope).astype(BF16).astype(F32)
            note_delta(1, p, delta)

    def part_copy(l, p):
        rows = rows_of(p)
        return remote(
            part_send.at[l, :, rows], part_recv.at[l, :, rows], rs_send.at[l, p], rs_recv.at[l, p], sibling
        )

    def cross_copy(l, p, k):
        rows = rows_of(p)
        return remote(
            cross_send.at[l, k, rows],
            cross_recv.at[l, k, rows],
            rx_send.at[l, p, k],
            rx_recv.at[l, p, k],
            (d, cross_rank(k)),
        )

    def back_product(l, group, which):
        blocks = [
            w_all[l, pl.ds((2 * j + which) * sz.slots, sz.slots)].reshape(sz.out, sz.cols) for j in range(sz.pairs)
        ]
        right = jnp.concatenate(blocks, axis=0).astype(BF16)
        left = deltas[group[0] * sz.piece : group[1] * sz.piece]
        out = lax.dot_general(left, right, (((1,), (1,)), ((), ())), preferred_element_type=F32)
        return [out[:, j * sz.out : (j + 1) * sz.out] for j in range(sz.pairs)]

    def back_to_sibling(l, group):
        rows = slice(group[0] * sz.piece, group[1] * sz.piece)
        for j, block in enumerate(back_product(l, group, 1 - side)):
            part_send[l, j, rows] = block.astype(BF16)
        for p in range(*group):
            part_copy(l, p).start()

    def back_own(l, group):
        rows = slice(group[0] * sz.piece, group[1] * sz.piece)
        for j, block in enumerate(back_product(l, group, side)):
            part_own[j, rows] = block

    def back_across(l, group):
        @pl.loop(*group)
        def _(p):
            part_copy(l, p).wait_recv()
            for k in cross_steps:
                j = lax.rem(pair + k, sz.pairs)
                total = part_own[j, rows_of(p)] + part_recv[l, j, rows_of(p)].astype(F32)
                cross_send[l, k, rows_of(p)] = total.astype(BF16)
                cross_copy(l, p, k).start()

    def back_products(l):
        one, two = sz.groups
        back_to_sibling(l, one)
        back_own(l, one)
        back_to_sibling(l, two)
        back_across(l, one)
        back_own(l, two)
        back_across(l, two)

    def back_total(l, p):
        total = part_own[pair, rows_of(p)] + part_recv[l, pair, rows_of(p)].astype(F32)
        for k in cross_steps:
            cross_copy(l, p, k).wait_recv()
            total += cross_recv[l, k, rows_of(p)].astype(F32)
        return total

    def near_copy(l, k):
        return remote(near_send.at[l, k], near_recv.at[l, k], gy_send.at[l, k], gy_recv.at[l, k], near)

    def far_copy(l, k):
        return remote(far_send.at[l, k], far_recv.at[l, k], gz_send.at[l, k], gz_recv.at[l, k], far(k))

    half = sz.tensor // 2
    far_half = [k for k in far_steps if k >= sz.major // 2]
    near_half = [k for k in far_steps if k < sz.major // 2]

    def grads_half(l, maps, other):
        own = lax.div(major, sz.major // 2)
        first = (1 - own if other else own) * half
        left = jnp.concatenate([maps[first + q] for q in range(half)], axis=1)
        into = pl.ds(first * sz.slots, half * sz.slots)
        for start in range(0, sz.cols, WIDE):
            stop = min(start + WIDE, sz.cols)
            product = lax.dot_general(left, deltas[:, start:stop], (((0,), (0,)), ((), ())), preferred_element_type=F32)
            kgrad[l, into, :, start:stop] = product.reshape(half * sz.slots, sz.own_in, stop - start)
        for k in far_half if other else [*near_half, 0]:
            near_send[l, k] = kgrad[l, near_slot(k)].astype(sz.wire)
            near_copy(l, k).start()

    def grads_far(l, k):
        near_copy(l, k).wait_recv()
        far_send[l, k] = (kgrad[l, far_slot(k)] + near_recv[l, k].astype(F32)).astype(sz.wire)
        far_copy(l, k).start()

    def grads_done(l):
        near_copy(l, 0).wait_recv()
        for k in far_steps:
            far_copy(l, k).wait_recv()
        total = kgrad[l, d] + near_recv[l, 0].astype(F32)
        for k in far_steps:
            total += far_recv[l, k].astype(F32)
        shard[...] = total
        squares = jnp.sum((total * total).reshape(sz.own_in // 8, 8, sz.cols), axis=0)
        for tap in range(TAPS):
            rows_out[l, pl.ds(tap, sz.own_in, stride=TAPS), :] = shard[:, tap * sz.out : (tap + 1) * sz.out]
        return sum(squares[:, tap * sz.out : (tap + 1) * sz.out] for tap in range(TAPS))

    round_weights(0)
    joined = 1 + sz.pairs + above.astype(jnp.int32) + below.astype(jnp.int32)
    pl.semaphore_wait(barrier, joined)
    for part in (0, 1):
        weight_over(0, part, major).start()
        weights_out(0, part)
    tail = sz.span - 16
    frames[t, tail:] = jnp.zeros((16, sz.out), BF16)
    load_frames.wait()
    frames[t, 0 : sz.real] = stage[0]
    for copy in gather_sends(0, frames, 0, whole):
        copy.start()
    round_weights(1)
    for part in (0, 1):
        weight_over(1, part, major).start()

    rest = sz.halo + sz.span
    for first in (0, rest):
        spread[first : first + sz.halo, :] = jnp.zeros((sz.halo, sz.cols), F32)
        shifted[:, first : first + sz.halo, :] = jnp.zeros((3, sz.halo, sz.out), F32)
    edges[...] = jnp.ones_like(edges)
    nothing = jnp.zeros((sz.items, sz.out), F32)
    for i in range(sz.height):
        for e, j in ((0, 0), (1, sz.width - 1)):
            first = (i * sz.width + j) * sz.items
            edges[e, first : first + sz.items, :] = nothing
    edges[2, sz.real :, :] = jnp.zeros((sz.span - sz.real, sz.out), F32)
    bias_sum[...] = jnp.zeros_like(bias_sum)

    cot[tail:] = jnp.zeros((16, sz.out), BF16)
    load_cot.wait()
    cot[0 : sz.real] = stage[1]
    load_biases.wait()
    load_mask.wait()
    item = lax.broadcasted_iota(jnp.int32, (sz.items, sz.out), 0)
    kept = jnp.zeros((sz.items, sz.out), F32)
    for n in range(sz.items):
        kept = jnp.where(item == n, mask[n].astype(F32), kept)
    keep[...] = kept

    one, two = sz.groups
    weights_on(0, 0)
    for part in (0, 1):
        weights_out(1, part)
    gather_pass_on(0, frames, 0, whole)
    weights_on(0, 1)
    gather_here(0, frames, 0, whole)
    weights_here(0, 0)
    product(0, 0, frames, one)
    product(0, 0, frames, two)
    weights_here(0, 1)
    product(0, 1, frames, one)
    finish_four(0, one[1] - 1)
    product(0, 1, frames, two)
    finish_four(one[1] - 1, sz.pieces)

    weights_on(1, 0)
    stage[0] = acts[t, 0 : sz.real]
    save_act4 = pltpu.make_async_copy(stage.at[0], act4_out, out_sem.at[0])
    save_act4.start()
    for p in range(*one):
        gather_pass_on(1, acts, p, rows_of(p))
    weights_on(1, 1)
    for p in range(*two):
        gather_pass_on(1, acts, p, rows_of(p))
    for p in all_pieces:
        gather_here(1, acts, p, rows_of(p))
    weights_here(1, 0)
    product(1, 0, acts, one)
    product(1, 0, acts, two)
    weights_here(1, 1)
    product(1, 1, acts, one)
    finish_five(0, one[1] - 1)
    product(1, 1, acts, two)
    finish_five(one[1] - 1, sz.pieces)
    spread_delta()

    grads_half(1, acts, True)
    back_products(1)
    grads_half(1, acts, False)
    stage[1] = act5[0 : sz.real]
    save_act5 = pltpu.make_async_copy(stage.at[1], act5_out, out_sem.at[1])
    save_act5.start()
    for k in far_half:
        grads_far(1, k)

    @pl.loop(0, sz.pieces)
    def _(p):
        note_delta(0, p, (back_total(1, p) * slope4[rows_of(p)]).astype(BF16).astype(F32))

    spread_delta()
    grads_half(0, frames, True)
    for k in near_half:
        grads_far(1, k)
    grads_half(0, frames, False)
    back_products(0)
    for k in far_half:
        grads_far(0, k)
    squares = grads_done(1)
    save_grads = [pltpu.make_async_copy(rows_out.at[l], grads_out.at[l], out_sem.at[3 + l]) for l in (0, 1)]
    save_grads[1].start()
    for k in near_half:
        grads_far(0, k)

    @pl.loop(0, sz.pieces)
    def _(p):
        igrad[rows_of(p)] = back_total(0, p)

    save_igrad = pltpu.make_async_copy(igrad.at[0 : sz.real], igrad_out, out_sem.at[2])
    save_igrad.start()

    squares += grads_done(0)
    save_grads[0].start()

    me = d * sz.tensor + t
    stats_all[me, 0:1, :] = jnp.sum(squares, axis=0, keepdims=True)
    for l in (0, 1):
        stats_all[me, l + 1 : l + 2, :] = jnp.sum(bias_sum[l], axis=0, keepdims=True)
    stats_all[me, 3:8, :] = jnp.zeros((5, sz.out), F32)

    def stats_copy(k, slot):
        other = lax.rem(me + k, sz.devices)
        device = (lax.div(other, sz.tensor), lax.rem(other, sz.tensor))
        return same(stats_all.at[slot], st_send.at[k], st_recv.at[k], device)

    @pl.loop(1, sz.devices)
    def _(k):
        stats_copy(k, me).start()

    @pl.loop(1, sz.devices)
    def _(k):
        stats_copy(k, lax.rem(me + sz.devices - k, sz.devices)).wait_recv()

    for q in range(sz.tensor):
        total = stats_all[q]
        for slot in range(q + sz.tensor, sz.devices, sz.tensor):
            total += stats_all[slot]
        stats_t[q] = total
    save_stats = pltpu.make_async_copy(stats_t, stats_out, out_sem.at[5])
    save_stats.start()

    for l in (0, 1):
        for part in (0, 1):
            weights_sent(l, part)
        for k in far_steps:
            far_copy(l, k).wait_send()
        for k in range(sz.major):
            near_copy(l, k).wait_send()

        @pl.loop(0, sz.pieces)
        def _(p):
            part_copy(l, p).wait_send()
            for k in cross_steps:
                cross_copy(l, p, k).wait_send()

    gather_sent(0, frames, 0, whole)

    @pl.loop(0, sz.pieces)
    def _(p):
        gather_sent(1, acts, p, rows_of(p))

    @pl.loop(1, sz.devices)
    def _(k):
        stats_copy(k, me).wait_send()

    for copy in (save_act4, save_act5, save_igrad, *save_grads, save_stats):
        copy.wait()


def train_step(sz, frames, item_mask, weights, biases, cotangent):
    sem = pltpu.SemaphoreType.DMA
    vmem = pltpu.VMEM
    maps = (sz.span, sz.out)
    block = (sz.own_in, sz.cols)
    shapes = [
        vmem((2, sz.rows, sz.out), F32),
        vmem((2, sz.real, sz.out), BF16),
        vmem(maps, BF16),
        vmem((2, sz.chan), F32),
        pltpu.SMEM((sz.items,), jnp.int32),
        vmem((sz.items, sz.out), F32),
        vmem((2, sz.dp, *block), sz.wire),
        vmem((sz.tensor, *maps), BF16),
        vmem((sz.tensor, *maps), BF16),
        vmem((sz.span + 2 * sz.halo, sz.cols), F32),
        vmem((3, *maps), F32),
        vmem(maps, F32),
        vmem(maps, BF16),
        vmem((3, sz.span + 2 * sz.halo, sz.out), F32),
        vmem((sz.span, sz.cols), BF16),
        vmem((2, sz.pairs, *maps), BF16),
        vmem((2, sz.pairs, *maps), BF16),
        vmem((sz.pairs, *maps), F32),
        vmem((2, sz.pairs, *maps), BF16),
        vmem((2, sz.pairs, *maps), BF16),
        vmem(maps, F32),
        vmem((2, sz.dp, *block), F32),
        vmem((2, sz.major, *block), sz.wire),
        vmem((2, sz.major, *block), sz.wire),
        vmem((2, sz.major, *block), sz.wire),
        vmem((2, sz.major, *block), sz.wire),
        vmem(block, F32),
        vmem((2, sz.rows, sz.out), F32),
        vmem((2, 8, sz.out), F32),
        vmem((sz.devices, 8, sz.out), F32),
        vmem((sz.tensor, 8, sz.out), F32),
        sem((6,)),
        sem((6,)),
        sem((2, 2, sz.major)),
        sem((2, 2, sz.major)),
        sem((2, 2, sz.major)),
        sem((2, 2, sz.major)),
        sem((2, 2, sz.major)),
        sem((2, sz.pieces, sz.pairs)),
        sem((2, sz.pieces, sz.pairs)),
        sem((2, sz.pieces)),
        sem((2, sz.pieces)),
        sem((2, sz.pieces, sz.pairs)),
        sem((2, sz.pieces, sz.pairs)),
        sem((2, sz.pieces)),
        sem((2, sz.pieces)),
        sem((2, sz.pieces, sz.pairs)),
        sem((2, sz.pieces, sz.pairs)),
        sem((2, sz.major)),
        sem((2, sz.major)),
        sem((2, sz.major)),
        sem((2, sz.major)),
        sem((sz.devices,)),
        sem((sz.devices,)),
    ]
    anywhere = pl.BlockSpec(memory_space=pl.ANY)
    macs = 6 * sz.real * TAPS * sz.chan * sz.out
    rows = (sz.real, sz.out)
    return pl.pallas_call(
        functools.partial(body, sz),
        out_shape=[
            jax.ShapeDtypeStruct(rows, BF16),
            jax.ShapeDtypeStruct(rows, BF16),
            jax.ShapeDtypeStruct(rows, F32),
            jax.ShapeDtypeStruct((2, sz.rows, sz.out), F32),
            jax.ShapeDtypeStruct((sz.tensor, 8, sz.out), F32),
        ],
        in_specs=[anywhere] * 5,
        out_specs=[anywhere] * 5,
        scratch_shapes=shapes,
        compiler_params=pltpu.CompilerParams(
            collective_id=0, has_side_effects=True, vmem_limit_bytes=60 * 1024 * 1024
        ),
        cost_estimate=pl.CostEstimate(flops=2 * macs, bytes_accessed=6_000_000, transcendentals=0),
        name="train_step",
    )(frames, item_mask, weights, biases, cotangent)


def finish_body(
    sz,
    act4_ref,
    act5_ref,
    igrad_ref,
    grads_ref,
    stats_ref,
    weights_ref,
    first_ref,
    second_ref,
    biases,
    bias_first,
    bias_second,
    act4_out,
    act5_out,
    igrad_out,
    norm_out,
    weights_out,
    first_out,
    second_out,
    biases_out,
    bias_first_out,
    bias_second_out,
    stats,
    maps,
    igrad,
    olds,
    news,
    in_sem,
    out_sem,
    move_sem,
):
    sources = (weights_ref, grads_ref, first_ref, second_ref)
    targets = (weights_out, first_out, second_out)
    loads = [
        [pltpu.make_async_copy(ref.at[l], olds.at[l, i], in_sem.at[l, i]) for i, ref in enumerate(sources)]
        for l in (0, 1)
    ]
    stores = [
        [pltpu.make_async_copy(news.at[l, i], ref.at[l], out_sem.at[l, i]) for i, ref in enumerate(targets)]
        for l in (0, 1)
    ]
    moves = (
        (act4_ref, maps.at[0], act4_out),
        (act5_ref, maps.at[1], act5_out),
        (igrad_ref, igrad, igrad_out),
    )
    moves_in = [pltpu.make_async_copy(src, held, move_sem.at[0, i]) for i, (src, held, _) in enumerate(moves)]
    moves_out = [pltpu.make_async_copy(held, dst, move_sem.at[1, i]) for i, (_, held, dst) in enumerate(moves)]
    load_stats = pltpu.make_async_copy(stats_ref, stats, move_sem.at[0, 3])
    for copy in (load_stats, *loads[0], *moves_in, *loads[1]):
        copy.start()
    load_stats.wait()
    bias_grad = jnp.concatenate([stats[q, 1:3, :] for q in range(sz.tensor)], axis=1)
    squares = jnp.sum(stats[:, 0, :], axis=(0, 1), keepdims=True) + jnp.sum(
        bias_grad * bias_grad, axis=(0, 1), keepdims=True
    )
    grad_norm = jnp.sqrt(squares)
    factor = jnp.minimum(1.0, CLIP_NORM / (grad_norm + 1e-06))
    norm_out[...] = grad_norm
    biases_out[...], bias_first_out[...], bias_second_out[...] = adam_update(
        biases[...], bias_grad * factor, bias_first[...], bias_second[...], BIAS_RATE, 0.0
    )
    for l in (0, 1):
        for copy in loads[l]:
            copy.wait()
        news[l, 0], news[l, 1], news[l, 2] = adam_update(
            olds[l, 0], olds[l, 1] * factor, olds[l, 2], olds[l, 3], RATE, DECAY
        )
        for copy in stores[l]:
            copy.start()
        if l == 0:
            for here, there in zip(moves_in, moves_out):
                here.wait()
                there.start()
    for copy in (*stores[0], *stores[1], *moves_out):
        copy.wait()


def finish(sz, act4, act5, igrad, grads, stats, weights, first, second, biases, bias_first, bias_second):
    anywhere = pl.BlockSpec(memory_space=pl.ANY)
    inside = pl.BlockSpec(memory_space=pltpu.VMEM)
    outside = pl.BlockSpec(memory_space=pltpu.HBM)
    like = lambda x: jax.ShapeDtypeStruct(x.shape, x.dtype)
    sem = pltpu.SemaphoreType.DMA
    return pl.pallas_call(
        functools.partial(finish_body, sz),
        out_shape=[
            like(act4),
            like(act5),
            like(igrad),
            jax.ShapeDtypeStruct((1, 1), F32),
            like(weights),
            like(first),
            like(second),
            like(biases),
            like(bias_first),
            like(bias_second),
        ],
        in_specs=[outside] * 5 + [anywhere] * 3 + [inside] * 3,
        out_specs=[outside] * 3 + [inside] + [outside] * 3 + [inside] * 3,
        scratch_shapes=[
            pltpu.VMEM((sz.tensor, 8, sz.out), F32),
            pltpu.VMEM((2, sz.real, sz.out), BF16),
            pltpu.VMEM((sz.real, sz.out), F32),
            pltpu.VMEM((2, 4, sz.rows, sz.out), F32),
            pltpu.VMEM((2, 3, sz.rows, sz.out), F32),
            sem((2, 4)),
            sem((2, 3)),
            sem((2, 4)),
        ],
        compiler_params=pltpu.CompilerParams(vmem_limit_bytes=60 * 1024 * 1024),
        cost_estimate=pl.CostEstimate(flops=5_000_000, bytes_accessed=7_000_000, transcendentals=0),
        name="clip_and_adamw",
    )(act4, act5, igrad, grads, stats, weights, first, second, biases, bias_first, bias_second)


def on_device(
    mesh,
    frames,
    item_mask,
    weights,
    biases,
    cotangent,
    weight_first,
    weight_second,
    bias_first,
    bias_second,
):
    sz = Sizes(mesh, frames.shape, weights.shape)

    def flat(maps):
        return jnp.transpose(maps, (1, 2, 0, 3)).reshape(sz.real, sz.out)

    def square(rows):
        return jnp.transpose(rows.reshape(sz.height, sz.width, sz.items, sz.out), (2, 0, 1, 3))

    made = train_step(sz, flat(frames), item_mask, weights, biases, flat(cotangent))
    act_four, act_five, input_grad, grad_norm, *rest = finish(
        sz, *made, weights, weight_first, weight_second, biases, bias_first, bias_second
    )
    return (square(act_four), square(act_five), square(input_grad), grad_norm.reshape(()), *rest)


def solution(mesh):
    split = P("dp", None, None, "tensor")
    rows = P(None, "dp", "tensor")
    in_specs = (split, P("dp"), rows, P(), split, rows, rows, P(), P())
    out_specs = (split, split, split, P(), rows, rows, rows, P(), P(), P())
    return jax.shard_map(
        functools.partial(on_device, mesh), mesh=mesh, in_specs=in_specs, out_specs=out_specs, check_vma=False
    )
```

```python
import functools
import math

import jax
import jax.numpy as jnp
from jax import lax
from jax.experimental import pallas as pl
from jax.experimental.pallas import tpu as pltpu
from jax.sharding import PartitionSpec as P

STEP = 5
CLIP_NORM = 1.0
BETA_ONE = 0.5
BETA_TWO = 0.5
RATE = 0.01
BIAS_RATE = 0.03
DECAY = 0.1
EPSILON = 1e-08

MESH = pl.DeviceIdType.MESH
BF16 = jnp.bfloat16
F32 = jnp.float32
ROOT = math.sqrt(2.0 / math.pi)
CUBE = 0.044715
TAPS = 9
WIDE = 256


def gelu_parts(value):
    square = value * value
    th = jnp.tanh(ROOT * value * (1.0 + CUBE * square))
    half = 0.5 * (1.0 + th)
    slope = half + 0.5 * value * (1.0 - th * th) * (ROOT * (1.0 + 3.0 * CUBE * square))
    return value * half, slope


def flip_bits(index, mask):
    bit = 1
    while bit <= mask:
        if mask & bit:
            index = index + bit - 2 * bit * lax.rem(lax.div(index, bit), 2)
        bit *= 2
    return index


def adam_update(param, grad, first, second, rate, decay):
    first_new = BETA_ONE * first + (1.0 - BETA_ONE) * grad
    second_new = BETA_TWO * second + (1.0 - BETA_TWO) * grad * grad
    corrected = first_new * (1.0 / (1.0 - BETA_ONE**STEP))
    scaled = jnp.sqrt(second_new * (1.0 / (1.0 - BETA_TWO**STEP))) + EPSILON
    return (param - rate * (corrected / scaled + decay * param), first_new, second_new)


class Sizes:
    def __init__(self, mesh, frames_shape, weights_shape):
        self.dp = mesh.shape["dp"]
        self.tensor = mesh.shape["tensor"]
        self.items, self.height, self.width, self.out = frames_shape
        self.chan = self.out * self.tensor
        self.rows = weights_shape[1]
        self.own_in = self.rows // TAPS
        self.cols = TAPS * self.out
        self.major = self.dp // 2
        self.pairs = self.tensor // 2
        self.slots = self.dp // self.tensor
        self.spots = self.height * self.width
        self.real = self.spots * self.items
        self.span = -(-self.real // 16) * 16
        self.halo = (self.width + 1) * self.items
        self.pieces = next(n for n in (5, 4, 3, 2, 1) if self.span // 16 % n == 0)
        self.piece = self.span // self.pieces
        self.groups = ((0, self.pieces // 2), (self.pieces // 2, self.pieces))
        self.wire = BF16 if self.own_in % 16 == 0 else F32
        self.line = self.major == 4
        self.far_order = (2, 1, 3) if self.line else tuple(range(1, self.major))
        self.devices = self.dp * self.tensor
        self.grant = (44 if self.wire == BF16 else 54) * 1024 * 1024


def body(
    sz,
    frames_ref,
    mask_ref,
    weights_ref,
    biases_ref,
    cot_ref,
    act4_out,
    act5_out,
    igrad_out,
    grads_out,
    stats_out,
    w_in,
    stage,
    cot,
    biases,
    mask,
    keep,
    w_all,
    frames,
    acts,
    spread,
    edges,
    slope4,
    act5,
    shifted,
    deltas,
    part_send,
    part_recv,
    part_own,
    cross_send,
    cross_recv,
    igrad,
    kgrad,
    near_send,
    near_recv,
    far_send,
    far_recv,
    shard,
    bias_sum,
    stats_all,
    local_sem,
    ready,
    wz_send,
    wz_recv,
    wf_send,
    wy_send,
    wy_recv,
    ax_send,
    ax_recv,
    as_send,
    as_recv,
    af_send,
    af_recv,
    rs_send,
    rs_recv,
    rx_send,
    rx_recv,
    gy_send,
    gy_recv,
    gz_send,
    gz_recv,
    st_send,
    st_recv,
):
    d = lax.axis_index("dp")
    t = lax.axis_index("tensor")
    major, minor = lax.div(d, 2), lax.rem(d, 2)
    near = (2 * major + 1 - minor, t)
    pair, side = lax.div(t, 2), lax.rem(t, 2)
    sibling = (d, 2 * pair + 1 - side)

    def far_slot(k):
        return 2 * flip_bits(major, k) + minor

    def near_slot(k):
        return 2 * flip_bits(major, k) + 1 - minor

    def far(k):
        return (far_slot(k), t)

    def cross_rank(k):
        return 2 * lax.rem(pair + k, sz.pairs) + side

    def cross_from(k):
        return 2 * lax.rem(pair + sz.pairs - k, sz.pairs) + side

    def remote(src, dst, send, recv, device):
        return pltpu.make_async_remote_copy(
            src_ref=src, dst_ref=dst, send_sem=send, recv_sem=recv, device_id=device, device_id_type=MESH
        )

    def same(block, send, recv, device):
        return remote(block, block, send, recv, device)

    all_pieces = range(sz.pieces)

    def rows_of(p):
        return pl.ds(pl.multiple_of(p * sz.piece, 16), sz.piece)

    far_steps = range(1, sz.major)
    cross_steps = range(1, sz.pairs)
    middle = jnp.logical_and(major > 0, major < sz.major - 1)
    far_steps = range(1, sz.major)
    cross_steps = range(1, sz.pairs)
    signal = functools.partial(pl.semaphore_signal, inc=1, device_id_type=MESH)

    barrier = pltpu.get_barrier_semaphore()
    if sz.line:
        pl.when(major > 0)(lambda: signal(barrier, device_id=(d - 2, t)))
        pl.when(major < sz.major - 1)(lambda: signal(barrier, device_id=(d + 2, t)))
        joined = jnp.where(middle, 2, 1) + 1 + sz.pairs
    else:
        for k in far_steps:
            signal(barrier, device_id=far(k))
        joined = sz.major + sz.pairs
    signal(barrier, device_id=near)
    for k in cross_steps:
        signal(barrier, device_id=(d, cross_rank(k)))
    signal(barrier, device_id=sibling)

    load_w = [pltpu.make_async_copy(weights_ref.at[l], w_in.at[l], local_sem.at[l]) for l in (0, 1)]
    load_frames = pltpu.make_async_copy(frames_ref, stage.at[0], local_sem.at[2])
    load_cot = pltpu.make_async_copy(cot_ref, stage.at[1], local_sem.at[3])
    load_biases = pltpu.make_async_copy(biases_ref, biases, local_sem.at[4])
    load_mask = pltpu.make_async_copy(mask_ref, mask, local_sem.at[5])
    for copy in (load_w[0], load_frames, load_w[1], load_cot, load_biases, load_mask):
        copy.start()

    def weight_out(l, k):
        return same(w_all.at[l, d], wz_send.at[l, k], wz_recv.at[l, k], far(k))

    def weight_relay(l):
        return same(w_all.at[l, far_slot(2)], wf_send.at[l], wz_recv.at[l, 3], far(1))

    def weight_over(l, k):
        return same(w_all.at[l, far_slot(k)], wy_send.at[l, k], wy_recv.at[l, k], near)

    def weights_out(l):
        for k in sz.far_order:
            if sz.line and k == 3:
                pl.when(middle)(weight_out(l, k).start)
            else:
                weight_out(l, k).start()

    def weights_on(l, steps):
        for k in steps:
            same(w_all.at[l, far_slot(k)], wz_send.at[l, k], wz_recv.at[l, k], far(k)).wait_recv()
            if sz.line and k == 2:
                pl.when(middle)(weight_relay(l).start)
            weight_over(l, k).start()

    def weights_here(l):
        for k in range(sz.major):
            same(w_all.at[l, near_slot(k)], wy_send.at[l, k], wy_recv.at[l, k], near).wait_recv()

    def weights_sent(l):
        for k in range(sz.major):
            weight_over(l, k).wait_send()
            if sz.line and k == 3:

                @pl.when(middle)
                def _():
                    weight_out(l, k).wait_send()
                    weight_relay(l).wait_send()

            elif k:
                weight_out(l, k).wait_send()

    def round_weights(l):
        load_w[l].wait()
        for tap in range(TAPS):
            w_all[l, d, :, tap * sz.out : (tap + 1) * sz.out] = w_in[
                l, pl.ds(tap, sz.own_in, stride=TAPS), :
            ].astype(sz.wire)

    def gather_sends(g, maps, p, rows):
        own = maps.at[t, rows]
        out = [same(own, ax_send.at[g, p, k], ax_recv.at[g, p, k], (d, cross_rank(k))) for k in cross_steps]
        out.append(same(own, as_send.at[g, p], as_recv.at[g, p], sibling))
        return out

    def gather_forward(g, maps, p, rows, k):
        return same(maps.at[cross_from(k), rows], af_send.at[g, p, k], af_recv.at[g, p, k], sibling)

    def gather_pass_on(g, maps, p, rows):
        for k in cross_steps:
            same(maps.at[cross_from(k), rows], ax_send.at[g, p, k], ax_recv.at[g, p, k], sibling).wait_recv()
            gather_forward(g, maps, p, rows, k).start()

    def gather_here(g, maps, p, rows):
        same(maps.at[sibling[1], rows], as_send.at[g, p], as_recv.at[g, p], sibling).wait_recv()
        for k in cross_steps:
            rank = 2 * lax.rem(pair + sz.pairs - k, sz.pairs) + 1 - side
            same(maps.at[rank, rows], af_send.at[g, p, k], af_recv.at[g, p, k], sibling).wait_recv()

    def gather_sent(g, maps, p, rows):
        for copy in gather_sends(g, maps, p, rows):
            copy.wait_send()
        for k in cross_steps:
            gather_forward(g, maps, p, rows, k).wait_send()

    whole = pl.ds(0, sz.span)

    def product(l, maps, group):
        rows = slice(group[0] * sz.piece, group[1] * sz.piece)
        left = jnp.concatenate([maps[q, rows] for q in range(sz.tensor)], axis=1)
        for start in range(0, sz.cols, WIDE):
            stop = min(start + WIDE, sz.cols)
            right = w_all[l, :, :, start:stop].reshape(sz.chan, stop - start).astype(BF16)
            spread[sz.halo + rows.start : sz.halo + rows.stop, start:stop] = jnp.dot(
                left, right, preferred_element_type=F32
            )

    def own_bias(l):
        return biases[l : l + 1, pl.ds(pl.multiple_of(t * sz.out, sz.out), sz.out)]

    def shifted_sum(p):
        sums = []
        for b in range(3):
            total = None
            for a in range(3):
                shift = sz.items * (sz.width * (a - 1) + b - 1)
                tap = 3 * a + b
                rows = pl.ds(pl.multiple_of(p * sz.piece + sz.halo + shift, 8), sz.piece)
                term = spread[rows, tap * sz.out : (tap + 1) * sz.out]
                total = term if total is None else total + term
            sums.append(total)
        return sums[1] + sums[0] * edges[0, rows_of(p)] + sums[2] * edges[1, rows_of(p)]

    def note_delta(l, p, delta):
        bias_sum[l] += jnp.sum(delta.reshape(sz.piece // 8, 8, sz.out), axis=0)
        rows = pl.ds(pl.multiple_of(p * sz.piece + sz.halo, 8), sz.piece)
        shifted[0, rows] = delta * edges[0, rows_of(p)]
        shifted[1, rows] = delta
        shifted[2, rows] = delta * edges[1, rows_of(p)]

    def spread_delta():
        @pl.loop(0, sz.pieces)
        def _(p):
            for a in range(3):
                for b in range(3):
                    shift = sz.items * (sz.width * (a - 1) + b - 1)
                    tap = 3 * a + b
                    rows = pl.ds(pl.multiple_of(p * sz.piece + sz.halo - shift, 8), sz.piece)
                    deltas[rows_of(p), tap * sz.out : (tap + 1) * sz.out] = shifted[b, rows].astype(BF16)

    def finish_four(first, last):
        @pl.loop(first, last)
        def _(p):
            act, slope = gelu_parts(shifted_sum(p) + own_bias(0))
            acts[t, rows_of(p)] = (act * edges[2, rows_of(p)]).astype(BF16)
            slope4[rows_of(p)] = slope * edges[2, rows_of(p)]
            for copy in gather_sends(1, acts, p, rows_of(p)):
                copy.start()

    def by_item(value):
        return (value.reshape(sz.piece // sz.items, sz.items, sz.out) * keep[...]).reshape(sz.piece, sz.out)

    def finish_five(first, last):
        @pl.loop(first, last)
        def _(p):
            act, slope = gelu_parts(shifted_sum(p) + own_bias(1))
            act5[rows_of(p)] = by_item(act).astype(BF16)
            delta = (by_item(cot[rows_of(p)].astype(F32)) * slope).astype(BF16).astype(F32)
            note_delta(1, p, delta)

    def part_copy(l, p):
        rows = rows_of(p)
        return remote(
            part_send.at[l, :, rows], part_recv.at[l, :, rows], rs_send.at[l, p], rs_recv.at[l, p], sibling
        )

    def cross_copy(l, p, k):
        rows = rows_of(p)
        return remote(
            cross_send.at[l, k, rows],
            cross_recv.at[l, k, rows],
            rx_send.at[l, p, k],
            rx_recv.at[l, p, k],
            (d, cross_rank(k)),
        )

    def back_product(l, group, which):
        blocks = [
            w_all[l, pl.ds((2 * j + which) * sz.slots, sz.slots)].reshape(sz.out, sz.cols) for j in range(sz.pairs)
        ]
        right = jnp.concatenate(blocks, axis=0).astype(BF16)
        left = deltas[group[0] * sz.piece : group[1] * sz.piece]
        out = lax.dot_general(left, right, (((1,), (1,)), ((), ())), preferred_element_type=F32)
        return [out[:, j * sz.out : (j + 1) * sz.out] for j in range(sz.pairs)]

    def back_to_sibling(l, group):
        rows = slice(group[0] * sz.piece, group[1] * sz.piece)
        for j, block in enumerate(back_product(l, group, 1 - side)):
            part_send[l, j, rows] = block.astype(BF16)
        for p in range(*group):
            part_copy(l, p).start()

    def back_own(l, group):
        rows = slice(group[0] * sz.piece, group[1] * sz.piece)
        for j, block in enumerate(back_product(l, group, side)):
            part_own[j, rows] = block

    def back_across(l, group):
        @pl.loop(*group)
        def _(p):
            part_copy(l, p).wait_recv()
            for k in cross_steps:
                j = lax.rem(pair + k, sz.pairs)
                total = part_own[j, rows_of(p)] + part_recv[l, j, rows_of(p)].astype(F32)
                cross_send[l, k, rows_of(p)] = total.astype(BF16)
                cross_copy(l, p, k).start()

    def back_products(l):
        one, two = sz.groups
        back_to_sibling(l, one)
        back_own(l, one)
        back_to_sibling(l, two)
        back_across(l, one)
        back_own(l, two)
        back_across(l, two)

    def back_total(l, p):
        total = part_own[pair, rows_of(p)] + part_recv[l, pair, rows_of(p)].astype(F32)
        for k in cross_steps:
            cross_copy(l, p, k).wait_recv()
            total += cross_recv[l, k, rows_of(p)].astype(F32)
        return total

    def near_copy(l, k):
        return remote(near_send.at[l, k], near_recv.at[l, k], gy_send.at[l, k], gy_recv.at[l, k], near)

    def far_copy(l, k):
        return remote(far_send.at[l, k], far_recv.at[l, k], gz_send.at[l, k], gz_recv.at[l, k], far(k))

    half = sz.tensor // 2
    far_half = [k for k in far_steps if k >= sz.major // 2]
    near_half = [k for k in far_steps if k < sz.major // 2]

    def grads_half(l, maps, other):
        own = lax.div(major, sz.major // 2)
        first = (1 - own if other else own) * half
        left = jnp.concatenate([maps[first + q] for q in range(half)], axis=1)
        into = pl.ds(first * sz.slots, half * sz.slots)
        for start in range(0, sz.cols, WIDE):
            stop = min(start + WIDE, sz.cols)
            product = lax.dot_general(left, deltas[:, start:stop], (((0,), (0,)), ((), ())), preferred_element_type=F32)
            kgrad[l, into, :, start:stop] = product.reshape(half * sz.slots, sz.own_in, stop - start)
        for k in far_half if other else [*near_half, 0]:
            near_send[l, k] = kgrad[l, near_slot(k)].astype(sz.wire)
            near_copy(l, k).start()

    def grads_far(l, k):
        near_copy(l, k).wait_recv()
        far_send[l, k] = (kgrad[l, far_slot(k)] + near_recv[l, k].astype(F32)).astype(sz.wire)
        far_copy(l, k).start()

    def grads_done(l):
        near_copy(l, 0).wait_recv()
        for k in far_steps:
            far_copy(l, k).wait_recv()
        total = kgrad[l, d] + near_recv[l, 0].astype(F32)
        for k in far_steps:
            total += far_recv[l, k].astype(F32)
        shard[...] = total
        squares = jnp.sum((total * total).reshape(sz.own_in // 8, 8, sz.cols), axis=0)
        for tap in range(TAPS):
            grads_out[l, pl.ds(tap, sz.own_in, stride=TAPS), :] = shard[:, tap * sz.out : (tap + 1) * sz.out]
        return sum(squares[:, tap * sz.out : (tap + 1) * sz.out] for tap in range(TAPS))

    round_weights(0)
    pl.semaphore_wait(barrier, joined)
    if sz.line:

        @pl.when(middle)
        def _():
            signal(ready, device_id=(d - 2, t))
            signal(ready, device_id=(d + 2, t))

    weight_over(0, 0).start()
    tail = sz.span - 16
    frames[t, tail:] = jnp.zeros((16, sz.out), BF16)
    load_frames.wait()
    frames[t, 0 : sz.real] = stage[0]
    for copy in gather_sends(0, frames, 0, whole):
        copy.start()
    round_weights(1)
    weight_over(1, 0).start()
    if sz.line:
        pl.semaphore_wait(ready, 1)
    weights_out(0)

    rest = sz.halo + sz.span
    for first in (0, rest):
        spread[first : first + sz.halo, :] = jnp.zeros((sz.halo, sz.cols), F32)
        shifted[:, first : first + sz.halo, :] = jnp.zeros((3, sz.halo, sz.out), F32)
    edges[...] = jnp.ones_like(edges)
    nothing = jnp.zeros((sz.items, sz.out), F32)
    for i in range(sz.height):
        for e, j in ((0, 0), (1, sz.width - 1)):
            first = (i * sz.width + j) * sz.items
            edges[e, first : first + sz.items, :] = nothing
    edges[2, sz.real :, :] = jnp.zeros((sz.span - sz.real, sz.out), F32)
    bias_sum[...] = jnp.zeros_like(bias_sum)

    cot[tail:] = jnp.zeros((16, sz.out), BF16)
    load_cot.wait()
    cot[0 : sz.real] = stage[1]
    load_biases.wait()
    load_mask.wait()
    item = lax.broadcasted_iota(jnp.int32, (sz.items, sz.out), 0)
    kept = jnp.zeros((sz.items, sz.out), F32)
    for n in range(sz.items):
        kept = jnp.where(item == n, mask[n].astype(F32), kept)
    keep[...] = kept

    one, two = sz.groups
    weights_on(0, far_steps)
    weights_out(1)
    gather_pass_on(0, frames, 0, whole)
    gather_here(0, frames, 0, whole)
    weights_here(0)
    weights_on(1, far_steps[:1])
    product(0, frames, one)
    finish_four(0, one[1] - 1)
    weights_on(1, far_steps[1:2])
    product(0, frames, two)
    finish_four(one[1] - 1, sz.pieces)

    weights_on(1, far_steps[2:])
    act4_out[...] = acts[t, 0 : sz.real]
    for p in all_pieces:
        gather_pass_on(1, acts, p, rows_of(p))
    for p in all_pieces:
        gather_here(1, acts, p, rows_of(p))
    weights_here(1)
    product(1, acts, one)
    finish_five(0, one[1] - 1)
    product(1, acts, two)
    finish_five(one[1] - 1, sz.pieces)
    spread_delta()

    grads_half(1, acts, True)
    back_products(1)
    grads_half(1, acts, False)
    act5_out[...] = act5[0 : sz.real]
    for k in far_half:
        grads_far(1, k)

    @pl.loop(0, sz.pieces)
    def _(p):
        note_delta(0, p, (back_total(1, p) * slope4[rows_of(p)]).astype(BF16).astype(F32))

    spread_delta()
    grads_half(0, frames, True)
    for k in near_half:
        grads_far(1, k)
    grads_half(0, frames, False)
    back_products(0)
    for k in far_half:
        grads_far(0, k)
    squares = grads_done(1)
    for k in near_half:
        grads_far(0, k)

    @pl.loop(0, sz.pieces)
    def _(p):
        igrad[rows_of(p)] = back_total(0, p)

    igrad_out[...] = igrad[0 : sz.real]

    squares += grads_done(0)

    me = d * sz.tensor + t
    stats_all[me, 0:1, :] = jnp.sum(squares, axis=0, keepdims=True)
    for l in (0, 1):
        stats_all[me, l + 1 : l + 2, :] = jnp.sum(bias_sum[l], axis=0, keepdims=True)
    stats_all[me, 3:8, :] = jnp.zeros((5, sz.out), F32)

    def stats_copy(k, slot):
        other = lax.rem(me + k, sz.devices)
        device = (lax.div(other, sz.tensor), lax.rem(other, sz.tensor))
        return same(stats_all.at[slot], st_send.at[k], st_recv.at[k], device)

    @pl.loop(1, sz.devices)
    def _(k):
        stats_copy(k, me).start()

    @pl.loop(1, sz.devices)
    def _(k):
        stats_copy(k, lax.rem(me + sz.devices - k, sz.devices)).wait_recv()

    for q in range(sz.tensor):
        total = stats_all[q]
        for slot in range(q + sz.tensor, sz.devices, sz.tensor):
            total += stats_all[slot]
        stats_out[q] = total

    for l in (0, 1):
        weights_sent(l)
        for k in far_steps:
            far_copy(l, k).wait_send()
        for k in range(sz.major):
            near_copy(l, k).wait_send()

        @pl.loop(0, sz.pieces)
        def _(p):
            part_copy(l, p).wait_send()
            for k in cross_steps:
                cross_copy(l, p, k).wait_send()

    gather_sent(0, frames, 0, whole)

    @pl.loop(0, sz.pieces)
    def _(p):
        gather_sent(1, acts, p, rows_of(p))

    @pl.loop(1, sz.devices)
    def _(k):
        stats_copy(k, me).wait_send()


def train_step(sz, frames, item_mask, weights, biases, cotangent):
    sem = pltpu.SemaphoreType.DMA
    vmem = pltpu.VMEM
    maps = (sz.span, sz.out)
    block = (sz.own_in, sz.cols)
    shapes = [
        vmem((2, sz.rows, sz.out), F32),
        vmem((2, sz.real, sz.out), BF16),
        vmem(maps, BF16),
        vmem((2, sz.chan), F32),
        pltpu.SMEM((sz.items,), jnp.int32),
        vmem((sz.items, sz.out), F32),
        vmem((2, sz.dp, *block), sz.wire),
        vmem((sz.tensor, *maps), BF16),
        vmem((sz.tensor, *maps), BF16),
        vmem((sz.span + 2 * sz.halo, sz.cols), F32),
        vmem((3, *maps), F32),
        vmem(maps, F32),
        vmem(maps, BF16),
        vmem((3, sz.span + 2 * sz.halo, sz.out), F32),
        vmem((sz.span, sz.cols), BF16),
        vmem((2, sz.pairs, *maps), BF16),
        vmem((2, sz.pairs, *maps), BF16),
        vmem((sz.pairs, *maps), F32),
        vmem((2, sz.pairs, *maps), BF16),
        vmem((2, sz.pairs, *maps), BF16),
        vmem(maps, F32),
        vmem((2, sz.dp, *block), F32),
        vmem((2, sz.major, *block), sz.wire),
        vmem((2, sz.major, *block), sz.wire),
        vmem((2, sz.major, *block), sz.wire),
        vmem((2, sz.major, *block), sz.wire),
        vmem(block, F32),
        vmem((2, 8, sz.out), F32),
        vmem((sz.devices, 8, sz.out), F32),
        sem((6,)),
        pltpu.SemaphoreType.REGULAR,
        sem((2, sz.major)),
        sem((2, sz.major)),
        sem((2,)),
        sem((2, sz.major)),
        sem((2, sz.major)),
        sem((2, sz.pieces, sz.pairs)),
        sem((2, sz.pieces, sz.pairs)),
        sem((2, sz.pieces)),
        sem((2, sz.pieces)),
        sem((2, sz.pieces, sz.pairs)),
        sem((2, sz.pieces, sz.pairs)),
        sem((2, sz.pieces)),
        sem((2, sz.pieces)),
        sem((2, sz.pieces, sz.pairs)),
        sem((2, sz.pieces, sz.pairs)),
        sem((2, sz.major)),
        sem((2, sz.major)),
        sem((2, sz.major)),
        sem((2, sz.major)),
        sem((sz.devices,)),
        sem((sz.devices,)),
    ]
    macs = 6 * sz.real * TAPS * sz.chan * sz.out
    rows = (sz.real, sz.out)
    return pl.pallas_call(
        functools.partial(body, sz),
        out_shape=[
            vmem(rows, BF16),
            vmem(rows, BF16),
            vmem(rows, F32),
            vmem((2, sz.rows, sz.out), F32),
            vmem((sz.tensor, 8, sz.out), F32),
        ],
        in_specs=[pl.BlockSpec(memory_space=pltpu.HBM)] * 5,
        out_specs=[pl.BlockSpec(memory_space=vmem)] * 5,
        scratch_shapes=shapes,
        compiler_params=pltpu.CompilerParams(
            collective_id=0, has_side_effects=True, vmem_limit_bytes=sz.grant
        ),
        cost_estimate=pl.CostEstimate(flops=2 * macs, bytes_accessed=6_000_000, transcendentals=0),
        name="train_step",
    )(*(pltpu.with_memory_space_constraint(x, pltpu.HBM) for x in (frames, item_mask, weights, biases, cotangent)))


def finish_body(
    sz,
    act4,
    act5,
    igrad,
    grads,
    stats,
    weights,
    first,
    second,
    biases_ref,
    bias_first_ref,
    bias_second_ref,
    act4_out,
    act5_out,
    igrad_out,
    norm_out,
    weights_out,
    first_out,
    second_out,
    biases_out,
    bias_first_out,
    bias_second_out,
    olds,
    news,
    in_sem,
    out_sem,
    move_sem,
):
    targets = (weights_out, first_out, second_out)
    stores = [
        [pltpu.make_async_copy(news.at[l, i], ref.at[l], out_sem.at[l, i]) for i, ref in enumerate(targets)]
        for l in (0, 1)
    ]
    moves = [
        pltpu.make_async_copy(held, ref, move_sem.at[i])
        for i, (held, ref) in enumerate(((act4, act4_out), (act5, act5_out), (igrad, igrad_out)))
    ]
    loads = [
        pltpu.make_async_copy(ref, olds.at[i], in_sem.at[i])
        for i, ref in enumerate((biases_ref, bias_first_ref, bias_second_ref))
    ]
    for copy in (*loads, *moves):
        copy.start()
    bias_grad = jnp.concatenate([stats[q, 1:3, :] for q in range(sz.tensor)], axis=1)
    squares = jnp.sum(stats[:, 0, :], axis=(0, 1), keepdims=True) + jnp.sum(
        bias_grad * bias_grad, axis=(0, 1), keepdims=True
    )
    grad_norm = jnp.sqrt(squares)
    factor = jnp.minimum(1.0, CLIP_NORM / (grad_norm + 1e-06))
    norm_out[...] = grad_norm
    for l in (0, 1):
        news[l, 0], news[l, 1], news[l, 2] = adam_update(
            weights[l], grads[l] * factor, first[l], second[l], RATE, DECAY
        )
        for copy in stores[l]:
            copy.start()
    for copy in loads:
        copy.wait()
    biases_out[...], bias_first_out[...], bias_second_out[...] = adam_update(
        olds[0], bias_grad * factor, olds[1], olds[2], BIAS_RATE, 0.0
    )
    for copy in (*moves, *stores[0], *stores[1]):
        copy.wait()


def finish(sz, act4, act5, igrad, grads, stats, weights, first, second, biases, bias_first, bias_second):
    inside = pl.BlockSpec(memory_space=pltpu.VMEM)
    outside = pl.BlockSpec(memory_space=pltpu.HBM)
    like = lambda x: jax.ShapeDtypeStruct(x.shape, x.dtype)
    sem = pltpu.SemaphoreType.DMA
    held = [pltpu.with_memory_space_constraint(x, pltpu.VMEM) for x in (act4, act5, igrad, grads, stats, weights, first, second)]
    given = [pltpu.with_memory_space_constraint(x, pltpu.HBM) for x in (biases, bias_first, bias_second)]
    return pl.pallas_call(
        functools.partial(finish_body, sz),
        out_shape=[
            like(act4),
            like(act5),
            like(igrad),
            jax.ShapeDtypeStruct((1, 1), F32),
            like(weights),
            like(first),
            like(second),
            like(biases),
            like(bias_first),
            like(bias_second),
        ],
        in_specs=[inside] * 8 + [outside] * 3,
        out_specs=[outside] * 3 + [inside] + [outside] * 3 + [inside] * 3,
        scratch_shapes=[
            pltpu.VMEM((3, *biases.shape), F32),
            pltpu.VMEM((2, 3, sz.rows, sz.out), F32),
            sem((3,)),
            sem((2, 3)),
            sem((3,)),
        ],
        compiler_params=pltpu.CompilerParams(vmem_limit_bytes=8 * 1024 * 1024),
        cost_estimate=pl.CostEstimate(flops=5_000_000, bytes_accessed=7_000_000, transcendentals=0),
        name="clip_and_adamw",
    )(*held, *given)


def on_device(
    mesh,
    frames,
    item_mask,
    weights,
    biases,
    cotangent,
    weight_first,
    weight_second,
    bias_first,
    bias_second,
):
    sz = Sizes(mesh, frames.shape, weights.shape)

    def flat(maps):
        return jnp.transpose(maps, (1, 2, 0, 3)).reshape(sz.real, sz.out)

    def square(rows):
        return jnp.transpose(rows.reshape(sz.height, sz.width, sz.items, sz.out), (2, 0, 1, 3))

    made = train_step(sz, flat(frames), item_mask, weights, biases, flat(cotangent))
    act_four, act_five, input_grad, grad_norm, *rest = finish(
        sz, *made, weights, weight_first, weight_second, biases, bias_first, bias_second
    )
    return (square(act_four), square(act_five), square(input_grad), grad_norm.reshape(()), *rest)


def solution(mesh):
    split = P("dp", None, None, "tensor")
    rows = P(None, "dp", "tensor")
    in_specs = (split, P("dp"), rows, P(), split, rows, rows, P(), P())
    out_specs = (split, split, split, P(), rows, rows, rows, P(), P(), P())
    return jax.shard_map(
        functools.partial(on_device, mesh), mesh=mesh, in_specs=in_specs, out_specs=out_specs, check_vma=False
    )
```

```python
import functools
import math

import jax
import jax.numpy as jnp
from jax import lax
from jax.experimental import pallas as pl
from jax.experimental.pallas import tpu as pltpu
from jax.sharding import PartitionSpec as P

STEP = 5
CLIP_NORM = 1.0
BETA_ONE = 0.5
BETA_TWO = 0.5
RATE = 0.01
BIAS_RATE = 0.03
DECAY = 0.1
EPSILON = 1e-08

MESH = pl.DeviceIdType.MESH
BF16 = jnp.bfloat16
F32 = jnp.float32
ROOT = math.sqrt(2.0 / math.pi)
CUBE = 0.044715
TAPS = 9
WIDE = 256


def gelu_parts(value):
    square = value * value
    th = jnp.tanh(ROOT * value * (1.0 + CUBE * square))
    half = 0.5 * (1.0 + th)
    slope = half + 0.5 * value * (1.0 - th * th) * (ROOT * (1.0 + 3.0 * CUBE * square))
    return value * half, slope


def flip_bits(index, mask):
    bit = 1
    while bit <= mask:
        if mask & bit:
            index = index + bit - 2 * bit * lax.rem(lax.div(index, bit), 2)
        bit *= 2
    return index


def adam_update(param, grad, first, second, rate, decay):
    first_new = BETA_ONE * first + (1.0 - BETA_ONE) * grad
    second_new = BETA_TWO * second + (1.0 - BETA_TWO) * grad * grad
    corrected = first_new * (1.0 / (1.0 - BETA_ONE**STEP))
    scaled = jnp.sqrt(second_new * (1.0 / (1.0 - BETA_TWO**STEP))) + EPSILON
    return (param - rate * (corrected / scaled + decay * param), first_new, second_new)


class Sizes:
    def __init__(self, mesh, frames_shape, weights_shape):
        self.dp = mesh.shape["dp"]
        self.tensor = mesh.shape["tensor"]
        self.items, self.height, self.width, self.out = frames_shape
        self.chan = self.out * self.tensor
        self.rows = weights_shape[1]
        self.own_in = self.rows // TAPS
        self.cols = TAPS * self.out
        self.major = self.dp // 2
        self.pairs = self.tensor // 2
        self.slots = self.dp // self.tensor
        self.spots = self.height * self.width
        self.real = self.spots * self.items
        self.span = -(-self.real // 16) * 16
        self.halo = (self.width + 1) * self.items
        self.pieces = next(n for n in (5, 4, 3, 2, 1) if self.span // 16 % n == 0)
        self.piece = self.span // self.pieces
        self.groups = ((0, self.pieces // 2), (self.pieces // 2, self.pieces))
        self.wire = BF16 if self.own_in % 16 == 0 else F32
        self.line = self.major == 4
        self.far_order = (2, 1, 3) if self.line else tuple(range(1, self.major))
        self.devices = self.dp * self.tensor
        self.shares = 2 if self.own_in % 32 == 0 else 1
        self.share = self.own_in // self.shares
        self.grant = (44 if self.wire == BF16 else 54) * 1024 * 1024


def body(
    sz,
    frames_ref,
    mask_ref,
    weights_ref,
    biases_ref,
    cot_ref,
    act4_out,
    act5_out,
    igrad_out,
    grads_out,
    stats_out,
    w_in,
    stage,
    cot,
    biases,
    mask,
    keep,
    w_all,
    frames,
    acts,
    spread,
    edges,
    slope4,
    act5,
    shifted,
    deltas,
    part_send,
    part_recv,
    part_own,
    cross_send,
    cross_recv,
    igrad,
    kgrad,
    near_send,
    near_recv,
    far_send,
    far_recv,
    relay_recv,
    shard,
    bias_sum,
    stats_all,
    local_sem,
    ready,
    wz_send,
    wz_recv,
    wf_send,
    wy_send,
    wy_recv,
    ax_send,
    ax_recv,
    as_send,
    as_recv,
    af_send,
    af_recv,
    rs_send,
    rs_recv,
    rx_send,
    rx_recv,
    gy_send,
    gy_recv,
    gz_send,
    gz_recv,
    gr_recv,
    st_send,
    st_recv,
):
    d = lax.axis_index("dp")
    t = lax.axis_index("tensor")
    major, minor = lax.div(d, 2), lax.rem(d, 2)
    near = (2 * major + 1 - minor, t)
    pair, side = lax.div(t, 2), lax.rem(t, 2)
    sibling = (d, 2 * pair + 1 - side)

    def far_slot(k):
        return 2 * flip_bits(major, k) + minor

    def near_slot(k):
        return 2 * flip_bits(major, k) + 1 - minor

    def far(k):
        return (far_slot(k), t)

    def cross_rank(k):
        return 2 * lax.rem(pair + k, sz.pairs) + side

    def cross_from(k):
        return 2 * lax.rem(pair + sz.pairs - k, sz.pairs) + side

    def remote(src, dst, send, recv, device):
        return pltpu.make_async_remote_copy(
            src_ref=src, dst_ref=dst, send_sem=send, recv_sem=recv, device_id=device, device_id_type=MESH
        )

    def same(block, send, recv, device):
        return remote(block, block, send, recv, device)

    all_pieces = range(sz.pieces)

    def rows_of(p):
        return pl.ds(pl.multiple_of(p * sz.piece, 16), sz.piece)

    far_steps = range(1, sz.major)
    cross_steps = range(1, sz.pairs)
    middle = jnp.logical_and(major > 0, major < sz.major - 1)
    far_steps = range(1, sz.major)
    cross_steps = range(1, sz.pairs)
    signal = functools.partial(pl.semaphore_signal, inc=1, device_id_type=MESH)

    barrier = pltpu.get_barrier_semaphore()
    if sz.line:
        pl.when(major > 0)(lambda: signal(barrier, device_id=(d - 2, t)))
        pl.when(major < sz.major - 1)(lambda: signal(barrier, device_id=(d + 2, t)))
        joined = jnp.where(middle, 2, 1) + 1 + sz.pairs
    else:
        for k in far_steps:
            signal(barrier, device_id=far(k))
        joined = sz.major + sz.pairs
    signal(barrier, device_id=near)
    for k in cross_steps:
        signal(barrier, device_id=(d, cross_rank(k)))
    signal(barrier, device_id=sibling)

    load_w = [pltpu.make_async_copy(weights_ref.at[l], w_in.at[l], local_sem.at[l]) for l in (0, 1)]
    load_frames = pltpu.make_async_copy(frames_ref, stage.at[0], local_sem.at[2])
    load_cot = pltpu.make_async_copy(cot_ref, stage.at[1], local_sem.at[3])
    load_biases = pltpu.make_async_copy(biases_ref, biases, local_sem.at[4])
    load_mask = pltpu.make_async_copy(mask_ref, mask, local_sem.at[5])
    for copy in (load_w[0], load_frames, load_w[1], load_cot, load_biases, load_mask):
        copy.start()

    def weight_out(l, k):
        return same(w_all.at[l, d], wz_send.at[l, k], wz_recv.at[l, k], far(k))

    def weight_relay(l):
        return same(w_all.at[l, far_slot(2)], wf_send.at[l], wz_recv.at[l, 3], far(1))

    def weight_over(l, k):
        return same(w_all.at[l, far_slot(k)], wy_send.at[l, k], wy_recv.at[l, k], near)

    def weights_out(l):
        for k in sz.far_order:
            if sz.line and k == 3:
                pl.when(middle)(weight_out(l, k).start)
            else:
                weight_out(l, k).start()

    def weights_on(l, steps):
        for k in steps:
            same(w_all.at[l, far_slot(k)], wz_send.at[l, k], wz_recv.at[l, k], far(k)).wait_recv()
            if sz.line and k == 2:
                pl.when(middle)(weight_relay(l).start)
            weight_over(l, k).start()

    def weights_here(l):
        for k in range(sz.major):
            same(w_all.at[l, near_slot(k)], wy_send.at[l, k], wy_recv.at[l, k], near).wait_recv()

    def weights_sent(l):
        for k in range(sz.major):
            weight_over(l, k).wait_send()
            if sz.line and k == 3:

                @pl.when(middle)
                def _():
                    weight_out(l, k).wait_send()
                    weight_relay(l).wait_send()

            elif k:
                weight_out(l, k).wait_send()

    def round_weights(l):
        load_w[l].wait()
        for tap in range(TAPS):
            w_all[l, d, :, tap * sz.out : (tap + 1) * sz.out] = w_in[
                l, pl.ds(tap, sz.own_in, stride=TAPS), :
            ].astype(sz.wire)

    def gather_sends(g, maps, p, rows):
        own = maps.at[t, rows]
        out = [same(own, ax_send.at[g, p, k], ax_recv.at[g, p, k], (d, cross_rank(k))) for k in cross_steps]
        out.append(same(own, as_send.at[g, p], as_recv.at[g, p], sibling))
        return out

    def gather_forward(g, maps, p, rows, k):
        return same(maps.at[cross_from(k), rows], af_send.at[g, p, k], af_recv.at[g, p, k], sibling)

    def gather_pass_on(g, maps, p, rows):
        for k in cross_steps:
            same(maps.at[cross_from(k), rows], ax_send.at[g, p, k], ax_recv.at[g, p, k], sibling).wait_recv()
            gather_forward(g, maps, p, rows, k).start()

    def gather_here(g, maps, p, rows):
        same(maps.at[sibling[1], rows], as_send.at[g, p], as_recv.at[g, p], sibling).wait_recv()
        for k in cross_steps:
            rank = 2 * lax.rem(pair + sz.pairs - k, sz.pairs) + 1 - side
            same(maps.at[rank, rows], af_send.at[g, p, k], af_recv.at[g, p, k], sibling).wait_recv()

    def gather_sent(g, maps, p, rows):
        for copy in gather_sends(g, maps, p, rows):
            copy.wait_send()
        for k in cross_steps:
            gather_forward(g, maps, p, rows, k).wait_send()

    whole = pl.ds(0, sz.span)

    def product(l, maps, group):
        rows = slice(group[0] * sz.piece, group[1] * sz.piece)
        left = jnp.concatenate([maps[q, rows] for q in range(sz.tensor)], axis=1)
        for start in range(0, sz.cols, WIDE):
            stop = min(start + WIDE, sz.cols)
            right = w_all[l, :, :, start:stop].reshape(sz.chan, stop - start).astype(BF16)
            spread[sz.halo + rows.start : sz.halo + rows.stop, start:stop] = jnp.dot(
                left, right, preferred_element_type=F32
            )

    def own_bias(l):
        return biases[l : l + 1, pl.ds(pl.multiple_of(t * sz.out, sz.out), sz.out)]

    def shifted_sum(p):
        sums = []
        for b in range(3):
            total = None
            for a in range(3):
                shift = sz.items * (sz.width * (a - 1) + b - 1)
                tap = 3 * a + b
                rows = pl.ds(pl.multiple_of(p * sz.piece + sz.halo + shift, 8), sz.piece)
                term = spread[rows, tap * sz.out : (tap + 1) * sz.out]
                total = term if total is None else total + term
            sums.append(total)
        return sums[1] + sums[0] * edges[0, rows_of(p)] + sums[2] * edges[1, rows_of(p)]

    def note_delta(l, p, delta):
        bias_sum[l] += jnp.sum(delta.reshape(sz.piece // 8, 8, sz.out), axis=0)
        rows = pl.ds(pl.multiple_of(p * sz.piece + sz.halo, 8), sz.piece)
        shifted[0, rows] = delta * edges[0, rows_of(p)]
        shifted[1, rows] = delta
        shifted[2, rows] = delta * edges[1, rows_of(p)]

    def spread_delta():
        @pl.loop(0, sz.pieces)
        def _(p):
            for a in range(3):
                for b in range(3):
                    shift = sz.items * (sz.width * (a - 1) + b - 1)
                    tap = 3 * a + b
                    rows = pl.ds(pl.multiple_of(p * sz.piece + sz.halo - shift, 8), sz.piece)
                    deltas[rows_of(p), tap * sz.out : (tap + 1) * sz.out] = shifted[b, rows].astype(BF16)

    def finish_four(first, last):
        @pl.loop(first, last)
        def _(p):
            act, slope = gelu_parts(shifted_sum(p) + own_bias(0))
            acts[t, rows_of(p)] = (act * edges[2, rows_of(p)]).astype(BF16)
            slope4[rows_of(p)] = slope * edges[2, rows_of(p)]
            for copy in gather_sends(1, acts, p, rows_of(p)):
                copy.start()

    def by_item(value):
        return (value.reshape(sz.piece // sz.items, sz.items, sz.out) * keep[...]).reshape(sz.piece, sz.out)

    def finish_five(first, last):
        @pl.loop(first, last)
        def _(p):
            act, slope = gelu_parts(shifted_sum(p) + own_bias(1))
            act5[rows_of(p)] = by_item(act).astype(BF16)
            delta = (by_item(cot[rows_of(p)].astype(F32)) * slope).astype(BF16).astype(F32)
            note_delta(1, p, delta)

    def part_copy(l, p):
        rows = rows_of(p)
        return remote(
            part_send.at[l, :, rows], part_recv.at[l, :, rows], rs_send.at[l, p], rs_recv.at[l, p], sibling
        )

    def cross_copy(l, p, k):
        rows = rows_of(p)
        return remote(
            cross_send.at[l, k, rows],
            cross_recv.at[l, k, rows],
            rx_send.at[l, p, k],
            rx_recv.at[l, p, k],
            (d, cross_rank(k)),
        )

    def back_product(l, group, which):
        blocks = [
            w_all[l, pl.ds((2 * j + which) * sz.slots, sz.slots)].reshape(sz.out, sz.cols) for j in range(sz.pairs)
        ]
        right = jnp.concatenate(blocks, axis=0).astype(BF16)
        left = deltas[group[0] * sz.piece : group[1] * sz.piece]
        out = lax.dot_general(left, right, (((1,), (1,)), ((), ())), preferred_element_type=F32)
        return [out[:, j * sz.out : (j + 1) * sz.out] for j in range(sz.pairs)]

    def back_to_sibling(l, group):
        rows = slice(group[0] * sz.piece, group[1] * sz.piece)
        for j, block in enumerate(back_product(l, group, 1 - side)):
            part_send[l, j, rows] = block.astype(BF16)
        for p in range(*group):
            part_copy(l, p).start()

    def back_own(l, group):
        rows = slice(group[0] * sz.piece, group[1] * sz.piece)
        for j, block in enumerate(back_product(l, group, side)):
            part_own[j, rows] = block

    def back_across(l, group):
        @pl.loop(*group)
        def _(p):
            part_copy(l, p).wait_recv()
            for k in cross_steps:
                j = lax.rem(pair + k, sz.pairs)
                total = part_own[j, rows_of(p)] + part_recv[l, j, rows_of(p)].astype(F32)
                cross_send[l, k, rows_of(p)] = total.astype(BF16)
                cross_copy(l, p, k).start()

    def back_products(l, between=None):
        one, two = sz.groups
        back_to_sibling(l, one)
        back_own(l, one)
        back_to_sibling(l, two)
        back_across(l, one)
        if between:
            between()
        back_own(l, two)
        back_across(l, two)

    def back_total(l, p):
        total = part_own[pair, rows_of(p)] + part_recv[l, pair, rows_of(p)].astype(F32)
        for k in cross_steps:
            cross_copy(l, p, k).wait_recv()
            total += cross_recv[l, k, rows_of(p)].astype(F32)
        return total

    shares = range(sz.shares)

    def share_of(h):
        return slice(h * sz.share, (h + 1) * sz.share)

    def near_copy(l, k, h):
        return remote(
            near_send.at[l, k, share_of(h)],
            near_recv.at[l, k, share_of(h)],
            gy_send.at[l, k, h],
            gy_recv.at[l, k, h],
            near,
        )

    def far_copy(l, k, h):
        return remote(
            far_send.at[l, k, share_of(h)],
            far_recv.at[l, k, share_of(h)],
            gz_send.at[l, k, h],
            gz_recv.at[l, k, h],
            far(k),
        )

    half = sz.tensor // 2
    far_half = [k for k in reversed(far_steps) if k >= sz.major // 2]
    near_half = [k for k in far_steps if k < sz.major // 2]

    def grads_block(l, maps, block, width, steps):
        left = jnp.concatenate([maps[block + q] for q in range(width)], axis=1)
        into = pl.ds(block * sz.slots, width * sz.slots)
        for start in range(0, sz.cols, WIDE):
            stop = min(start + WIDE, sz.cols)
            product = lax.dot_general(
                left, deltas[:, start:stop], (((0,), (0,)), ((), ())), preferred_element_type=F32
            )
            kgrad[l, into, :, start:stop] = product.reshape(width * sz.slots, sz.own_in, stop - start)
        for k in steps:
            near_send[l, k] = kgrad[l, near_slot(k)].astype(sz.wire)
            for h in shares:
                near_copy(l, k, h).start()

    own_half = lax.div(major, sz.major // 2)

    def grads_half(l, maps, other):
        first = (1 - own_half if other else own_half) * half
        grads_block(l, maps, first, half, far_half if other else [*near_half, 0])

    def grads_place(l, maps, k):
        grads_block(l, maps, flip_bits(major, k), 1, [k])

    def relay_copy(l, h):
        rows = share_of(h)
        return remote(
            far_send.at[l, 3, rows], relay_recv.at[l, rows], gz_send.at[l, 3, h], gr_recv.at[l, h], far(1)
        )

    def grads_far(l, k):
        for h in shares:
            rows = share_of(h)
            near_copy(l, k, h).wait_recv()
            total = kgrad[l, far_slot(k), rows] + near_recv[l, k, rows].astype(F32)
            if sz.line and k == 2:

                @pl.when(middle)
                def _():
                    relay_copy(l, h).wait_recv()
                    far_send[l, k, rows] = (total + relay_recv[l, rows].astype(F32)).astype(sz.wire)

                @pl.when(jnp.logical_not(middle))
                def _():
                    far_send[l, k, rows] = total.astype(sz.wire)

            else:
                far_send[l, k, rows] = total.astype(sz.wire)
            if sz.line and k == 3:
                pl.when(middle)(far_copy(l, k, h).start)
                pl.when(jnp.logical_not(middle))(relay_copy(l, h).start)
            else:
                far_copy(l, k, h).start()

    def grads_sum(l):
        for h in shares:
            near_copy(l, 0, h).wait_recv()
            for k in far_steps:
                if sz.line and k == 3:
                    pl.when(middle)(far_copy(l, k, h).wait_recv)
                else:
                    far_copy(l, k, h).wait_recv()
        total = kgrad[l, d] + near_recv[l, 0].astype(F32)
        for k in far_steps:
            total += far_recv[l, k].astype(F32)
        shard[...] = total
        squares = jnp.sum((total * total).reshape(sz.own_in // 8, 8, sz.cols), axis=0)
        return sum(squares[:, tap * sz.out : (tap + 1) * sz.out] for tap in range(TAPS))

    def grads_out_rows(l):
        for tap in range(TAPS):
            grads_out[l, pl.ds(tap, sz.own_in, stride=TAPS), :] = shard[:, tap * sz.out : (tap + 1) * sz.out]

    round_weights(0)
    pl.semaphore_wait(barrier, joined)
    if sz.line:

        @pl.when(middle)
        def _():
            signal(ready, device_id=(d - 2, t))
            signal(ready, device_id=(d + 2, t))

    weight_over(0, 0).start()
    tail = sz.span - 16
    frames[t, tail:] = jnp.zeros((16, sz.out), BF16)
    load_frames.wait()
    frames[t, 0 : sz.real] = stage[0]
    for copy in gather_sends(0, frames, 0, whole):
        copy.start()
    round_weights(1)
    weight_over(1, 0).start()
    if sz.line:
        pl.semaphore_wait(ready, 1)
    weights_out(0)

    rest = sz.halo + sz.span
    for first in (0, rest):
        spread[first : first + sz.halo, :] = jnp.zeros((sz.halo, sz.cols), F32)
        shifted[:, first : first + sz.halo, :] = jnp.zeros((3, sz.halo, sz.out), F32)
    edges[...] = jnp.ones_like(edges)
    nothing = jnp.zeros((sz.items, sz.out), F32)
    for i in range(sz.height):
        for e, j in ((0, 0), (1, sz.width - 1)):
            first = (i * sz.width + j) * sz.items
            edges[e, first : first + sz.items, :] = nothing
    edges[2, sz.real :, :] = jnp.zeros((sz.span - sz.real, sz.out), F32)
    bias_sum[...] = jnp.zeros_like(bias_sum)
    if sz.line:

        @pl.when(jnp.logical_not(middle))
        def _():
            far_recv[:, 3] = jnp.zeros((2, sz.own_in, sz.cols), sz.wire)


    cot[tail:] = jnp.zeros((16, sz.out), BF16)
    load_cot.wait()
    cot[0 : sz.real] = stage[1]
    load_biases.wait()
    load_mask.wait()
    item = lax.broadcasted_iota(jnp.int32, (sz.items, sz.out), 0)
    kept = jnp.zeros((sz.items, sz.out), F32)
    for n in range(sz.items):
        kept = jnp.where(item == n, mask[n].astype(F32), kept)
    keep[...] = kept

    one, two = sz.groups
    weights_on(0, far_steps)
    weights_out(1)
    gather_pass_on(0, frames, 0, whole)
    gather_here(0, frames, 0, whole)
    weights_here(0)
    weights_on(1, far_steps[:1])
    product(0, frames, one)
    finish_four(0, one[1] - 1)
    weights_on(1, far_steps[1:2])
    product(0, frames, two)
    finish_four(one[1] - 1, sz.pieces)

    weights_on(1, far_steps[2:])
    act4_out[...] = acts[t, 0 : sz.real]
    for p in all_pieces:
        gather_pass_on(1, acts, p, rows_of(p))
    for p in all_pieces:
        gather_here(1, acts, p, rows_of(p))
    weights_here(1)
    product(1, acts, one)
    finish_five(0, one[1] - 1)
    product(1, acts, two)
    finish_five(one[1] - 1, sz.pieces)
    spread_delta()

    if sz.line and sz.tensor == sz.major:
        grads_place(1, acts, 3)
        back_products(1, lambda: grads_place(1, acts, 2))
    else:
        grads_half(1, acts, True)
        back_products(1)
    grads_half(1, acts, False)
    act5_out[...] = act5[0 : sz.real]
    grads_far(1, far_half[0])

    @pl.loop(0, sz.pieces)
    def _(p):
        note_delta(0, p, (back_total(1, p) * slope4[rows_of(p)]).astype(BF16).astype(F32))

    spread_delta()
    if sz.line and sz.tensor == sz.major:
        grads_place(0, frames, 3)
        grads_place(0, frames, 2)
    else:
        grads_half(0, frames, True)
    for k in far_half[1:]:
        grads_far(1, k)
    grads_half(0, frames, False)
    for k in near_half:
        grads_far(1, k)
    back_products(0, lambda: grads_far(0, far_half[0]))
    for k in (*far_half[1:], *near_half):
        grads_far(0, k)
    squares = grads_sum(1)
    grads_out_rows(1)

    @pl.loop(0, sz.pieces)
    def _(p):
        igrad[rows_of(p)] = back_total(0, p)

    igrad_out[...] = igrad[0 : sz.real]

    squares += grads_sum(0)

    me = d * sz.tensor + t
    stats_all[me, 0:1, :] = jnp.sum(squares, axis=0, keepdims=True)
    for l in (0, 1):
        stats_all[me, l + 1 : l + 2, :] = jnp.sum(bias_sum[l], axis=0, keepdims=True)

    def stats_copy(k, slot):
        other = lax.rem(me + k, sz.devices)
        device = (lax.div(other, sz.tensor), lax.rem(other, sz.tensor))
        return same(stats_all.at[slot, 0:3], st_send.at[k], st_recv.at[k], device)

    def each_device(act):
        if sz.devices <= 32:
            for k in range(1, sz.devices):
                act(k)
        else:
            pl.loop(1, sz.devices)(act)

    each_device(lambda k: stats_copy(k, me).start())

    grads_out_rows(0)
    for l in (0, 1):
        weights_sent(l)
        for h in shares:
            for k in far_steps:
                far_copy(l, k, h).wait_send()
            for k in range(sz.major):
                near_copy(l, k, h).wait_send()

        @pl.loop(0, sz.pieces)
        def _(p):
            part_copy(l, p).wait_send()
            for k in cross_steps:
                cross_copy(l, p, k).wait_send()

    gather_sent(0, frames, 0, whole)

    @pl.loop(0, sz.pieces)
    def _(p):
        gather_sent(1, acts, p, rows_of(p))

    each_device(lambda k: stats_copy(k, lax.rem(me + sz.devices - k, sz.devices)).wait_recv())

    for q in range(sz.tensor):
        total = stats_all[q, 0:3]
        for slot in range(q + sz.tensor, sz.devices, sz.tensor):
            total += stats_all[slot, 0:3]
        stats_out[q, 0:3] = total

    each_device(lambda k: stats_copy(k, me).wait_send())


def train_step(sz, frames, item_mask, weights, biases, cotangent):
    sem = pltpu.SemaphoreType.DMA
    vmem = pltpu.VMEM
    maps = (sz.span, sz.out)
    block = (sz.own_in, sz.cols)
    shapes = [
        vmem((2, sz.rows, sz.out), F32),
        vmem((2, sz.real, sz.out), BF16),
        vmem(maps, BF16),
        vmem((2, sz.chan), F32),
        pltpu.SMEM((sz.items,), jnp.int32),
        vmem((sz.items, sz.out), F32),
        vmem((2, sz.dp, *block), sz.wire),
        vmem((sz.tensor, *maps), BF16),
        vmem((sz.tensor, *maps), BF16),
        vmem((sz.span + 2 * sz.halo, sz.cols), F32),
        vmem((3, *maps), F32),
        vmem(maps, F32),
        vmem(maps, BF16),
        vmem((3, sz.span + 2 * sz.halo, sz.out), F32),
        vmem((sz.span, sz.cols), BF16),
        vmem((2, sz.pairs, *maps), BF16),
        vmem((2, sz.pairs, *maps), BF16),
        vmem((sz.pairs, *maps), F32),
        vmem((2, sz.pairs, *maps), BF16),
        vmem((2, sz.pairs, *maps), BF16),
        vmem(maps, F32),
        vmem((2, sz.dp, *block), F32),
        vmem((2, sz.major, *block), sz.wire),
        vmem((2, sz.major, *block), sz.wire),
        vmem((2, sz.major, *block), sz.wire),
        vmem((2, sz.major, *block), sz.wire),
        vmem((2, *block), sz.wire),
        vmem(block, F32),
        vmem((2, 8, sz.out), F32),
        vmem((sz.devices, 8, sz.out), F32),
        sem((6,)),
        pltpu.SemaphoreType.REGULAR,
        sem((2, sz.major)),
        sem((2, sz.major)),
        sem((2,)),
        sem((2, sz.major)),
        sem((2, sz.major)),
        sem((2, sz.pieces, sz.pairs)),
        sem((2, sz.pieces, sz.pairs)),
        sem((2, sz.pieces)),
        sem((2, sz.pieces)),
        sem((2, sz.pieces, sz.pairs)),
        sem((2, sz.pieces, sz.pairs)),
        sem((2, sz.pieces)),
        sem((2, sz.pieces)),
        sem((2, sz.pieces, sz.pairs)),
        sem((2, sz.pieces, sz.pairs)),
        sem((2, sz.major, sz.shares)),
        sem((2, sz.major, sz.shares)),
        sem((2, sz.major, sz.shares)),
        sem((2, sz.major, sz.shares)),
        sem((2, sz.shares)),
        sem((sz.devices,)),
        sem((sz.devices,)),
    ]
    macs = 6 * sz.real * TAPS * sz.chan * sz.out
    rows = (sz.real, sz.out)
    return pl.pallas_call(
        functools.partial(body, sz),
        out_shape=[
            vmem(rows, BF16),
            vmem(rows, BF16),
            vmem(rows, F32),
            vmem((2, sz.rows, sz.out), F32),
            vmem((sz.tensor, 8, sz.out), F32),
        ],
        in_specs=[pl.BlockSpec(memory_space=pltpu.HBM)] * 5,
        out_specs=[pl.BlockSpec(memory_space=vmem)] * 5,
        scratch_shapes=shapes,
        compiler_params=pltpu.CompilerParams(
            collective_id=0, has_side_effects=True, vmem_limit_bytes=sz.grant
        ),
        cost_estimate=pl.CostEstimate(flops=2 * macs, bytes_accessed=6_000_000, transcendentals=0),
        name="train_step",
    )(*(pltpu.with_memory_space_constraint(x, pltpu.HBM) for x in (frames, item_mask, weights, biases, cotangent)))


def finish_body(
    sz,
    act4,
    act5,
    igrad,
    grads,
    stats,
    weights,
    first,
    second,
    biases_ref,
    bias_first_ref,
    bias_second_ref,
    act4_out,
    act5_out,
    igrad_out,
    norm_out,
    weights_out,
    first_out,
    second_out,
    biases_out,
    bias_first_out,
    bias_second_out,
    olds,
    news,
    in_sem,
    out_sem,
    move_sem,
):
    targets = (weights_out, first_out, second_out)
    parts = [(l, pl.ds(r * sz.rows // 2, sz.rows // 2)) for l in (0, 1) for r in (0, 1)]
    if sz.rows % 16:
        parts = [(l, pl.ds(0, sz.rows)) for l in (0, 1)]
    stores = [
        [pltpu.make_async_copy(news.at[l, i, r], ref.at[l, r], out_sem.at[p, i]) for i, ref in enumerate(targets)]
        for p, (l, r) in enumerate(parts)
    ]
    moves = [
        pltpu.make_async_copy(held, ref, move_sem.at[i])
        for i, (held, ref) in enumerate(((act4, act4_out), (act5, act5_out), (igrad, igrad_out)))
    ]
    loads = [
        pltpu.make_async_copy(ref, olds.at[i], in_sem.at[i])
        for i, ref in enumerate((biases_ref, bias_first_ref, bias_second_ref))
    ]
    for copy in (*loads, *moves):
        copy.start()
    bias_grad = jnp.concatenate([stats[q, 1:3, :] for q in range(sz.tensor)], axis=1)
    squares = jnp.sum(stats[:, 0, :], axis=(0, 1), keepdims=True) + jnp.sum(
        bias_grad * bias_grad, axis=(0, 1), keepdims=True
    )
    grad_norm = jnp.sqrt(squares)
    factor = jnp.minimum(1.0, CLIP_NORM / (grad_norm + 1e-06))
    norm_out[...] = grad_norm
    for p, (l, r) in enumerate(parts):
        news[l, 0, r], news[l, 1, r], news[l, 2, r] = adam_update(
            weights[l, r], grads[l, r] * factor, first[l, r], second[l, r], RATE, DECAY
        )
        for copy in stores[p]:
            copy.start()
    for copy in loads:
        copy.wait()
    biases_out[...], bias_first_out[...], bias_second_out[...] = adam_update(
        olds[0], bias_grad * factor, olds[1], olds[2], BIAS_RATE, 0.0
    )
    for copy in (*moves, *(copy for part in stores for copy in part)):
        copy.wait()


def finish(sz, act4, act5, igrad, grads, stats, weights, first, second, biases, bias_first, bias_second):
    inside = pl.BlockSpec(memory_space=pltpu.VMEM)
    outside = pl.BlockSpec(memory_space=pltpu.HBM)
    like = lambda x: jax.ShapeDtypeStruct(x.shape, x.dtype)
    sem = pltpu.SemaphoreType.DMA
    held = [pltpu.with_memory_space_constraint(x, pltpu.VMEM) for x in (act4, act5, igrad, grads, stats, weights, first, second)]
    given = [pltpu.with_memory_space_constraint(x, pltpu.HBM) for x in (biases, bias_first, bias_second)]
    return pl.pallas_call(
        functools.partial(finish_body, sz),
        out_shape=[
            like(act4),
            like(act5),
            like(igrad),
            jax.ShapeDtypeStruct((1, 1), F32),
            like(weights),
            like(first),
            like(second),
            like(biases),
            like(bias_first),
            like(bias_second),
        ],
        in_specs=[inside] * 8 + [outside] * 3,
        out_specs=[outside] * 3 + [inside] + [outside] * 3 + [inside] * 3,
        scratch_shapes=[
            pltpu.VMEM((3, *biases.shape), F32),
            pltpu.VMEM((2, 3, sz.rows, sz.out), F32),
            sem((3,)),
            sem((4, 3)),
            sem((3,)),
        ],
        compiler_params=pltpu.CompilerParams(vmem_limit_bytes=8 * 1024 * 1024),
        cost_estimate=pl.CostEstimate(flops=5_000_000, bytes_accessed=7_000_000, transcendentals=0),
        name="clip_and_adamw",
    )(*held, *given)


def on_device(
    mesh,
    frames,
    item_mask,
    weights,
    biases,
    cotangent,
    weight_first,
    weight_second,
    bias_first,
    bias_second,
):
    sz = Sizes(mesh, frames.shape, weights.shape)

    def flat(maps):
        return jnp.transpose(maps, (1, 2, 0, 3)).reshape(sz.real, sz.out)

    def square(rows):
        return jnp.transpose(rows.reshape(sz.height, sz.width, sz.items, sz.out), (2, 0, 1, 3))

    made = train_step(sz, flat(frames), item_mask, weights, biases, flat(cotangent))
    act_four, act_five, input_grad, grad_norm, *rest = finish(
        sz, *made, weights, weight_first, weight_second, biases, bias_first, bias_second
    )
    return (square(act_four), square(act_five), square(input_grad), grad_norm.reshape(()), *rest)


def solution(mesh):
    split = P("dp", None, None, "tensor")
    rows = P(None, "dp", "tensor")
    in_specs = (split, P("dp"), rows, P(), split, rows, rows, P(), P())
    out_specs = (split, split, split, P(), rows, rows, rows, P(), P(), P())
    return jax.shard_map(
        functools.partial(on_device, mesh), mesh=mesh, in_specs=in_specs, out_specs=out_specs, check_vma=False
    )
```

```python
import functools
import math

import jax
import jax.numpy as jnp
from jax import lax
from jax.experimental import pallas as pl
from jax.experimental.pallas import tpu as pltpu
from jax.sharding import PartitionSpec as P

STEP = 5
CLIP_NORM = 1.0
BETA_ONE = 0.5
BETA_TWO = 0.5
RATE = 0.01
BIAS_RATE = 0.03
DECAY = 0.1
EPSILON = 1e-08

MESH = pl.DeviceIdType.MESH
BF16 = jnp.bfloat16
F32 = jnp.float32
ROOT = math.sqrt(2.0 / math.pi)
CUBE = 0.044715
TAPS = 9
WIDE = 256


def gelu_parts(value):
    square = value * value
    th = jnp.tanh(ROOT * value * (1.0 + CUBE * square))
    half = 0.5 * (1.0 + th)
    slope = half + 0.5 * value * (1.0 - th * th) * (ROOT * (1.0 + 3.0 * CUBE * square))
    return value * half, slope


def flip_bits(index, mask):
    bit = 1
    while bit <= mask:
        if mask & bit:
            index = index + bit - 2 * bit * lax.rem(lax.div(index, bit), 2)
        bit *= 2
    return index


def adam_update(param, grad, first, second, rate, decay):
    first_new = BETA_ONE * first + (1.0 - BETA_ONE) * grad
    second_new = BETA_TWO * second + (1.0 - BETA_TWO) * grad * grad
    corrected = first_new * (1.0 / (1.0 - BETA_ONE**STEP))
    scaled = jnp.sqrt(second_new * (1.0 / (1.0 - BETA_TWO**STEP))) + EPSILON
    return (param - rate * (corrected / scaled + decay * param), first_new, second_new)


class Sizes:
    def __init__(self, mesh, frames_shape, weights_shape):
        self.dp = mesh.shape["dp"]
        self.tensor = mesh.shape["tensor"]
        self.items, self.height, self.width, self.out = frames_shape
        self.chan = self.out * self.tensor
        self.rows = weights_shape[1]
        self.own_in = self.rows // TAPS
        self.cols = TAPS * self.out
        self.major = self.dp // 2
        self.pairs = self.tensor // 2
        self.slots = self.dp // self.tensor
        self.spots = self.height * self.width
        self.real = self.spots * self.items
        self.span = -(-self.real // 16) * 16
        self.halo = (self.width + 1) * self.items
        self.pieces = next(n for n in (5, 4, 3, 2, 1) if self.span // 16 % n == 0)
        self.piece = self.span // self.pieces
        self.groups = ((0, self.pieces // 2), (self.pieces // 2, self.pieces))
        self.wire = BF16 if self.own_in % 16 == 0 else F32
        self.line = self.major == 4
        self.far_order = (2, 1, 3) if self.line else tuple(range(1, self.major))
        cut = (TAPS + 1) // 2 * self.out
        self.parts = (((0, cut), (cut, self.cols)), ((0, self.cols),))
        self.devices = self.dp * self.tensor
        self.shares = 2 if self.own_in % 32 == 0 else 1
        self.share = self.own_in // self.shares
        self.grant = (44 if self.wire == BF16 else 54) * 1024 * 1024


def body(
    sz,
    frames_ref,
    mask_ref,
    weights_ref,
    biases_ref,
    cot_ref,
    act4_out,
    act5_out,
    igrad_out,
    grads_out,
    stats_out,
    w_in,
    stage,
    cot,
    biases,
    mask,
    keep,
    w_all,
    frames,
    acts,
    spread,
    edges,
    slope4,
    act5,
    shifted,
    deltas,
    part_send,
    part_recv,
    part_own,
    cross_send,
    cross_recv,
    igrad,
    kgrad,
    near_send,
    near_recv,
    far_send,
    far_recv,
    relay_recv,
    shard,
    bias_sum,
    stats_all,
    local_sem,
    ready,
    wz_send,
    wz_recv,
    wf_send,
    wy_send,
    wy_recv,
    ax_send,
    ax_recv,
    as_send,
    as_recv,
    af_send,
    af_recv,
    rs_send,
    rs_recv,
    rx_send,
    rx_recv,
    gy_send,
    gy_recv,
    gz_send,
    gz_recv,
    gr_recv,
    st_send,
    st_recv,
):
    d = lax.axis_index("dp")
    t = lax.axis_index("tensor")
    major, minor = lax.div(d, 2), lax.rem(d, 2)
    near = (2 * major + 1 - minor, t)
    pair, side = lax.div(t, 2), lax.rem(t, 2)
    sibling = (d, 2 * pair + 1 - side)

    def far_slot(k):
        return 2 * flip_bits(major, k) + minor

    def near_slot(k):
        return 2 * flip_bits(major, k) + 1 - minor

    def far(k):
        return (far_slot(k), t)

    def cross_rank(k):
        return 2 * lax.rem(pair + k, sz.pairs) + side

    def cross_from(k):
        return 2 * lax.rem(pair + sz.pairs - k, sz.pairs) + side

    def remote(src, dst, send, recv, device):
        return pltpu.make_async_remote_copy(
            src_ref=src, dst_ref=dst, send_sem=send, recv_sem=recv, device_id=device, device_id_type=MESH
        )

    def same(block, send, recv, device):
        return remote(block, block, send, recv, device)

    all_pieces = range(sz.pieces)

    def rows_of(p):
        return pl.ds(pl.multiple_of(p * sz.piece, 16), sz.piece)

    far_steps = range(1, sz.major)
    cross_steps = range(1, sz.pairs)
    middle = jnp.logical_and(major > 0, major < sz.major - 1)
    far_steps = range(1, sz.major)
    cross_steps = range(1, sz.pairs)
    signal = functools.partial(pl.semaphore_signal, inc=1, device_id_type=MESH)

    barrier = pltpu.get_barrier_semaphore()
    if sz.line:
        pl.when(major > 0)(lambda: signal(barrier, device_id=(d - 2, t)))
        pl.when(major < sz.major - 1)(lambda: signal(barrier, device_id=(d + 2, t)))
        joined = jnp.where(middle, 2, 1) + 1 + sz.pairs
    else:
        for k in far_steps:
            signal(barrier, device_id=far(k))
        joined = sz.major + sz.pairs
    signal(barrier, device_id=near)
    for k in cross_steps:
        signal(barrier, device_id=(d, cross_rank(k)))
    signal(barrier, device_id=sibling)

    load_w = [pltpu.make_async_copy(weights_ref.at[l], w_in.at[l], local_sem.at[l]) for l in (0, 1)]
    load_frames = pltpu.make_async_copy(frames_ref, stage.at[0], local_sem.at[2])
    load_cot = pltpu.make_async_copy(cot_ref, stage.at[1], local_sem.at[3])
    load_biases = pltpu.make_async_copy(biases_ref, biases, local_sem.at[4])
    load_mask = pltpu.make_async_copy(mask_ref, mask, local_sem.at[5])
    for copy in (load_w[0], load_frames, load_w[1], load_cot, load_biases, load_mask):
        copy.start()

    def weight_out(l, k):
        return same(w_all.at[l, d], wz_send.at[l, k], wz_recv.at[l, k], far(k))

    def weight_relay(l):
        return same(w_all.at[l, far_slot(2)], wf_send.at[l], wz_recv.at[l, 3], far(1))

    def weight_over(l, k, part):
        first, last = sz.parts[l][part]
        block = w_all.at[l, far_slot(k), :, first:last]
        return same(block, wy_send.at[l, k, part], wy_recv.at[l, k, part], near)

    def weights_over(l, k):
        for part in range(len(sz.parts[l])):
            weight_over(l, k, part).start()

    def weights_out(l):
        for k in sz.far_order:
            if sz.line and k == 3:
                pl.when(middle)(weight_out(l, k).start)
            else:
                weight_out(l, k).start()

    def weights_on(l, steps):
        for k in steps:
            same(w_all.at[l, far_slot(k)], wz_send.at[l, k], wz_recv.at[l, k], far(k)).wait_recv()
            if sz.line and k == 2:
                pl.when(middle)(weight_relay(l).start)
            weights_over(l, k)

    def weights_here(l, part):
        first, last = sz.parts[l][part]
        for k in range(sz.major):
            block = w_all.at[l, near_slot(k), :, first:last]
            same(block, wy_send.at[l, k, part], wy_recv.at[l, k, part], near).wait_recv()

    def weights_sent(l):
        for k in range(sz.major):
            for part in range(len(sz.parts[l])):
                weight_over(l, k, part).wait_send()
            if sz.line and k == 3:

                @pl.when(middle)
                def _():
                    weight_out(l, k).wait_send()
                    weight_relay(l).wait_send()

            elif k:
                weight_out(l, k).wait_send()

    def round_weights(l):
        load_w[l].wait()
        for tap in range(TAPS):
            w_all[l, d, :, tap * sz.out : (tap + 1) * sz.out] = w_in[
                l, pl.ds(tap, sz.own_in, stride=TAPS), :
            ].astype(sz.wire)

    def gather_sends(g, maps, p, rows):
        own = maps.at[t, rows]
        out = [same(own, ax_send.at[g, p, k], ax_recv.at[g, p, k], (d, cross_rank(k))) for k in cross_steps]
        out.append(same(own, as_send.at[g, p], as_recv.at[g, p], sibling))
        return out

    def gather_forward(g, maps, p, rows, k):
        return same(maps.at[cross_from(k), rows], af_send.at[g, p, k], af_recv.at[g, p, k], sibling)

    def gather_pass_on(g, maps, p, rows):
        for k in cross_steps:
            same(maps.at[cross_from(k), rows], ax_send.at[g, p, k], ax_recv.at[g, p, k], sibling).wait_recv()
            gather_forward(g, maps, p, rows, k).start()

    def gather_here(g, maps, p, rows):
        same(maps.at[sibling[1], rows], as_send.at[g, p], as_recv.at[g, p], sibling).wait_recv()
        for k in cross_steps:
            rank = 2 * lax.rem(pair + sz.pairs - k, sz.pairs) + 1 - side
            same(maps.at[rank, rows], af_send.at[g, p, k], af_recv.at[g, p, k], sibling).wait_recv()

    def gather_sent(g, maps, p, rows):
        for copy in gather_sends(g, maps, p, rows):
            copy.wait_send()
        for k in cross_steps:
            gather_forward(g, maps, p, rows, k).wait_send()

    whole = pl.ds(0, sz.span)

    def product(l, part, maps, group):
        rows = slice(group[0] * sz.piece, group[1] * sz.piece)
        left = jnp.concatenate([maps[q, rows] for q in range(sz.tensor)], axis=1)
        first, last = sz.parts[l][part]
        for start in range(first, last, WIDE):
            stop = min(start + WIDE, last)
            right = w_all[l, :, :, start:stop].reshape(sz.chan, stop - start).astype(BF16)
            spread[sz.halo + rows.start : sz.halo + rows.stop, start:stop] = jnp.dot(
                left, right, preferred_element_type=F32
            )

    def own_bias(l):
        return biases[l : l + 1, pl.ds(pl.multiple_of(t * sz.out, sz.out), sz.out)]

    def shifted_sum(p):
        sums = []
        for b in range(3):
            total = None
            for a in range(3):
                shift = sz.items * (sz.width * (a - 1) + b - 1)
                tap = 3 * a + b
                rows = pl.ds(pl.multiple_of(p * sz.piece + sz.halo + shift, 8), sz.piece)
                term = spread[rows, tap * sz.out : (tap + 1) * sz.out]
                total = term if total is None else total + term
            sums.append(total)
        return sums[1] + sums[0] * edges[0, rows_of(p)] + sums[2] * edges[1, rows_of(p)]

    def note_delta(l, p, delta):
        bias_sum[l] += jnp.sum(delta.reshape(sz.piece // 8, 8, sz.out), axis=0)
        rows = pl.ds(pl.multiple_of(p * sz.piece + sz.halo, 8), sz.piece)
        shifted[0, rows] = delta * edges[0, rows_of(p)]
        shifted[1, rows] = delta
        shifted[2, rows] = delta * edges[1, rows_of(p)]

    def spread_delta(p):
        for a in range(3):
            for b in range(3):
                shift = sz.items * (sz.width * (a - 1) + b - 1)
                tap = 3 * a + b
                rows = pl.ds(pl.multiple_of(p * sz.piece + sz.halo - shift, 8), sz.piece)
                deltas[rows_of(p), tap * sz.out : (tap + 1) * sz.out] = shifted[b, rows].astype(BF16)

    def finish_four(first, last):
        @pl.loop(first, last)
        def _(p):
            act, slope = gelu_parts(shifted_sum(p) + own_bias(0))
            acts[t, rows_of(p)] = (act * edges[2, rows_of(p)]).astype(BF16)
            slope4[rows_of(p)] = slope * edges[2, rows_of(p)]
            for copy in gather_sends(1, acts, p, rows_of(p)):
                copy.start()

    def by_item(value):
        return (value.reshape(sz.piece // sz.items, sz.items, sz.out) * keep[...]).reshape(sz.piece, sz.out)

    def finish_five(first, last):
        @pl.loop(first, last)
        def _(p):
            act, slope = gelu_parts(shifted_sum(p) + own_bias(1))
            act5[rows_of(p)] = by_item(act).astype(BF16)
            delta = (by_item(cot[rows_of(p)].astype(F32)) * slope).astype(BF16).astype(F32)
            note_delta(1, p, delta)
            pl.when(p > 0)(lambda: spread_delta(p - 1))

    def part_copy(l, p):
        rows = rows_of(p)
        return remote(
            part_send.at[l, :, rows], part_recv.at[l, :, rows], rs_send.at[l, p], rs_recv.at[l, p], sibling
        )

    def cross_copy(l, p, k):
        rows = rows_of(p)
        return remote(
            cross_send.at[l, k, rows],
            cross_recv.at[l, k, rows],
            rx_send.at[l, p, k],
            rx_recv.at[l, p, k],
            (d, cross_rank(k)),
        )

    def back_product(l, group, which):
        blocks = [
            w_all[l, pl.ds((2 * j + which) * sz.slots, sz.slots)].reshape(sz.out, sz.cols) for j in range(sz.pairs)
        ]
        right = jnp.concatenate(blocks, axis=0).astype(BF16)
        left = deltas[group[0] * sz.piece : group[1] * sz.piece]
        out = lax.dot_general(left, right, (((1,), (1,)), ((), ())), preferred_element_type=F32)
        return [out[:, j * sz.out : (j + 1) * sz.out] for j in range(sz.pairs)]

    def back_to_sibling(l, group):
        rows = slice(group[0] * sz.piece, group[1] * sz.piece)
        for j, block in enumerate(back_product(l, group, 1 - side)):
            part_send[l, j, rows] = block.astype(BF16)
        for p in range(*group):
            part_copy(l, p).start()

    def back_own(l, group):
        rows = slice(group[0] * sz.piece, group[1] * sz.piece)
        for j, block in enumerate(back_product(l, group, side)):
            part_own[j, rows] = block

    def back_across(l, group):
        @pl.loop(*group)
        def _(p):
            part_copy(l, p).wait_recv()
            for k in cross_steps:
                j = lax.rem(pair + k, sz.pairs)
                total = part_own[j, rows_of(p)] + part_recv[l, j, rows_of(p)].astype(F32)
                cross_send[l, k, rows_of(p)] = total.astype(BF16)
                cross_copy(l, p, k).start()

    def back_products(l, first=None, second=None):
        for group, meanwhile in zip(sz.groups, (first, second)):
            back_to_sibling(l, group)
            if meanwhile:
                meanwhile()
            back_own(l, group)
            back_across(l, group)

    def back_total(l, p):
        total = part_own[pair, rows_of(p)] + part_recv[l, pair, rows_of(p)].astype(F32)
        for k in cross_steps:
            cross_copy(l, p, k).wait_recv()
            total += cross_recv[l, k, rows_of(p)].astype(F32)
        return total

    shares = range(sz.shares)

    def share_of(h):
        return slice(h * sz.share, (h + 1) * sz.share)

    def near_copy(l, k, h):
        return remote(
            near_send.at[l, k, share_of(h)],
            near_recv.at[l, k, share_of(h)],
            gy_send.at[l, k, h],
            gy_recv.at[l, k, h],
            near,
        )

    def far_copy(l, k, h):
        return remote(
            far_send.at[l, k, share_of(h)],
            far_recv.at[l, k, share_of(h)],
            gz_send.at[l, k, h],
            gz_recv.at[l, k, h],
            far(k),
        )

    half = sz.tensor // 2
    far_half = [k for k in reversed(far_steps) if k >= sz.major // 2]
    near_half = [k for k in far_steps if k < sz.major // 2]

    def grads_block(l, maps, block, width, steps):
        left = jnp.concatenate([maps[block + q] for q in range(width)], axis=1)
        into = pl.ds(block * sz.slots, width * sz.slots)
        for start in range(0, sz.cols, WIDE):
            stop = min(start + WIDE, sz.cols)
            product = lax.dot_general(
                left, deltas[:, start:stop], (((0,), (0,)), ((), ())), preferred_element_type=F32
            )
            kgrad[l, into, :, start:stop] = product.reshape(width * sz.slots, sz.own_in, stop - start)
        for k in steps:
            near_send[l, k] = kgrad[l, near_slot(k)].astype(sz.wire)
            for h in shares:
                near_copy(l, k, h).start()

    own_half = lax.div(major, sz.major // 2)

    def grads_half(l, maps, other):
        first = (1 - own_half if other else own_half) * half
        grads_block(l, maps, first, half, far_half if other else [*near_half, 0])

    def grads_place(l, maps, k):
        grads_block(l, maps, flip_bits(major, k), 1, [k])

    def relay_copy(l, h):
        rows = share_of(h)
        return remote(
            far_send.at[l, 3, rows], relay_recv.at[l, rows], gz_send.at[l, 3, h], gr_recv.at[l, h], far(1)
        )

    def grads_far(l, k):
        for h in shares:
            rows = share_of(h)
            near_copy(l, k, h).wait_recv()
            total = kgrad[l, far_slot(k), rows] + near_recv[l, k, rows].astype(F32)
            if sz.line and k == 2:

                @pl.when(middle)
                def _():
                    relay_copy(l, h).wait_recv()
                    far_send[l, k, rows] = (total + relay_recv[l, rows].astype(F32)).astype(sz.wire)

                @pl.when(jnp.logical_not(middle))
                def _():
                    far_send[l, k, rows] = total.astype(sz.wire)

            else:
                far_send[l, k, rows] = total.astype(sz.wire)
            if sz.line and k == 3:
                pl.when(middle)(far_copy(l, k, h).start)
                pl.when(jnp.logical_not(middle))(relay_copy(l, h).start)
            else:
                far_copy(l, k, h).start()

    def grads_sum(l):
        for h in shares:
            near_copy(l, 0, h).wait_recv()
            for k in far_steps:
                if sz.line and k == 3:
                    pl.when(middle)(far_copy(l, k, h).wait_recv)
                else:
                    far_copy(l, k, h).wait_recv()
        total = kgrad[l, d] + near_recv[l, 0].astype(F32)
        for k in far_steps:
            total += far_recv[l, k].astype(F32)
        shard[...] = total
        squares = jnp.sum((total * total).reshape(sz.own_in // 8, 8, sz.cols), axis=0)
        return sum(squares[:, tap * sz.out : (tap + 1) * sz.out] for tap in range(TAPS))

    def grads_out_rows(l):
        for tap in range(TAPS):
            grads_out[l, pl.ds(tap, sz.own_in, stride=TAPS), :] = shard[:, tap * sz.out : (tap + 1) * sz.out]

    round_weights(0)
    pl.semaphore_wait(barrier, joined)
    if sz.line:

        @pl.when(middle)
        def _():
            signal(ready, device_id=(d - 2, t))
            signal(ready, device_id=(d + 2, t))

    weights_over(0, 0)
    tail = sz.span - 16
    frames[t, tail:] = jnp.zeros((16, sz.out), BF16)
    load_frames.wait()
    frames[t, 0 : sz.real] = stage[0]
    for copy in gather_sends(0, frames, 0, whole):
        copy.start()
    round_weights(1)
    weights_over(1, 0)
    if sz.line:
        pl.semaphore_wait(ready, 1)
    weights_out(0)

    rest = sz.halo + sz.span
    for first in (0, rest):
        spread[first : first + sz.halo, :] = jnp.zeros((sz.halo, sz.cols), F32)
        shifted[:, first : first + sz.halo, :] = jnp.zeros((3, sz.halo, sz.out), F32)
    edges[...] = jnp.ones_like(edges)
    nothing = jnp.zeros((sz.items, sz.out), F32)
    for i in range(sz.height):
        for e, j in ((0, 0), (1, sz.width - 1)):
            first = (i * sz.width + j) * sz.items
            edges[e, first : first + sz.items, :] = nothing
    edges[2, sz.real :, :] = jnp.zeros((sz.span - sz.real, sz.out), F32)
    bias_sum[...] = jnp.zeros_like(bias_sum)
    if sz.line:

        @pl.when(jnp.logical_not(middle))
        def _():
            far_recv[:, 3] = jnp.zeros((2, sz.own_in, sz.cols), sz.wire)


    cot[tail:] = jnp.zeros((16, sz.out), BF16)
    load_cot.wait()
    cot[0 : sz.real] = stage[1]
    load_biases.wait()
    load_mask.wait()
    item = lax.broadcasted_iota(jnp.int32, (sz.items, sz.out), 0)
    kept = jnp.zeros((sz.items, sz.out), F32)
    for n in range(sz.items):
        kept = jnp.where(item == n, mask[n].astype(F32), kept)
    keep[...] = kept

    one, two = sz.groups
    weights_on(0, far_steps)
    weights_out(1)
    gather_pass_on(0, frames, 0, whole)
    gather_here(0, frames, 0, whole)
    weights_here(0, 0)
    product(0, 0, frames, one)
    product(0, 0, frames, two)
    weights_here(0, 1)
    weights_on(1, far_steps[:1])
    product(0, 1, frames, one)
    finish_four(0, one[1] - 1)
    weights_on(1, far_steps[1:2])
    product(0, 1, frames, two)
    finish_four(one[1] - 1, sz.pieces)

    weights_on(1, far_steps[2:])
    act4_out[...] = acts[t, 0 : sz.real]
    for p in all_pieces:
        gather_pass_on(1, acts, p, rows_of(p))
    for p in range(*one):
        gather_here(1, acts, p, rows_of(p))
    weights_here(1, 0)
    product(1, 0, acts, one)
    for p in range(*two):
        gather_here(1, acts, p, rows_of(p))
    finish_five(0, one[1] - 1)
    product(1, 0, acts, two)
    finish_five(one[1] - 1, sz.pieces)
    spread_delta(sz.pieces - 1)
    if sz.line and sz.tensor == sz.major:
        back_products(1, lambda: grads_place(1, acts, 3), lambda: grads_place(1, acts, 2))
    else:
        grads_half(1, acts, True)
        back_products(1)
    grads_half(1, acts, False)
    act5_out[...] = act5[0 : sz.real]
    grads_far(1, far_half[0])

    @pl.loop(0, sz.pieces)
    def _(p):
        note_delta(0, p, (back_total(1, p) * slope4[rows_of(p)]).astype(BF16).astype(F32))
        pl.when(p > 0)(lambda: spread_delta(p - 1))

    spread_delta(sz.pieces - 1)
    if sz.line and sz.tensor == sz.major:
        grads_place(0, frames, 3)
        grads_place(0, frames, 2)
    else:
        grads_half(0, frames, True)
    for k in far_half[1:]:
        grads_far(1, k)
    grads_half(0, frames, False)
    for k in near_half:
        grads_far(1, k)
    back_products(0, second=lambda: grads_far(0, far_half[0]))
    for k in (*far_half[1:], *near_half):
        grads_far(0, k)
    squares = grads_sum(1)
    grads_out_rows(1)

    @pl.loop(0, sz.pieces)
    def _(p):
        igrad[rows_of(p)] = back_total(0, p)

    igrad_out[...] = igrad[0 : sz.real]

    me = d * sz.tensor + t
    for l in (0, 1):
        stats_all[me, l + 1 : l + 2, :] = jnp.sum(bias_sum[l], axis=0, keepdims=True)
    squares += grads_sum(0)
    stats_all[me, 0:1, :] = jnp.sum(squares, axis=0, keepdims=True)
    def stats_copy(a, b, mine):
        device = (flip_bits(d, a), flip_bits(t, b))
        slot = me if mine else device[0] * sz.tensor + device[1]
        k = a * sz.tensor + b
        return same(stats_all.at[slot, 0:3], st_send.at[k], st_recv.at[k], device)

    others = [(a, b) for a in reversed(range(sz.dp)) for b in reversed(range(sz.tensor)) if a or b]
    for a, b in others:
        stats_copy(a, b, True).start()

    grads_out_rows(0)
    for l in (0, 1):
        weights_sent(l)
        for h in shares:
            for k in far_steps:
                far_copy(l, k, h).wait_send()
            for k in range(sz.major):
                near_copy(l, k, h).wait_send()

        @pl.loop(0, sz.pieces)
        def _(p):
            part_copy(l, p).wait_send()
            for k in cross_steps:
                cross_copy(l, p, k).wait_send()

    gather_sent(0, frames, 0, whole)

    @pl.loop(0, sz.pieces)
    def _(p):
        gather_sent(1, acts, p, rows_of(p))

    for a, b in others:
        stats_copy(a, b, False).wait_recv()

    for q in range(sz.tensor):
        total = stats_all[q, 0:3]
        for slot in range(q + sz.tensor, sz.devices, sz.tensor):
            total += stats_all[slot, 0:3]
        stats_out[q, 0:3] = total

    for a, b in others:
        stats_copy(a, b, True).wait_send()


def train_step(sz, frames, item_mask, weights, biases, cotangent):
    sem = pltpu.SemaphoreType.DMA
    vmem = pltpu.VMEM
    maps = (sz.span, sz.out)
    block = (sz.own_in, sz.cols)
    shapes = [
        vmem((2, sz.rows, sz.out), F32),
        vmem((2, sz.real, sz.out), BF16),
        vmem(maps, BF16),
        vmem((2, sz.chan), F32),
        pltpu.SMEM((sz.items,), jnp.int32),
        vmem((sz.items, sz.out), F32),
        vmem((2, sz.dp, *block), sz.wire),
        vmem((sz.tensor, *maps), BF16),
        vmem((sz.tensor, *maps), BF16),
        vmem((sz.span + 2 * sz.halo, sz.cols), F32),
        vmem((3, *maps), F32),
        vmem(maps, F32),
        vmem(maps, BF16),
        vmem((3, sz.span + 2 * sz.halo, sz.out), F32),
        vmem((sz.span, sz.cols), BF16),
        vmem((2, sz.pairs, *maps), BF16),
        vmem((2, sz.pairs, *maps), BF16),
        vmem((sz.pairs, *maps), F32),
        vmem((2, sz.pairs, *maps), BF16),
        vmem((2, sz.pairs, *maps), BF16),
        vmem(maps, F32),
        vmem((2, sz.dp, *block), F32),
        vmem((2, sz.major, *block), sz.wire),
        vmem((2, sz.major, *block), sz.wire),
        vmem((2, sz.major, *block), sz.wire),
        vmem((2, sz.major, *block), sz.wire),
        vmem((2, *block), sz.wire),
        vmem(block, F32),
        vmem((2, 8, sz.out), F32),
        vmem((sz.devices, 8, sz.out), F32),
        sem((6,)),
        pltpu.SemaphoreType.REGULAR,
        sem((2, sz.major)),
        sem((2, sz.major)),
        sem((2,)),
        sem((2, sz.major, 2)),
        sem((2, sz.major, 2)),
        sem((2, sz.pieces, sz.pairs)),
        sem((2, sz.pieces, sz.pairs)),
        sem((2, sz.pieces)),
        sem((2, sz.pieces)),
        sem((2, sz.pieces, sz.pairs)),
        sem((2, sz.pieces, sz.pairs)),
        sem((2, sz.pieces)),
        sem((2, sz.pieces)),
        sem((2, sz.pieces, sz.pairs)),
        sem((2, sz.pieces, sz.pairs)),
        sem((2, sz.major, sz.shares)),
        sem((2, sz.major, sz.shares)),
        sem((2, sz.major, sz.shares)),
        sem((2, sz.major, sz.shares)),
        sem((2, sz.shares)),
        sem((sz.devices,)),
        sem((sz.devices,)),
    ]
    macs = 6 * sz.real * TAPS * sz.chan * sz.out
    rows = (sz.real, sz.out)
    return pl.pallas_call(
        functools.partial(body, sz),
        out_shape=[
            vmem(rows, BF16),
            vmem(rows, BF16),
            vmem(rows, F32),
            vmem((2, sz.rows, sz.out), F32),
            vmem((sz.tensor, 8, sz.out), F32),
        ],
        in_specs=[pl.BlockSpec(memory_space=pltpu.HBM)] * 5,
        out_specs=[pl.BlockSpec(memory_space=vmem)] * 5,
        scratch_shapes=shapes,
        compiler_params=pltpu.CompilerParams(
            collective_id=0, has_side_effects=True, vmem_limit_bytes=sz.grant
        ),
        cost_estimate=pl.CostEstimate(flops=2 * macs, bytes_accessed=6_000_000, transcendentals=0),
        name="train_step",
    )(*(pltpu.with_memory_space_constraint(x, pltpu.HBM) for x in (frames, item_mask, weights, biases, cotangent)))


def finish_body(
    sz,
    act4,
    act5,
    igrad,
    grads,
    stats,
    weights,
    first,
    second,
    biases_ref,
    bias_first_ref,
    bias_second_ref,
    act4_out,
    act5_out,
    igrad_out,
    norm_out,
    weights_out,
    first_out,
    second_out,
    biases_out,
    bias_first_out,
    bias_second_out,
    olds,
    news,
    in_sem,
    out_sem,
    move_sem,
):
    targets = (weights_out, first_out, second_out)
    parts = [(l, pl.ds(r * sz.rows // 2, sz.rows // 2)) for l in (0, 1) for r in (0, 1)]
    if sz.rows % 16:
        parts = [(l, pl.ds(0, sz.rows)) for l in (0, 1)]
    stores = [
        [pltpu.make_async_copy(news.at[l, i, r], ref.at[l, r], out_sem.at[p, i]) for i, ref in enumerate(targets)]
        for p, (l, r) in enumerate(parts)
    ]
    moves = [
        pltpu.make_async_copy(held, ref, move_sem.at[i])
        for i, (held, ref) in enumerate(((act4, act4_out), (act5, act5_out), (igrad, igrad_out)))
    ]
    loads = [
        pltpu.make_async_copy(ref, olds.at[i], in_sem.at[i])
        for i, ref in enumerate((biases_ref, bias_first_ref, bias_second_ref))
    ]
    for copy in (*loads, *moves):
        copy.start()
    bias_grad = jnp.concatenate([stats[q, 1:3, :] for q in range(sz.tensor)], axis=1)
    squares = jnp.sum(stats[:, 0, :], axis=(0, 1), keepdims=True) + jnp.sum(
        bias_grad * bias_grad, axis=(0, 1), keepdims=True
    )
    grad_norm = jnp.sqrt(squares)
    factor = jnp.minimum(1.0, CLIP_NORM / (grad_norm + 1e-06))
    norm_out[...] = grad_norm
    for p, (l, r) in enumerate(parts):
        news[l, 0, r], news[l, 1, r], news[l, 2, r] = adam_update(
            weights[l, r], grads[l, r] * factor, first[l, r], second[l, r], RATE, DECAY
        )
        for copy in stores[p]:
            copy.start()
    for copy in loads:
        copy.wait()
    biases_out[...], bias_first_out[...], bias_second_out[...] = adam_update(
        olds[0], bias_grad * factor, olds[1], olds[2], BIAS_RATE, 0.0
    )
    for copy in (*moves, *(copy for part in stores for copy in part)):
        copy.wait()


def finish(sz, act4, act5, igrad, grads, stats, weights, first, second, biases, bias_first, bias_second):
    inside = pl.BlockSpec(memory_space=pltpu.VMEM)
    outside = pl.BlockSpec(memory_space=pltpu.HBM)
    like = lambda x: jax.ShapeDtypeStruct(x.shape, x.dtype)
    sem = pltpu.SemaphoreType.DMA
    held = [pltpu.with_memory_space_constraint(x, pltpu.VMEM) for x in (act4, act5, igrad, grads, stats, weights, first, second)]
    given = [pltpu.with_memory_space_constraint(x, pltpu.HBM) for x in (biases, bias_first, bias_second)]
    return pl.pallas_call(
        functools.partial(finish_body, sz),
        out_shape=[
            like(act4),
            like(act5),
            like(igrad),
            jax.ShapeDtypeStruct((1, 1), F32),
            like(weights),
            like(first),
            like(second),
            like(biases),
            like(bias_first),
            like(bias_second),
        ],
        in_specs=[inside] * 8 + [outside] * 3,
        out_specs=[outside] * 3 + [inside] + [outside] * 3 + [inside] * 3,
        scratch_shapes=[
            pltpu.VMEM((3, *biases.shape), F32),
            pltpu.VMEM((2, 3, sz.rows, sz.out), F32),
            sem((3,)),
            sem((4, 3)),
            sem((3,)),
        ],
        compiler_params=pltpu.CompilerParams(vmem_limit_bytes=8 * 1024 * 1024),
        cost_estimate=pl.CostEstimate(flops=5_000_000, bytes_accessed=7_000_000, transcendentals=0),
        name="clip_and_adamw",
    )(*held, *given)


def on_device(
    mesh,
    frames,
    item_mask,
    weights,
    biases,
    cotangent,
    weight_first,
    weight_second,
    bias_first,
    bias_second,
):
    sz = Sizes(mesh, frames.shape, weights.shape)

    def flat(maps):
        return jnp.transpose(maps, (1, 2, 0, 3)).reshape(sz.real, sz.out)

    def square(rows):
        return jnp.transpose(rows.reshape(sz.height, sz.width, sz.items, sz.out), (2, 0, 1, 3))

    made = train_step(sz, flat(frames), item_mask, weights, biases, flat(cotangent))
    act_four, act_five, input_grad, grad_norm, *rest = finish(
        sz, *made, weights, weight_first, weight_second, biases, bias_first, bias_second
    )
    return (square(act_four), square(act_five), square(input_grad), grad_norm.reshape(()), *rest)


def solution(mesh):
    split = P("dp", None, None, "tensor")
    rows = P(None, "dp", "tensor")
    in_specs = (split, P("dp"), rows, P(), split, rows, rows, P(), P())
    out_specs = (split, split, split, P(), rows, rows, rows, P(), P(), P())
    return jax.shard_map(
        functools.partial(on_device, mesh), mesh=mesh, in_specs=in_specs, out_specs=out_specs, check_vma=False
    )
```

```python
import functools
import math

import jax
import jax.numpy as jnp
from jax import lax
from jax.experimental import pallas as pl
from jax.experimental.pallas import tpu as pltpu
from jax.sharding import PartitionSpec as P

STEP = 5
CLIP_NORM = 1.0
BETA_ONE = 0.5
BETA_TWO = 0.5
RATE = 0.01
BIAS_RATE = 0.03
DECAY = 0.1
EPSILON = 1e-08

MESH = pl.DeviceIdType.MESH
BF16 = jnp.bfloat16
F32 = jnp.float32
ROOT = math.sqrt(2.0 / math.pi)
CUBE = 0.044715
TAPS = 9
WIDE = 256


def gelu_parts(value):
    square = value * value
    th = jnp.tanh(ROOT * value * (1.0 + CUBE * square))
    half = 0.5 * (1.0 + th)
    slope = half + 0.5 * value * (1.0 - th * th) * (ROOT * (1.0 + 3.0 * CUBE * square))
    return value * half, slope


def flip_bits(index, mask):
    bit = 1
    while bit <= mask:
        if mask & bit:
            index = index + bit - 2 * bit * lax.rem(lax.div(index, bit), 2)
        bit *= 2
    return index


def adam_update(param, grad, first, second, rate, decay):
    first_new = BETA_ONE * first + (1.0 - BETA_ONE) * grad
    second_new = BETA_TWO * second + (1.0 - BETA_TWO) * grad * grad
    corrected = first_new * (1.0 / (1.0 - BETA_ONE**STEP))
    scaled = jnp.sqrt(second_new * (1.0 / (1.0 - BETA_TWO**STEP))) + EPSILON
    return (param - rate * (corrected / scaled + decay * param), first_new, second_new)


class Sizes:
    def __init__(self, mesh, frames_shape, weights_shape):
        self.dp = mesh.shape["dp"]
        self.tensor = mesh.shape["tensor"]
        self.items, self.height, self.width, self.out = frames_shape
        self.chan = self.out * self.tensor
        self.rows = weights_shape[1]
        self.own_in = self.rows // TAPS
        self.cols = TAPS * self.out
        self.major = self.dp // 2
        self.pairs = self.tensor // 2
        self.slots = self.dp // self.tensor
        self.spots = self.height * self.width
        self.real = self.spots * self.items
        self.span = -(-self.real // 16) * 16
        self.halo = (self.width + 1) * self.items
        self.pieces = next(n for n in (5, 4, 3, 2, 1) if self.span // 16 % n == 0)
        self.piece = self.span // self.pieces
        self.groups = ((0, self.pieces // 2), (self.pieces // 2, self.pieces))
        self.wire = BF16 if self.own_in % 16 == 0 else F32
        self.line = self.major == 4
        self.far_order = (2, 1, 3) if self.line else tuple(range(1, self.major))
        cut = (TAPS + 1) // 2 * self.out
        self.parts = (((0, cut), (cut, self.cols)),) * 2
        self.devices = self.dp * self.tensor
        self.shares = 2 if self.own_in % 32 == 0 else 1
        self.share = self.own_in // self.shares
        self.grant = (44 if self.wire == BF16 else 54) * 1024 * 1024


def body(
    sz,
    frames_ref,
    mask_ref,
    weights_ref,
    biases_ref,
    cot_ref,
    act4_out,
    act5_out,
    igrad_out,
    grads_out,
    stats_out,
    w_in,
    stage,
    cot,
    biases,
    mask,
    keep,
    w_all,
    frames,
    acts,
    spread,
    edges,
    slope4,
    act5,
    shifted,
    deltas,
    part_send,
    part_recv,
    part_own,
    cross_send,
    cross_recv,
    igrad,
    kgrad,
    near_send,
    near_recv,
    far_send,
    far_recv,
    relay_recv,
    shard,
    bias_sum,
    stats_all,
    local_sem,
    ready,
    wz_send,
    wz_recv,
    wf_send,
    wy_send,
    wy_recv,
    ax_send,
    ax_recv,
    as_send,
    as_recv,
    af_send,
    af_recv,
    rs_send,
    rs_recv,
    rx_send,
    rx_recv,
    gy_send,
    gy_recv,
    gz_send,
    gz_recv,
    gr_recv,
    st_send,
    st_recv,
):
    d = lax.axis_index("dp")
    t = lax.axis_index("tensor")
    major, minor = lax.div(d, 2), lax.rem(d, 2)
    near = (2 * major + 1 - minor, t)
    pair, side = lax.div(t, 2), lax.rem(t, 2)
    sibling = (d, 2 * pair + 1 - side)

    def far_slot(k):
        return 2 * flip_bits(major, k) + minor

    def near_slot(k):
        return 2 * flip_bits(major, k) + 1 - minor

    def far(k):
        return (far_slot(k), t)

    def cross_rank(k):
        return 2 * lax.rem(pair + k, sz.pairs) + side

    def cross_from(k):
        return 2 * lax.rem(pair + sz.pairs - k, sz.pairs) + side

    def remote(src, dst, send, recv, device):
        return pltpu.make_async_remote_copy(
            src_ref=src, dst_ref=dst, send_sem=send, recv_sem=recv, device_id=device, device_id_type=MESH
        )

    def same(block, send, recv, device):
        return remote(block, block, send, recv, device)

    all_pieces = range(sz.pieces)

    def rows_of(p):
        return pl.ds(pl.multiple_of(p * sz.piece, 16), sz.piece)

    far_steps = range(1, sz.major)
    cross_steps = range(1, sz.pairs)
    middle = jnp.logical_and(major > 0, major < sz.major - 1)
    far_steps = range(1, sz.major)
    cross_steps = range(1, sz.pairs)
    signal = functools.partial(pl.semaphore_signal, inc=1, device_id_type=MESH)

    barrier = pltpu.get_barrier_semaphore()
    if sz.line:
        pl.when(major > 0)(lambda: signal(barrier, device_id=(d - 2, t)))
        pl.when(major < sz.major - 1)(lambda: signal(barrier, device_id=(d + 2, t)))
        joined = jnp.where(middle, 2, 1) + 1 + sz.pairs
    else:
        for k in far_steps:
            signal(barrier, device_id=far(k))
        joined = sz.major + sz.pairs
    signal(barrier, device_id=near)
    for k in cross_steps:
        signal(barrier, device_id=(d, cross_rank(k)))
    signal(barrier, device_id=sibling)

    load_w = [pltpu.make_async_copy(weights_ref.at[l], w_in.at[l], local_sem.at[l]) for l in (0, 1)]
    load_frames = pltpu.make_async_copy(frames_ref, stage.at[0], local_sem.at[2])
    load_cot = pltpu.make_async_copy(cot_ref, stage.at[1], local_sem.at[3])
    load_biases = pltpu.make_async_copy(biases_ref, biases, local_sem.at[4])
    load_mask = pltpu.make_async_copy(mask_ref, mask, local_sem.at[5])
    for copy in (load_w[0], load_frames, load_w[1], load_cot, load_biases, load_mask):
        copy.start()

    def parts_of(l):
        return range(len(sz.parts[l]))

    def weight_block(l, slot, part):
        first, last = sz.parts[l][part]
        return w_all.at[l, slot, :, first:last]

    def weight_out(l, k, part):
        return same(weight_block(l, d, part), wz_send.at[l, k, part], wz_recv.at[l, k, part], far(k))

    def weight_relay(l, part):
        return same(weight_block(l, far_slot(2), part), wf_send.at[l, part], wz_recv.at[l, 3, part], far(1))

    def weight_over(l, k, part):
        return same(weight_block(l, far_slot(k), part), wy_send.at[l, k, part], wy_recv.at[l, k, part], near)

    def weights_over(l, k):
        for part in parts_of(l):
            weight_over(l, k, part).start()

    def weights_out(l):
        for k in sz.far_order:
            for part in parts_of(l):
                if sz.line and k == 3:
                    pl.when(middle)(weight_out(l, k, part).start)
                else:
                    weight_out(l, k, part).start()

    def weights_on(l, steps):
        for k in steps:
            for part in parts_of(l):
                block = weight_block(l, far_slot(k), part)
                same(block, wz_send.at[l, k, part], wz_recv.at[l, k, part], far(k)).wait_recv()
                if sz.line and k == 2:
                    pl.when(middle)(weight_relay(l, part).start)
                weight_over(l, k, part).start()

    def weights_here(l, part):
        for k in range(sz.major):
            block = weight_block(l, near_slot(k), part)
            same(block, wy_send.at[l, k, part], wy_recv.at[l, k, part], near).wait_recv()

    def weights_sent(l):
        for k in range(sz.major):
            for part in parts_of(l):
                weight_over(l, k, part).wait_send()
                if sz.line and k == 3:

                    @pl.when(middle)
                    def _():
                        weight_out(l, k, part).wait_send()
                        weight_relay(l, part).wait_send()

                elif k:
                    weight_out(l, k, part).wait_send()

    def round_weights(l):
        load_w[l].wait()
        for tap in range(TAPS):
            w_all[l, d, :, tap * sz.out : (tap + 1) * sz.out] = w_in[
                l, pl.ds(tap, sz.own_in, stride=TAPS), :
            ].astype(sz.wire)

    def gather_sends(g, maps, p, rows):
        own = maps.at[t, rows]
        out = [same(own, ax_send.at[g, p, k], ax_recv.at[g, p, k], (d, cross_rank(k))) for k in cross_steps]
        out.append(same(own, as_send.at[g, p], as_recv.at[g, p], sibling))
        return out

    def gather_forward(g, maps, p, rows, k):
        return same(maps.at[cross_from(k), rows], af_send.at[g, p, k], af_recv.at[g, p, k], sibling)

    def gather_pass_on(g, maps, p, rows):
        for k in cross_steps:
            same(maps.at[cross_from(k), rows], ax_send.at[g, p, k], ax_recv.at[g, p, k], sibling).wait_recv()
            gather_forward(g, maps, p, rows, k).start()

    def gather_here(g, maps, p, rows):
        same(maps.at[sibling[1], rows], as_send.at[g, p], as_recv.at[g, p], sibling).wait_recv()
        for k in cross_steps:
            rank = 2 * lax.rem(pair + sz.pairs - k, sz.pairs) + 1 - side
            same(maps.at[rank, rows], af_send.at[g, p, k], af_recv.at[g, p, k], sibling).wait_recv()

    def gather_sent(g, maps, p, rows):
        for copy in gather_sends(g, maps, p, rows):
            copy.wait_send()
        for k in cross_steps:
            gather_forward(g, maps, p, rows, k).wait_send()

    whole = pl.ds(0, sz.span)

    def product(l, part, maps, group):
        rows = slice(group[0] * sz.piece, group[1] * sz.piece)
        left = jnp.concatenate([maps[q, rows] for q in range(sz.tensor)], axis=1)
        first, last = sz.parts[l][part]
        for start in range(first, last, WIDE):
            stop = min(start + WIDE, last)
            right = w_all[l, :, :, start:stop].reshape(sz.chan, stop - start).astype(BF16)
            spread[sz.halo + rows.start : sz.halo + rows.stop, start:stop] = jnp.dot(
                left, right, preferred_element_type=F32
            )

    def own_bias(l):
        return biases[l : l + 1, pl.ds(pl.multiple_of(t * sz.out, sz.out), sz.out)]

    def shifted_sum(p):
        sums = []
        for b in range(3):
            total = None
            for a in range(3):
                shift = sz.items * (sz.width * (a - 1) + b - 1)
                tap = 3 * a + b
                rows = pl.ds(pl.multiple_of(p * sz.piece + sz.halo + shift, 8), sz.piece)
                term = spread[rows, tap * sz.out : (tap + 1) * sz.out]
                total = term if total is None else total + term
            sums.append(total)
        return sums[1] + sums[0] * edges[0, rows_of(p)] + sums[2] * edges[1, rows_of(p)]

    def note_delta(l, p, delta):
        bias_sum[l] += jnp.sum(delta.reshape(sz.piece // 8, 8, sz.out), axis=0)
        rows = pl.ds(pl.multiple_of(p * sz.piece + sz.halo, 8), sz.piece)
        shifted[0, rows] = delta * edges[0, rows_of(p)]
        shifted[1, rows] = delta
        shifted[2, rows] = delta * edges[1, rows_of(p)]

    def spread_delta(p):
        for a in range(3):
            for b in range(3):
                shift = sz.items * (sz.width * (a - 1) + b - 1)
                tap = 3 * a + b
                rows = pl.ds(pl.multiple_of(p * sz.piece + sz.halo - shift, 8), sz.piece)
                deltas[rows_of(p), tap * sz.out : (tap + 1) * sz.out] = shifted[b, rows].astype(BF16)

    def finish_four(first, last):
        @pl.loop(first, last)
        def _(p):
            act, slope = gelu_parts(shifted_sum(p) + own_bias(0))
            acts[t, rows_of(p)] = (act * edges[2, rows_of(p)]).astype(BF16)
            slope4[rows_of(p)] = slope * edges[2, rows_of(p)]
            for copy in gather_sends(1, acts, p, rows_of(p)):
                copy.start()

    def by_item(value):
        return (value.reshape(sz.piece // sz.items, sz.items, sz.out) * keep[...]).reshape(sz.piece, sz.out)

    def finish_five(first, last):
        @pl.loop(first, last)
        def _(p):
            act, slope = gelu_parts(shifted_sum(p) + own_bias(1))
            act5[rows_of(p)] = by_item(act).astype(BF16)
            delta = (by_item(cot[rows_of(p)].astype(F32)) * slope).astype(BF16).astype(F32)
            note_delta(1, p, delta)
            pl.when(p > 0)(lambda: spread_delta(p - 1))

    def part_copy(l, p):
        rows = rows_of(p)
        return remote(
            part_send.at[l, :, rows], part_recv.at[l, :, rows], rs_send.at[l, p], rs_recv.at[l, p], sibling
        )

    def cross_copy(l, p, k):
        rows = rows_of(p)
        return remote(
            cross_send.at[l, k, rows],
            cross_recv.at[l, k, rows],
            rx_send.at[l, p, k],
            rx_recv.at[l, p, k],
            (d, cross_rank(k)),
        )

    def back_product(l, group, which):
        blocks = [
            w_all[l, pl.ds((2 * j + which) * sz.slots, sz.slots)].reshape(sz.out, sz.cols) for j in range(sz.pairs)
        ]
        right = jnp.concatenate(blocks, axis=0).astype(BF16)
        left = deltas[group[0] * sz.piece : group[1] * sz.piece]
        out = lax.dot_general(left, right, (((1,), (1,)), ((), ())), preferred_element_type=F32)
        return [out[:, j * sz.out : (j + 1) * sz.out] for j in range(sz.pairs)]

    def back_to_sibling(l, group):
        rows = slice(group[0] * sz.piece, group[1] * sz.piece)
        for j, block in enumerate(back_product(l, group, 1 - side)):
            part_send[l, j, rows] = block.astype(BF16)
        for p in range(*group):
            part_copy(l, p).start()

    def back_own(l, group):
        rows = slice(group[0] * sz.piece, group[1] * sz.piece)
        for j, block in enumerate(back_product(l, group, side)):
            part_own[j, rows] = block

    def back_across(l, group):
        @pl.loop(*group)
        def _(p):
            part_copy(l, p).wait_recv()
            for k in cross_steps:
                j = lax.rem(pair + k, sz.pairs)
                total = part_own[j, rows_of(p)] + part_recv[l, j, rows_of(p)].astype(F32)
                cross_send[l, k, rows_of(p)] = total.astype(BF16)
                cross_copy(l, p, k).start()

    def back_products(l, first=None, between=None, second=None):
        nothing_else = lambda: None
        for group, meanwhile, then in zip(sz.groups, (first, second), (between, None)):
            back_to_sibling(l, group)
            (meanwhile or nothing_else)()
            back_own(l, group)
            back_across(l, group)
            (then or nothing_else)()

    def back_total(l, p):
        total = part_own[pair, rows_of(p)] + part_recv[l, pair, rows_of(p)].astype(F32)
        for k in cross_steps:
            cross_copy(l, p, k).wait_recv()
            total += cross_recv[l, k, rows_of(p)].astype(F32)
        return total

    shares = range(sz.shares)

    def share_of(h):
        return slice(h * sz.share, (h + 1) * sz.share)

    def near_copy(l, k, h):
        return remote(
            near_send.at[l, k, share_of(h)],
            near_recv.at[l, k, share_of(h)],
            gy_send.at[l, k, h],
            gy_recv.at[l, k, h],
            near,
        )

    def far_copy(l, k, h):
        return remote(
            far_send.at[l, k, share_of(h)],
            far_recv.at[l, k, share_of(h)],
            gz_send.at[l, k, h],
            gz_recv.at[l, k, h],
            far(k),
        )

    half = sz.tensor // 2
    far_half = [k for k in reversed(far_steps) if k >= sz.major // 2]
    near_half = [k for k in far_steps if k < sz.major // 2]

    def grads_product(l, maps, block, width, first, last):
        rows = slice(first * sz.piece, last * sz.piece)
        left = jnp.concatenate([maps[block + q, rows] for q in range(width)], axis=1)
        into = pl.ds(block * sz.slots, width * sz.slots)
        for start in range(0, sz.cols, WIDE):
            stop = min(start + WIDE, sz.cols)
            product = lax.dot_general(
                left, deltas[rows, start:stop], (((0,), (0,)), ((), ())), preferred_element_type=F32
            ).reshape(width * sz.slots, sz.own_in, stop - start)
            if first:
                product += kgrad[l, into, :, start:stop]
            kgrad[l, into, :, start:stop] = product

    def grads_block(l, maps, block, width, steps, first=0):
        grads_product(l, maps, block, width, first, sz.pieces)
        for k in steps:
            near_send[l, k] = kgrad[l, near_slot(k)].astype(sz.wire)
            for h in shares:
                near_copy(l, k, h).start()

    own_half = lax.div(major, sz.major // 2)

    def grads_half(l, maps, other):
        first = (1 - own_half if other else own_half) * half
        grads_block(l, maps, first, half, far_half if other else [*near_half, 0])

    def grads_place(l, maps, k, first=0):
        grads_block(l, maps, flip_bits(major, k), 1, [k], first)

    def relay_copy(l, h):
        rows = share_of(h)
        return remote(
            far_send.at[l, 3, rows], relay_recv.at[l, rows], gz_send.at[l, 3, h], gr_recv.at[l, h], far(1)
        )

    def grads_far(l, k, some=shares):
        for h in some:
            rows = share_of(h)
            near_copy(l, k, h).wait_recv()
            total = kgrad[l, far_slot(k), rows] + near_recv[l, k, rows].astype(F32)
            if sz.line and k == 2:

                @pl.when(middle)
                def _():
                    relay_copy(l, h).wait_recv()
                    far_send[l, k, rows] = (total + relay_recv[l, rows].astype(F32)).astype(sz.wire)

                @pl.when(jnp.logical_not(middle))
                def _():
                    far_send[l, k, rows] = total.astype(sz.wire)

            else:
                far_send[l, k, rows] = total.astype(sz.wire)
            if sz.line and k == 3:
                pl.when(middle)(far_copy(l, k, h).start)
                pl.when(jnp.logical_not(middle))(relay_copy(l, h).start)
            else:
                far_copy(l, k, h).start()

    def grads_sum(l):
        for h in shares:
            near_copy(l, 0, h).wait_recv()
            for k in far_steps:
                if sz.line and k == 3:
                    pl.when(middle)(far_copy(l, k, h).wait_recv)
                else:
                    far_copy(l, k, h).wait_recv()
        total = kgrad[l, d] + near_recv[l, 0].astype(F32)
        for k in far_steps:
            total += far_recv[l, k].astype(F32)
        shard[...] = total
        squares = jnp.sum((total * total).reshape(sz.own_in // 8, 8, sz.cols), axis=0)
        return sum(squares[:, tap * sz.out : (tap + 1) * sz.out] for tap in range(TAPS))

    def grads_out_rows(l):
        for tap in range(TAPS):
            grads_out[l, pl.ds(tap, sz.own_in, stride=TAPS), :] = shard[:, tap * sz.out : (tap + 1) * sz.out]

    round_weights(0)
    pl.semaphore_wait(barrier, joined)
    if sz.line:

        @pl.when(middle)
        def _():
            signal(ready, device_id=(d - 2, t))
            signal(ready, device_id=(d + 2, t))

    weights_over(0, 0)
    tail = sz.span - 16
    frames[t, tail:] = jnp.zeros((16, sz.out), BF16)
    load_frames.wait()
    frames[t, 0 : sz.real] = stage[0]
    for copy in gather_sends(0, frames, 0, whole):
        copy.start()
    round_weights(1)
    weights_over(1, 0)
    if sz.line:
        pl.semaphore_wait(ready, 1)
    weights_out(0)

    rest = sz.halo + sz.span
    for first in (0, rest):
        spread[first : first + sz.halo, :] = jnp.zeros((sz.halo, sz.cols), F32)
        shifted[:, first : first + sz.halo, :] = jnp.zeros((3, sz.halo, sz.out), F32)
    edges[...] = jnp.ones_like(edges)
    nothing = jnp.zeros((sz.items, sz.out), F32)
    for i in range(sz.height):
        for e, j in ((0, 0), (1, sz.width - 1)):
            first = (i * sz.width + j) * sz.items
            edges[e, first : first + sz.items, :] = nothing
    edges[2, sz.real :, :] = jnp.zeros((sz.span - sz.real, sz.out), F32)
    bias_sum[...] = jnp.zeros_like(bias_sum)
    if sz.line:

        @pl.when(jnp.logical_not(middle))
        def _():
            far_recv[:, 3] = jnp.zeros((2, sz.own_in, sz.cols), sz.wire)


    cot[tail:] = jnp.zeros((16, sz.out), BF16)
    load_cot.wait()
    cot[0 : sz.real] = stage[1]
    load_biases.wait()
    load_mask.wait()
    item = lax.broadcasted_iota(jnp.int32, (sz.items, sz.out), 0)
    kept = jnp.zeros((sz.items, sz.out), F32)
    for n in range(sz.items):
        kept = jnp.where(item == n, mask[n].astype(F32), kept)
    keep[...] = kept

    one, two = sz.groups
    weights_on(0, far_steps)
    weights_out(1)
    gather_pass_on(0, frames, 0, whole)
    gather_here(0, frames, 0, whole)
    weights_here(0, 0)
    product(0, 0, frames, one)
    product(0, 0, frames, two)
    weights_on(1, far_steps[:1])
    weights_here(0, 1)
    product(0, 1, frames, one)
    finish_four(0, one[1] - 1)
    weights_on(1, far_steps[1:2])
    product(0, 1, frames, two)
    finish_four(one[1] - 1, sz.pieces)

    weights_on(1, far_steps[2:])
    act4_out[...] = acts[t, 0 : sz.real]
    for p in all_pieces:
        gather_pass_on(1, acts, p, rows_of(p))
    for p in range(*one):
        gather_here(1, acts, p, rows_of(p))
    weights_here(1, 0)
    product(1, 0, acts, one)
    weights_here(1, 1)
    product(1, 1, acts, one)
    for p in range(*two):
        gather_here(1, acts, p, rows_of(p))
    finish_five(0, one[1] - 1)
    product(1, 0, acts, two)
    product(1, 1, acts, two)
    finish_five(one[1] - 1, sz.pieces)
    spread_delta(sz.pieces - 1)
    if sz.line and sz.tensor == sz.major:
        back_products(1, lambda: grads_place(1, acts, 3), second=lambda: grads_place(1, acts, 2))
    else:
        grads_half(1, acts, True)
        back_products(1)
    grads_far(1, far_half[0], shares[:1])
    grads_half(1, acts, False)
    grads_far(1, far_half[0], shares[1:])

    def delta_four(first, last):
        @pl.loop(first, last)
        def _(p):
            note_delta(0, p, (back_total(1, p) * slope4[rows_of(p)]).astype(BF16).astype(F32))
            pl.when(p > 0)(lambda: spread_delta(p - 1))

    if sz.line and sz.tensor == sz.major and sz.pieces > 2:
        early = sz.pieces - 2
        delta_four(0, sz.pieces - 1)
        grads_far(1, 2)
        for k in (3, 2):
            grads_product(0, frames, flip_bits(major, k), 1, 0, early)
        delta_four(sz.pieces - 1, sz.pieces)
        spread_delta(sz.pieces - 1)
        grads_place(0, frames, 3, early)
        grads_place(0, frames, 2, early if 2 in (3, 2) else 0)
    else:
        delta_four(0, sz.pieces)
        spread_delta(sz.pieces - 1)
        grads_half(0, frames, True)
        for k in far_half[1:]:
            grads_far(1, k)
    for k in near_half:
        grads_far(1, k)
    grads_half(0, frames, False)
    back_products(
        0,
        between=lambda: grads_far(0, far_half[0], shares[:1]),
        second=lambda: grads_far(0, far_half[0], shares[1:]),
    )
    for k in (*far_half[1:], *near_half):
        grads_far(0, k)
    act5_out[...] = act5[0 : sz.real]
    squares = grads_sum(1)
    grads_out_rows(1)

    @pl.loop(0, sz.pieces)
    def _(p):
        igrad[rows_of(p)] = back_total(0, p)

    igrad_out[...] = igrad[0 : sz.real]

    me = d * sz.tensor + t
    for l in (0, 1):
        stats_all[me, l + 1 : l + 2, :] = jnp.sum(bias_sum[l], axis=0, keepdims=True)
    squares += grads_sum(0)
    stats_all[me, 0:1, :] = jnp.sum(squares, axis=0, keepdims=True)
    def stats_copy(a, b, mine):
        device = (flip_bits(d, a), flip_bits(t, b))
        slot = me if mine else device[0] * sz.tensor + device[1]
        k = a * sz.tensor + b
        return same(stats_all.at[slot, 0:3], st_send.at[k], st_recv.at[k], device)

    others = [(a, b) for a in reversed(range(sz.dp)) for b in reversed(range(sz.tensor)) if a or b]
    for a, b in others:
        stats_copy(a, b, True).start()

    grads_out_rows(0)
    for l in (0, 1):
        weights_sent(l)
        for h in shares:
            for k in far_steps:
                far_copy(l, k, h).wait_send()
            for k in range(sz.major):
                near_copy(l, k, h).wait_send()

        @pl.loop(0, sz.pieces)
        def _(p):
            part_copy(l, p).wait_send()
            for k in cross_steps:
                cross_copy(l, p, k).wait_send()

    gather_sent(0, frames, 0, whole)

    @pl.loop(0, sz.pieces)
    def _(p):
        gather_sent(1, acts, p, rows_of(p))

    for a, b in others:
        stats_copy(a, b, False).wait_recv()

    for q in range(sz.tensor):
        total = stats_all[q, 0:3]
        for slot in range(q + sz.tensor, sz.devices, sz.tensor):
            total += stats_all[slot, 0:3]
        stats_out[q, 0:3] = total

    for a, b in others:
        stats_copy(a, b, True).wait_send()


def train_step(sz, frames, item_mask, weights, biases, cotangent):
    sem = pltpu.SemaphoreType.DMA
    vmem = pltpu.VMEM
    maps = (sz.span, sz.out)
    block = (sz.own_in, sz.cols)
    shapes = [
        vmem((2, sz.rows, sz.out), F32),
        vmem((2, sz.real, sz.out), BF16),
        vmem(maps, BF16),
        vmem((2, sz.chan), F32),
        pltpu.SMEM((sz.items,), jnp.int32),
        vmem((sz.items, sz.out), F32),
        vmem((2, sz.dp, *block), sz.wire),
        vmem((sz.tensor, *maps), BF16),
        vmem((sz.tensor, *maps), BF16),
        vmem((sz.span + 2 * sz.halo, sz.cols), F32),
        vmem((3, *maps), F32),
        vmem(maps, F32),
        vmem(maps, BF16),
        vmem((3, sz.span + 2 * sz.halo, sz.out), F32),
        vmem((sz.span, sz.cols), BF16),
        vmem((2, sz.pairs, *maps), BF16),
        vmem((2, sz.pairs, *maps), BF16),
        vmem((sz.pairs, *maps), F32),
        vmem((2, sz.pairs, *maps), BF16),
        vmem((2, sz.pairs, *maps), BF16),
        vmem(maps, F32),
        vmem((2, sz.dp, *block), F32),
        vmem((2, sz.major, *block), sz.wire),
        vmem((2, sz.major, *block), sz.wire),
        vmem((2, sz.major, *block), sz.wire),
        vmem((2, sz.major, *block), sz.wire),
        vmem((2, *block), sz.wire),
        vmem(block, F32),
        vmem((2, 8, sz.out), F32),
        vmem((sz.devices, 8, sz.out), F32),
        sem((6,)),
        pltpu.SemaphoreType.REGULAR,
        sem((2, sz.major, 2)),
        sem((2, sz.major, 2)),
        sem((2, 2)),
        sem((2, sz.major, 2)),
        sem((2, sz.major, 2)),
        sem((2, sz.pieces, sz.pairs)),
        sem((2, sz.pieces, sz.pairs)),
        sem((2, sz.pieces)),
        sem((2, sz.pieces)),
        sem((2, sz.pieces, sz.pairs)),
        sem((2, sz.pieces, sz.pairs)),
        sem((2, sz.pieces)),
        sem((2, sz.pieces)),
        sem((2, sz.pieces, sz.pairs)),
        sem((2, sz.pieces, sz.pairs)),
        sem((2, sz.major, sz.shares)),
        sem((2, sz.major, sz.shares)),
        sem((2, sz.major, sz.shares)),
        sem((2, sz.major, sz.shares)),
        sem((2, sz.shares)),
        sem((sz.devices,)),
        sem((sz.devices,)),
    ]
    macs = 6 * sz.real * TAPS * sz.chan * sz.out
    rows = (sz.real, sz.out)
    return pl.pallas_call(
        functools.partial(body, sz),
        out_shape=[
            vmem(rows, BF16),
            vmem(rows, BF16),
            vmem(rows, F32),
            vmem((2, sz.rows, sz.out), F32),
            vmem((sz.tensor, 8, sz.out), F32),
        ],
        in_specs=[pl.BlockSpec(memory_space=pltpu.HBM)] * 5,
        out_specs=[pl.BlockSpec(memory_space=vmem)] * 5,
        scratch_shapes=shapes,
        compiler_params=pltpu.CompilerParams(
            collective_id=0, has_side_effects=True, vmem_limit_bytes=sz.grant
        ),
        cost_estimate=pl.CostEstimate(flops=2 * macs, bytes_accessed=6_000_000, transcendentals=0),
        name="train_step",
    )(*(pltpu.with_memory_space_constraint(x, pltpu.HBM) for x in (frames, item_mask, weights, biases, cotangent)))


def finish_body(
    sz,
    act4,
    act5,
    igrad,
    grads,
    stats,
    weights,
    first,
    second,
    biases_ref,
    bias_first_ref,
    bias_second_ref,
    act4_out,
    act5_out,
    igrad_out,
    norm_out,
    weights_out,
    first_out,
    second_out,
    biases_out,
    bias_first_out,
    bias_second_out,
    olds,
    news,
    in_sem,
    out_sem,
    move_sem,
):
    targets = (weights_out, first_out, second_out)
    parts = [(l, pl.ds(r * sz.rows // 2, sz.rows // 2)) for l in (0, 1) for r in (0, 1)]
    if sz.rows % 16:
        parts = [(l, pl.ds(0, sz.rows)) for l in (0, 1)]
    stores = [
        [pltpu.make_async_copy(news.at[l, i, r], ref.at[l, r], out_sem.at[p, i]) for i, ref in enumerate(targets)]
        for p, (l, r) in enumerate(parts)
    ]
    moves = [
        pltpu.make_async_copy(held, ref, move_sem.at[i])
        for i, (held, ref) in enumerate(((act4, act4_out), (act5, act5_out), (igrad, igrad_out)))
    ]
    loads = [
        pltpu.make_async_copy(ref, olds.at[i], in_sem.at[i])
        for i, ref in enumerate((biases_ref, bias_first_ref, bias_second_ref))
    ]
    for copy in (*loads, *moves):
        copy.start()
    bias_grad = jnp.concatenate([stats[q, 1:3, :] for q in range(sz.tensor)], axis=1)
    squares = jnp.sum(stats[:, 0, :], axis=(0, 1), keepdims=True) + jnp.sum(
        bias_grad * bias_grad, axis=(0, 1), keepdims=True
    )
    grad_norm = jnp.sqrt(squares)
    factor = jnp.minimum(1.0, CLIP_NORM / (grad_norm + 1e-06))
    norm_out[...] = grad_norm
    for p, (l, r) in enumerate(parts):
        news[l, 0, r], news[l, 1, r], news[l, 2, r] = adam_update(
            weights[l, r], grads[l, r] * factor, first[l, r], second[l, r], RATE, DECAY
        )
        for copy in stores[p]:
            copy.start()
    for copy in loads:
        copy.wait()
    biases_out[...], bias_first_out[...], bias_second_out[...] = adam_update(
        olds[0], bias_grad * factor, olds[1], olds[2], BIAS_RATE, 0.0
    )
    for copy in (*moves, *(copy for part in stores for copy in part)):
        copy.wait()


def finish(sz, act4, act5, igrad, grads, stats, weights, first, second, biases, bias_first, bias_second):
    inside = pl.BlockSpec(memory_space=pltpu.VMEM)
    outside = pl.BlockSpec(memory_space=pltpu.HBM)
    like = lambda x: jax.ShapeDtypeStruct(x.shape, x.dtype)
    sem = pltpu.SemaphoreType.DMA
    held = [pltpu.with_memory_space_constraint(x, pltpu.VMEM) for x in (act4, act5, igrad, grads, stats, weights, first, second)]
    given = [pltpu.with_memory_space_constraint(x, pltpu.HBM) for x in (biases, bias_first, bias_second)]
    return pl.pallas_call(
        functools.partial(finish_body, sz),
        out_shape=[
            like(act4),
            like(act5),
            like(igrad),
            jax.ShapeDtypeStruct((1, 1), F32),
            like(weights),
            like(first),
            like(second),
            like(biases),
            like(bias_first),
            like(bias_second),
        ],
        in_specs=[inside] * 8 + [outside] * 3,
        out_specs=[outside] * 3 + [inside] + [outside] * 3 + [inside] * 3,
        scratch_shapes=[
            pltpu.VMEM((3, *biases.shape), F32),
            pltpu.VMEM((2, 3, sz.rows, sz.out), F32),
            sem((3,)),
            sem((4, 3)),
            sem((3,)),
        ],
        compiler_params=pltpu.CompilerParams(vmem_limit_bytes=8 * 1024 * 1024),
        cost_estimate=pl.CostEstimate(flops=5_000_000, bytes_accessed=7_000_000, transcendentals=0),
        name="clip_and_adamw",
    )(*held, *given)


def on_device(
    mesh,
    frames,
    item_mask,
    weights,
    biases,
    cotangent,
    weight_first,
    weight_second,
    bias_first,
    bias_second,
):
    sz = Sizes(mesh, frames.shape, weights.shape)

    def flat(maps):
        return jnp.transpose(maps, (1, 2, 0, 3)).reshape(sz.real, sz.out)

    def square(rows):
        return jnp.transpose(rows.reshape(sz.height, sz.width, sz.items, sz.out), (2, 0, 1, 3))

    made = train_step(sz, flat(frames), item_mask, weights, biases, flat(cotangent))
    act_four, act_five, input_grad, grad_norm, *rest = finish(
        sz, *made, weights, weight_first, weight_second, biases, bias_first, bias_second
    )
    return (square(act_four), square(act_five), square(input_grad), grad_norm.reshape(()), *rest)


def solution(mesh):
    split = P("dp", None, None, "tensor")
    rows = P(None, "dp", "tensor")
    in_specs = (split, P("dp"), rows, P(), split, rows, rows, P(), P())
    out_specs = (split, split, split, P(), rows, rows, rows, P(), P(), P())
    return jax.shard_map(
        functools.partial(on_device, mesh), mesh=mesh, in_specs=in_specs, out_specs=out_specs, check_vma=False
    )
```

```python
import functools
import math

import jax
import jax.numpy as jnp
from jax import lax
from jax.experimental import pallas as pl
from jax.experimental.pallas import tpu as pltpu
from jax.sharding import PartitionSpec as P

STEP = 5
CLIP_NORM = 1.0
BETA_ONE = 0.5
BETA_TWO = 0.5
RATE = 0.01
BIAS_RATE = 0.03
DECAY = 0.1
EPSILON = 1e-08

MESH = pl.DeviceIdType.MESH
BF16 = jnp.bfloat16
F32 = jnp.float32
ROOT = math.sqrt(2.0 / math.pi)
CUBE = 0.044715
TAPS = 9
WIDE = 256


def gelu_parts(value):
    square = value * value
    th = jnp.tanh(ROOT * value * (1.0 + CUBE * square))
    half = 0.5 * (1.0 + th)
    slope = half + 0.5 * value * (1.0 - th * th) * (ROOT * (1.0 + 3.0 * CUBE * square))
    return value * half, slope


def flip_bits(index, mask):
    bit = 1
    while bit <= mask:
        if mask & bit:
            index = index + bit - 2 * bit * lax.rem(lax.div(index, bit), 2)
        bit *= 2
    return index


def adam_update(param, grad, first, second, rate, decay):
    first_new = BETA_ONE * first + (1.0 - BETA_ONE) * grad
    second_new = BETA_TWO * second + (1.0 - BETA_TWO) * grad * grad
    corrected = first_new * (1.0 / (1.0 - BETA_ONE**STEP))
    scaled = jnp.sqrt(second_new * (1.0 / (1.0 - BETA_TWO**STEP))) + EPSILON
    return (param - rate * (corrected / scaled + decay * param), first_new, second_new)


class Sizes:
    def __init__(self, mesh, frames_shape, weights_shape):
        self.dp = mesh.shape["dp"]
        self.tensor = mesh.shape["tensor"]
        self.items, self.height, self.width, self.out = frames_shape
        self.chan = self.out * self.tensor
        self.rows = weights_shape[1]
        self.own_in = self.rows // TAPS
        self.cols = TAPS * self.out
        self.major = self.dp // 2
        self.pairs = self.tensor // 2
        self.slots = self.dp // self.tensor
        self.spots = self.height * self.width
        self.real = self.spots * self.items
        self.span = -(-self.real // 16) * 16
        self.halo = (self.width + 1) * self.items
        self.pieces = next(n for n in (5, 4, 3, 2, 1) if self.span // 16 % n == 0)
        self.piece = self.span // self.pieces
        self.groups = ((0, self.pieces // 2), (self.pieces // 2, self.pieces))
        self.wire = BF16 if self.own_in % 16 == 0 else F32
        self.line = self.major == 4
        self.far_order = (2, 1, 3) if self.line else tuple(range(1, self.major))
        cut = (TAPS + 1) // 2 * self.out
        self.parts = (((0, cut), (cut, self.cols)),) * 2
        self.devices = self.dp * self.tensor
        self.shares = 2 if self.own_in % 32 == 0 else 1
        self.share = self.own_in // self.shares
        self.grant = (44 if self.wire == BF16 else 54) * 1024 * 1024


def body(
    sz,
    frames_ref,
    mask_ref,
    weights_ref,
    biases_ref,
    cot_ref,
    act4_out,
    act5_out,
    igrad_out,
    grads_out,
    stats_out,
    w_in,
    stage,
    cot,
    biases,
    mask,
    keep,
    w_all,
    frames,
    acts,
    spread,
    edges,
    slope4,
    act5,
    shifted,
    deltas,
    part_send,
    part_recv,
    part_own,
    cross_send,
    cross_recv,
    igrad,
    kgrad,
    near_send,
    near_recv,
    far_send,
    far_recv,
    relay_recv,
    shard,
    bias_sum,
    stats_all,
    local_sem,
    ready,
    wz_send,
    wz_recv,
    wf_send,
    wy_send,
    wy_recv,
    ax_send,
    ax_recv,
    as_send,
    as_recv,
    af_send,
    af_recv,
    rs_send,
    rs_recv,
    rx_send,
    rx_recv,
    gy_send,
    gy_recv,
    gz_send,
    gz_recv,
    gr_recv,
    st_send,
    st_recv,
):
    d = lax.axis_index("dp")
    t = lax.axis_index("tensor")
    major, minor = lax.div(d, 2), lax.rem(d, 2)
    near = (2 * major + 1 - minor, t)
    pair, side = lax.div(t, 2), lax.rem(t, 2)
    sibling = (d, 2 * pair + 1 - side)

    def far_slot(k):
        return 2 * flip_bits(major, k) + minor

    def near_slot(k):
        return 2 * flip_bits(major, k) + 1 - minor

    def far(k):
        return (far_slot(k), t)

    def cross_rank(k):
        return 2 * lax.rem(pair + k, sz.pairs) + side

    def cross_from(k):
        return 2 * lax.rem(pair + sz.pairs - k, sz.pairs) + side

    def remote(src, dst, send, recv, device):
        return pltpu.make_async_remote_copy(
            src_ref=src, dst_ref=dst, send_sem=send, recv_sem=recv, device_id=device, device_id_type=MESH
        )

    def same(block, send, recv, device):
        return remote(block, block, send, recv, device)

    all_pieces = range(sz.pieces)

    def rows_of(p):
        return pl.ds(pl.multiple_of(p * sz.piece, 16), sz.piece)

    far_steps = range(1, sz.major)
    cross_steps = range(1, sz.pairs)
    middle = jnp.logical_and(major > 0, major < sz.major - 1)
    far_steps = range(1, sz.major)
    cross_steps = range(1, sz.pairs)
    signal = functools.partial(pl.semaphore_signal, inc=1, device_id_type=MESH)

    barrier = pltpu.get_barrier_semaphore()
    if sz.line:
        pl.when(major > 0)(lambda: signal(barrier, device_id=(d - 2, t)))
        pl.when(major < sz.major - 1)(lambda: signal(barrier, device_id=(d + 2, t)))
        joined = jnp.where(middle, 2, 1) + 1 + sz.pairs
    else:
        for k in far_steps:
            signal(barrier, device_id=far(k))
        joined = sz.major + sz.pairs
    signal(barrier, device_id=near)
    for k in cross_steps:
        signal(barrier, device_id=(d, cross_rank(k)))
    signal(barrier, device_id=sibling)

    load_w = [pltpu.make_async_copy(weights_ref.at[l], w_in.at[l], local_sem.at[l]) for l in (0, 1)]
    load_frames = pltpu.make_async_copy(frames_ref, stage.at[0], local_sem.at[2])
    load_cot = pltpu.make_async_copy(cot_ref, stage.at[1], local_sem.at[3])
    load_biases = pltpu.make_async_copy(biases_ref, biases, local_sem.at[4])
    load_mask = pltpu.make_async_copy(mask_ref, mask, local_sem.at[5])
    for copy in (load_w[0], load_frames, load_w[1], load_cot, load_biases, load_mask):
        copy.start()

    def parts_of(l):
        return range(len(sz.parts[l]))

    def weight_block(l, slot, part):
        first, last = sz.parts[l][part]
        return w_all.at[l, slot, :, first:last]

    def weight_out(l, k, part):
        return same(weight_block(l, d, part), wz_send.at[l, k, part], wz_recv.at[l, k, part], far(k))

    def weight_relay(l, part):
        return same(weight_block(l, far_slot(2), part), wf_send.at[l, part], wz_recv.at[l, 3, part], far(1))

    def weight_over(l, k, part):
        return same(weight_block(l, far_slot(k), part), wy_send.at[l, k, part], wy_recv.at[l, k, part], near)

    def weights_over(l, k):
        for part in parts_of(l):
            weight_over(l, k, part).start()

    def weights_out(l):
        for k in sz.far_order:
            for part in parts_of(l):
                if sz.line and k == 3:
                    pl.when(middle)(weight_out(l, k, part).start)
                else:
                    weight_out(l, k, part).start()

    def weights_on(l, steps):
        for k in steps:
            for part in parts_of(l):
                block = weight_block(l, far_slot(k), part)
                same(block, wz_send.at[l, k, part], wz_recv.at[l, k, part], far(k)).wait_recv()
                if sz.line and k == 2:
                    pl.when(middle)(weight_relay(l, part).start)
                weight_over(l, k, part).start()

    def weights_here(l, part):
        for k in range(sz.major):
            block = weight_block(l, near_slot(k), part)
            same(block, wy_send.at[l, k, part], wy_recv.at[l, k, part], near).wait_recv()

    def weights_sent(l):
        for k in range(sz.major):
            for part in parts_of(l):
                weight_over(l, k, part).wait_send()
                if sz.line and k == 3:

                    @pl.when(middle)
                    def _():
                        weight_out(l, k, part).wait_send()
                        weight_relay(l, part).wait_send()

                elif k:
                    weight_out(l, k, part).wait_send()

    def round_weights(l):
        load_w[l].wait()
        for tap in range(TAPS):
            w_all[l, d, :, tap * sz.out : (tap + 1) * sz.out] = w_in[
                l, pl.ds(tap, sz.own_in, stride=TAPS), :
            ].astype(sz.wire)

    def gather_sends(g, maps, p, rows):
        own = maps.at[t, rows]
        out = [same(own, ax_send.at[g, p, k], ax_recv.at[g, p, k], (d, cross_rank(k))) for k in cross_steps]
        out.append(same(own, as_send.at[g, p], as_recv.at[g, p], sibling))
        return out

    def gather_forward(g, maps, p, rows, k):
        return same(maps.at[cross_from(k), rows], af_send.at[g, p, k], af_recv.at[g, p, k], sibling)

    def gather_pass_on(g, maps, p, rows):
        for k in cross_steps:
            same(maps.at[cross_from(k), rows], ax_send.at[g, p, k], ax_recv.at[g, p, k], sibling).wait_recv()
            gather_forward(g, maps, p, rows, k).start()

    def gather_here(g, maps, p, rows):
        same(maps.at[sibling[1], rows], as_send.at[g, p], as_recv.at[g, p], sibling).wait_recv()
        for k in cross_steps:
            rank = 2 * lax.rem(pair + sz.pairs - k, sz.pairs) + 1 - side
            same(maps.at[rank, rows], af_send.at[g, p, k], af_recv.at[g, p, k], sibling).wait_recv()

    def gather_sent(g, maps, p, rows):
        for copy in gather_sends(g, maps, p, rows):
            copy.wait_send()
        for k in cross_steps:
            gather_forward(g, maps, p, rows, k).wait_send()

    whole = pl.ds(0, sz.span)

    def product(l, part, maps, group):
        rows = slice(group[0] * sz.piece, group[1] * sz.piece)
        left = jnp.concatenate([maps[q, rows] for q in range(sz.tensor)], axis=1)
        first, last = sz.parts[l][part]
        for start in range(first, last, WIDE):
            stop = min(start + WIDE, last)
            right = w_all[l, :, :, start:stop].reshape(sz.chan, stop - start).astype(BF16)
            spread[sz.halo + rows.start : sz.halo + rows.stop, start:stop] = jnp.dot(
                left, right, preferred_element_type=F32
            )

    def own_bias(l):
        return biases[l : l + 1, pl.ds(pl.multiple_of(t * sz.out, sz.out), sz.out)]

    def shifted_sum(p):
        sums = []
        for b in range(3):
            total = None
            for a in range(3):
                shift = sz.items * (sz.width * (a - 1) + b - 1)
                tap = 3 * a + b
                rows = pl.ds(pl.multiple_of(p * sz.piece + sz.halo + shift, 8), sz.piece)
                term = spread[rows, tap * sz.out : (tap + 1) * sz.out]
                total = term if total is None else total + term
            sums.append(total)
        return sums[1] + sums[0] * edges[0, rows_of(p)] + sums[2] * edges[1, rows_of(p)]

    def note_delta(l, p, delta):
        bias_sum[l] += jnp.sum(delta.reshape(sz.piece // 8, 8, sz.out), axis=0)
        rows = pl.ds(pl.multiple_of(p * sz.piece + sz.halo, 8), sz.piece)
        shifted[0, rows] = delta * edges[0, rows_of(p)]
        shifted[1, rows] = delta
        shifted[2, rows] = delta * edges[1, rows_of(p)]

    def spread_delta(p):
        for a in range(3):
            for b in range(3):
                shift = sz.items * (sz.width * (a - 1) + b - 1)
                tap = 3 * a + b
                rows = pl.ds(pl.multiple_of(p * sz.piece + sz.halo - shift, 8), sz.piece)
                deltas[rows_of(p), tap * sz.out : (tap + 1) * sz.out] = shifted[b, rows].astype(BF16)

    def finish_four(first, last):
        @pl.loop(first, last)
        def _(p):
            act, slope = gelu_parts(shifted_sum(p) + own_bias(0))
            acts[t, rows_of(p)] = (act * edges[2, rows_of(p)]).astype(BF16)
            slope4[rows_of(p)] = slope * edges[2, rows_of(p)]
            for copy in gather_sends(1, acts, p, rows_of(p)):
                copy.start()

    def by_item(value):
        return (value.reshape(sz.piece // sz.items, sz.items, sz.out) * keep[...]).reshape(sz.piece, sz.out)

    def finish_five(first, last):
        @pl.loop(first, last)
        def _(p):
            act, slope = gelu_parts(shifted_sum(p) + own_bias(1))
            act5[rows_of(p)] = by_item(act).astype(BF16)
            delta = (by_item(cot[rows_of(p)].astype(F32)) * slope).astype(BF16).astype(F32)
            note_delta(1, p, delta)
            pl.when(p > 0)(lambda: spread_delta(p - 1))

    def part_copy(l, p):
        rows = rows_of(p)
        return remote(
            part_send.at[l, :, rows], part_recv.at[l, :, rows], rs_send.at[l, p], rs_recv.at[l, p], sibling
        )

    def cross_copy(l, p, k):
        rows = rows_of(p)
        return remote(
            cross_send.at[l, k, rows],
            cross_recv.at[l, k, rows],
            rx_send.at[l, p, k],
            rx_recv.at[l, p, k],
            (d, cross_rank(k)),
        )

    def back_product(l, group, which):
        blocks = [
            w_all[l, pl.ds((2 * j + which) * sz.slots, sz.slots)].reshape(sz.out, sz.cols) for j in range(sz.pairs)
        ]
        right = jnp.concatenate(blocks, axis=0).astype(BF16)
        left = deltas[group[0] * sz.piece : group[1] * sz.piece]
        out = lax.dot_general(left, right, (((1,), (1,)), ((), ())), preferred_element_type=F32)
        return [out[:, j * sz.out : (j + 1) * sz.out] for j in range(sz.pairs)]

    def back_to_sibling(l, group):
        rows = slice(group[0] * sz.piece, group[1] * sz.piece)
        for j, block in enumerate(back_product(l, group, 1 - side)):
            part_send[l, j, rows] = block.astype(BF16)
        for p in range(*group):
            part_copy(l, p).start()

    def back_own(l, group):
        rows = slice(group[0] * sz.piece, group[1] * sz.piece)
        for j, block in enumerate(back_product(l, group, side)):
            part_own[j, rows] = block

    def back_across(l, group):
        @pl.loop(*group)
        def _(p):
            part_copy(l, p).wait_recv()
            for k in cross_steps:
                j = lax.rem(pair + k, sz.pairs)
                total = part_own[j, rows_of(p)] + part_recv[l, j, rows_of(p)].astype(F32)
                cross_send[l, k, rows_of(p)] = total.astype(BF16)
                cross_copy(l, p, k).start()

    def back_products(l, first=None, between=None, second=None):
        nothing_else = lambda: None
        for group, meanwhile, then in zip(sz.groups, (first, second), (between, None)):
            back_to_sibling(l, group)
            (meanwhile or nothing_else)()
            back_own(l, group)
            back_across(l, group)
            (then or nothing_else)()

    def back_total(l, p):
        total = part_own[pair, rows_of(p)] + part_recv[l, pair, rows_of(p)].astype(F32)
        for k in cross_steps:
            cross_copy(l, p, k).wait_recv()
            total += cross_recv[l, k, rows_of(p)].astype(F32)
        return total

    shares = range(sz.shares)

    def share_of(h):
        return slice(h * sz.share, (h + 1) * sz.share)

    def near_copy(l, k, h):
        return remote(
            near_send.at[l, k, share_of(h)],
            near_recv.at[l, k, share_of(h)],
            gy_send.at[l, k, h],
            gy_recv.at[l, k, h],
            near,
        )

    def far_copy(l, k, h):
        return remote(
            far_send.at[l, k, share_of(h)],
            far_recv.at[l, k, share_of(h)],
            gz_send.at[l, k, h],
            gz_recv.at[l, k, h],
            far(k),
        )

    half = sz.tensor // 2
    far_half = [k for k in reversed(far_steps) if k >= sz.major // 2]
    near_half = [k for k in far_steps if k < sz.major // 2]

    def grads_product(l, maps, block, width, first, last):
        rows = slice(first * sz.piece, last * sz.piece)
        left = jnp.concatenate([maps[block + q, rows] for q in range(width)], axis=1)
        into = pl.ds(block * sz.slots, width * sz.slots)
        for start in range(0, sz.cols, WIDE):
            stop = min(start + WIDE, sz.cols)
            product = lax.dot_general(
                left, deltas[rows, start:stop], (((0,), (0,)), ((), ())), preferred_element_type=F32
            ).reshape(width * sz.slots, sz.own_in, stop - start)
            if first:
                product += kgrad[l, into, :, start:stop]
            kgrad[l, into, :, start:stop] = product

    def grads_block(l, maps, block, width, steps, first=0):
        grads_product(l, maps, block, width, first, sz.pieces)
        for k in steps:
            near_send[l, k] = kgrad[l, near_slot(k)].astype(sz.wire)
            for h in shares:
                near_copy(l, k, h).start()

    own_half = lax.div(major, sz.major // 2)

    def grads_half(l, maps, other):
        first = (1 - own_half if other else own_half) * half
        grads_block(l, maps, first, half, far_half if other else [*near_half, 0])

    def grads_place(l, maps, k, first=0):
        grads_block(l, maps, flip_bits(major, k), 1, [k], first)

    def relay_copy(l, h):
        rows = share_of(h)
        return remote(
            far_send.at[l, 3, rows], relay_recv.at[l, rows], gz_send.at[l, 3, h], gr_recv.at[l, h], far(1)
        )

    def grads_far(l, k, some=shares):
        for h in some:
            rows = share_of(h)
            near_copy(l, k, h).wait_recv()
            total = kgrad[l, far_slot(k), rows] + near_recv[l, k, rows].astype(F32)
            if sz.line and k == 2:

                @pl.when(middle)
                def _():
                    relay_copy(l, h).wait_recv()
                    far_send[l, k, rows] = (total + relay_recv[l, rows].astype(F32)).astype(sz.wire)

                @pl.when(jnp.logical_not(middle))
                def _():
                    far_send[l, k, rows] = total.astype(sz.wire)

            else:
                far_send[l, k, rows] = total.astype(sz.wire)
            if sz.line and k == 3:
                pl.when(middle)(far_copy(l, k, h).start)
                pl.when(jnp.logical_not(middle))(relay_copy(l, h).start)
            else:
                far_copy(l, k, h).start()

    def grads_sum(l):
        for h in shares:
            near_copy(l, 0, h).wait_recv()
            for k in far_steps:
                if sz.line and k == 3:
                    pl.when(middle)(far_copy(l, k, h).wait_recv)
                else:
                    far_copy(l, k, h).wait_recv()
        total = kgrad[l, d] + near_recv[l, 0].astype(F32)
        for k in far_steps:
            total += far_recv[l, k].astype(F32)
        shard[...] = total
        squares = jnp.sum((total * total).reshape(sz.own_in // 8, 8, sz.cols), axis=0)
        return sum(squares[:, tap * sz.out : (tap + 1) * sz.out] for tap in range(TAPS))

    def grads_out_rows(l):
        for tap in range(TAPS):
            grads_out[l, pl.ds(tap, sz.own_in, stride=TAPS), :] = shard[:, tap * sz.out : (tap + 1) * sz.out]

    round_weights(0)
    pl.semaphore_wait(barrier, joined)
    if sz.line:

        @pl.when(middle)
        def _():
            signal(ready, device_id=(d - 2, t))
            signal(ready, device_id=(d + 2, t))

    weights_over(0, 0)
    tail = sz.span - 16
    frames[t, tail:] = jnp.zeros((16, sz.out), BF16)
    load_frames.wait()
    frames[t, 0 : sz.real] = stage[0]
    for copy in gather_sends(0, frames, 0, whole):
        copy.start()
    round_weights(1)
    weights_over(1, 0)
    if sz.line:
        pl.semaphore_wait(ready, 1)
    weights_out(0)

    rest = sz.halo + sz.span
    for first in (0, rest):
        spread[first : first + sz.halo, :] = jnp.zeros((sz.halo, sz.cols), F32)
        shifted[:, first : first + sz.halo, :] = jnp.zeros((3, sz.halo, sz.out), F32)
    edges[...] = jnp.ones_like(edges)
    nothing = jnp.zeros((sz.items, sz.out), F32)
    for i in range(sz.height):
        for e, j in ((0, 0), (1, sz.width - 1)):
            first = (i * sz.width + j) * sz.items
            edges[e, first : first + sz.items, :] = nothing
    edges[2, sz.real :, :] = jnp.zeros((sz.span - sz.real, sz.out), F32)
    bias_sum[...] = jnp.zeros_like(bias_sum)
    if sz.line:

        @pl.when(jnp.logical_not(middle))
        def _():
            far_recv[:, 3] = jnp.zeros((2, sz.own_in, sz.cols), sz.wire)


    cot[tail:] = jnp.zeros((16, sz.out), BF16)
    load_cot.wait()
    cot[0 : sz.real] = stage[1]
    load_biases.wait()
    load_mask.wait()
    item = lax.broadcasted_iota(jnp.int32, (sz.items, sz.out), 0)
    kept = jnp.zeros((sz.items, sz.out), F32)
    for n in range(sz.items):
        kept = jnp.where(item == n, mask[n].astype(F32), kept)
    keep[...] = kept

    one, two = sz.groups
    weights_on(0, far_steps)
    weights_out(1)
    gather_pass_on(0, frames, 0, whole)
    gather_here(0, frames, 0, whole)
    weights_here(0, 0)
    product(0, 0, frames, one)
    product(0, 0, frames, two)
    weights_on(1, far_steps[:1])
    weights_here(0, 1)
    product(0, 1, frames, one)
    finish_four(0, one[1] - 1)
    weights_on(1, far_steps[1:2])
    product(0, 1, frames, two)
    finish_four(one[1] - 1, sz.pieces)

    for p in all_pieces[:1]:
        gather_pass_on(1, acts, p, rows_of(p))
    weights_on(1, far_steps[2:])
    for p in all_pieces[1:]:
        gather_pass_on(1, acts, p, rows_of(p))
    for p in range(*one):
        gather_here(1, acts, p, rows_of(p))
    weights_here(1, 0)
    product(1, 0, acts, one)
    weights_here(1, 1)
    product(1, 1, acts, one)
    finish_five(0, one[1] - 1)
    for p in range(*two):
        gather_here(1, acts, p, rows_of(p))
    product(1, 0, acts, two)
    product(1, 1, acts, two)
    finish_five(one[1] - 1, sz.pieces)
    spread_delta(sz.pieces - 1)
    if sz.line and sz.tensor == sz.major:
        back_products(1, lambda: grads_place(1, acts, 3), second=lambda: grads_place(1, acts, 2))
    else:
        grads_half(1, acts, True)
        back_products(1)
    grads_far(1, far_half[0], shares[:1])
    grads_half(1, acts, False)
    grads_far(1, far_half[0], shares[1:])

    def delta_four(first, last):
        @pl.loop(first, last)
        def _(p):
            note_delta(0, p, (back_total(1, p) * slope4[rows_of(p)]).astype(BF16).astype(F32))
            pl.when(p > 0)(lambda: spread_delta(p - 1))

    if sz.line and sz.tensor == sz.major and sz.pieces > 2:
        early = sz.pieces - 2
        delta_four(0, sz.pieces - 1)
        grads_far(1, 2)
        for k in (3, 2):
            grads_product(0, frames, flip_bits(major, k), 1, 0, early)
        delta_four(sz.pieces - 1, sz.pieces)
        spread_delta(sz.pieces - 1)
        grads_place(0, frames, 3, early)
        grads_place(0, frames, 2, early)
    else:
        delta_four(0, sz.pieces)
        spread_delta(sz.pieces - 1)
        grads_half(0, frames, True)
        for k in far_half[1:]:
            grads_far(1, k)
    for k in near_half:
        grads_far(1, k)
    grads_half(0, frames, False)
    back_products(
        0,
        between=lambda: grads_far(0, far_half[0], shares[:1]),
        second=lambda: grads_far(0, far_half[0], shares[1:]),
    )
    for k in (*far_half[1:], *near_half):
        grads_far(0, k)
    act4_out[...] = acts[t, 0 : sz.real]
    act5_out[...] = act5[0 : sz.real]
    squares = grads_sum(1)
    grads_out_rows(1)

    @pl.loop(0, sz.pieces)
    def _(p):
        igrad[rows_of(p)] = back_total(0, p)

    igrad_out[...] = igrad[0 : sz.real]

    me = d * sz.tensor + t
    for l in (0, 1):
        stats_all[me, l + 1 : l + 2, :] = jnp.sum(bias_sum[l], axis=0, keepdims=True)
    squares += grads_sum(0)
    stats_all[me, 0:1, :] = jnp.sum(squares, axis=0, keepdims=True)
    def stats_copy(a, b, mine):
        device = (flip_bits(d, a), flip_bits(t, b))
        slot = me if mine else device[0] * sz.tensor + device[1]
        k = a * sz.tensor + b
        return same(stats_all.at[slot, 0:3], st_send.at[k], st_recv.at[k], device)

    others = [(a, b) for a in reversed(range(sz.dp)) for b in reversed(range(sz.tensor)) if a or b]
    for a, b in others:
        stats_copy(a, b, True).start()

    grads_out_rows(0)
    for l in (0, 1):
        weights_sent(l)
        for h in shares:
            for k in far_steps:
                far_copy(l, k, h).wait_send()
            for k in range(sz.major):
                near_copy(l, k, h).wait_send()

        @pl.loop(0, sz.pieces)
        def _(p):
            part_copy(l, p).wait_send()
            for k in cross_steps:
                cross_copy(l, p, k).wait_send()

    gather_sent(0, frames, 0, whole)

    @pl.loop(0, sz.pieces)
    def _(p):
        gather_sent(1, acts, p, rows_of(p))

    for a, b in others:
        stats_copy(a, b, False).wait_recv()

    for q in range(sz.tensor):
        total = stats_all[q, 0:3]
        for slot in range(q + sz.tensor, sz.devices, sz.tensor):
            total += stats_all[slot, 0:3]
        stats_out[q, 0:3] = total

    for a, b in others:
        stats_copy(a, b, True).wait_send()


def train_step(sz, frames, item_mask, weights, biases, cotangent):
    sem = pltpu.SemaphoreType.DMA
    vmem = pltpu.VMEM
    maps = (sz.span, sz.out)
    block = (sz.own_in, sz.cols)
    shapes = [
        vmem((2, sz.rows, sz.out), F32),
        vmem((2, sz.real, sz.out), BF16),
        vmem(maps, BF16),
        vmem((2, sz.chan), F32),
        pltpu.SMEM((sz.items,), jnp.int32),
        vmem((sz.items, sz.out), F32),
        vmem((2, sz.dp, *block), sz.wire),
        vmem((sz.tensor, *maps), BF16),
        vmem((sz.tensor, *maps), BF16),
        vmem((sz.span + 2 * sz.halo, sz.cols), F32),
        vmem((3, *maps), F32),
        vmem(maps, F32),
        vmem(maps, BF16),
        vmem((3, sz.span + 2 * sz.halo, sz.out), F32),
        vmem((sz.span, sz.cols), BF16),
        vmem((2, sz.pairs, *maps), BF16),
        vmem((2, sz.pairs, *maps), BF16),
        vmem((sz.pairs, *maps), F32),
        vmem((2, sz.pairs, *maps), BF16),
        vmem((2, sz.pairs, *maps), BF16),
        vmem(maps, F32),
        vmem((2, sz.dp, *block), F32),
        vmem((2, sz.major, *block), sz.wire),
        vmem((2, sz.major, *block), sz.wire),
        vmem((2, sz.major, *block), sz.wire),
        vmem((2, sz.major, *block), sz.wire),
        vmem((2, *block), sz.wire),
        vmem(block, F32),
        vmem((2, 8, sz.out), F32),
        vmem((sz.devices, 8, sz.out), F32),
        sem((6,)),
        pltpu.SemaphoreType.REGULAR,
        sem((2, sz.major, 2)),
        sem((2, sz.major, 2)),
        sem((2, 2)),
        sem((2, sz.major, 2)),
        sem((2, sz.major, 2)),
        sem((2, sz.pieces, sz.pairs)),
        sem((2, sz.pieces, sz.pairs)),
        sem((2, sz.pieces)),
        sem((2, sz.pieces)),
        sem((2, sz.pieces, sz.pairs)),
        sem((2, sz.pieces, sz.pairs)),
        sem((2, sz.pieces)),
        sem((2, sz.pieces)),
        sem((2, sz.pieces, sz.pairs)),
        sem((2, sz.pieces, sz.pairs)),
        sem((2, sz.major, sz.shares)),
        sem((2, sz.major, sz.shares)),
        sem((2, sz.major, sz.shares)),
        sem((2, sz.major, sz.shares)),
        sem((2, sz.shares)),
        sem((sz.devices,)),
        sem((sz.devices,)),
    ]
    macs = 6 * sz.real * TAPS * sz.chan * sz.out
    rows = (sz.real, sz.out)
    return pl.pallas_call(
        functools.partial(body, sz),
        out_shape=[
            vmem(rows, BF16),
            vmem(rows, BF16),
            vmem(rows, F32),
            vmem((2, sz.rows, sz.out), F32),
            vmem((sz.tensor, 8, sz.out), F32),
        ],
        in_specs=[pl.BlockSpec(memory_space=pltpu.HBM)] * 5,
        out_specs=[pl.BlockSpec(memory_space=vmem)] * 5,
        scratch_shapes=shapes,
        compiler_params=pltpu.CompilerParams(
            collective_id=0, has_side_effects=True, vmem_limit_bytes=sz.grant
        ),
        cost_estimate=pl.CostEstimate(flops=2 * macs, bytes_accessed=6_000_000, transcendentals=0),
        name="train_step",
    )(*(pltpu.with_memory_space_constraint(x, pltpu.HBM) for x in (frames, item_mask, weights, biases, cotangent)))


def finish_body(
    sz,
    act4,
    act5,
    igrad,
    grads,
    stats,
    weights,
    first,
    second,
    biases_ref,
    bias_first_ref,
    bias_second_ref,
    act4_out,
    act5_out,
    igrad_out,
    norm_out,
    weights_out,
    first_out,
    second_out,
    biases_out,
    bias_first_out,
    bias_second_out,
    olds,
    news,
    in_sem,
    out_sem,
    move_sem,
):
    targets = (weights_out, first_out, second_out)
    parts = [(l, pl.ds(r * sz.rows // 2, sz.rows // 2)) for l in (0, 1) for r in (0, 1)]
    if sz.rows % 16:
        parts = [(l, pl.ds(0, sz.rows)) for l in (0, 1)]
    stores = [
        [pltpu.make_async_copy(news.at[l, i, r], ref.at[l, r], out_sem.at[p, i]) for i, ref in enumerate(targets)]
        for p, (l, r) in enumerate(parts)
    ]
    moves = [
        pltpu.make_async_copy(held, ref, move_sem.at[i])
        for i, (held, ref) in enumerate(((act4, act4_out), (act5, act5_out), (igrad, igrad_out)))
    ]
    loads = [
        pltpu.make_async_copy(ref, olds.at[i], in_sem.at[i])
        for i, ref in enumerate((biases_ref, bias_first_ref, bias_second_ref))
    ]
    for copy in (*loads, *moves):
        copy.start()
    bias_grad = jnp.concatenate([stats[q, 1:3, :] for q in range(sz.tensor)], axis=1)
    squares = jnp.sum(stats[:, 0, :], axis=(0, 1), keepdims=True) + jnp.sum(
        bias_grad * bias_grad, axis=(0, 1), keepdims=True
    )
    grad_norm = jnp.sqrt(squares)
    factor = jnp.minimum(1.0, CLIP_NORM / (grad_norm + 1e-06))
    norm_out[...] = grad_norm
    for p, (l, r) in enumerate(parts):
        news[l, 0, r], news[l, 1, r], news[l, 2, r] = adam_update(
            weights[l, r], grads[l, r] * factor, first[l, r], second[l, r], RATE, DECAY
        )
        for copy in stores[p]:
            copy.start()
    for copy in loads:
        copy.wait()
    biases_out[...], bias_first_out[...], bias_second_out[...] = adam_update(
        olds[0], bias_grad * factor, olds[1], olds[2], BIAS_RATE, 0.0
    )
    for copy in (*moves, *(copy for part in stores for copy in part)):
        copy.wait()


def finish(sz, act4, act5, igrad, grads, stats, weights, first, second, biases, bias_first, bias_second):
    inside = pl.BlockSpec(memory_space=pltpu.VMEM)
    outside = pl.BlockSpec(memory_space=pltpu.HBM)
    like = lambda x: jax.ShapeDtypeStruct(x.shape, x.dtype)
    sem = pltpu.SemaphoreType.DMA
    held = [pltpu.with_memory_space_constraint(x, pltpu.VMEM) for x in (act4, act5, igrad, grads, stats, weights, first, second)]
    given = [pltpu.with_memory_space_constraint(x, pltpu.HBM) for x in (biases, bias_first, bias_second)]
    return pl.pallas_call(
        functools.partial(finish_body, sz),
        out_shape=[
            like(act4),
            like(act5),
            like(igrad),
            jax.ShapeDtypeStruct((1, 1), F32),
            like(weights),
            like(first),
            like(second),
            like(biases),
            like(bias_first),
            like(bias_second),
        ],
        in_specs=[inside] * 8 + [outside] * 3,
        out_specs=[outside] * 3 + [inside] + [outside] * 3 + [inside] * 3,
        scratch_shapes=[
            pltpu.VMEM((3, *biases.shape), F32),
            pltpu.VMEM((2, 3, sz.rows, sz.out), F32),
            sem((3,)),
            sem((4, 3)),
            sem((3,)),
        ],
        compiler_params=pltpu.CompilerParams(vmem_limit_bytes=8 * 1024 * 1024),
        cost_estimate=pl.CostEstimate(flops=5_000_000, bytes_accessed=7_000_000, transcendentals=0),
        name="clip_and_adamw",
    )(*held, *given)


def on_device(
    mesh,
    frames,
    item_mask,
    weights,
    biases,
    cotangent,
    weight_first,
    weight_second,
    bias_first,
    bias_second,
):
    sz = Sizes(mesh, frames.shape, weights.shape)

    def flat(maps):
        return jnp.transpose(maps, (1, 2, 0, 3)).reshape(sz.real, sz.out)

    def square(rows):
        return jnp.transpose(rows.reshape(sz.height, sz.width, sz.items, sz.out), (2, 0, 1, 3))

    made = train_step(sz, flat(frames), item_mask, weights, biases, flat(cotangent))
    act_four, act_five, input_grad, grad_norm, *rest = finish(
        sz, *made, weights, weight_first, weight_second, biases, bias_first, bias_second
    )
    return (square(act_four), square(act_five), square(input_grad), grad_norm.reshape(()), *rest)


def solution(mesh):
    split = P("dp", None, None, "tensor")
    rows = P(None, "dp", "tensor")
    in_specs = (split, P("dp"), rows, P(), split, rows, rows, P(), P())
    out_specs = (split, split, split, P(), rows, rows, rows, P(), P(), P())
    return jax.shard_map(
        functools.partial(on_device, mesh), mesh=mesh, in_specs=in_specs, out_specs=out_specs, check_vma=False
    )
```

```python
import functools
import math

import jax
import jax.numpy as jnp
from jax import lax
from jax.experimental import pallas as pl
from jax.experimental.pallas import tpu as pltpu
from jax.sharding import PartitionSpec as P

STEP = 5
CLIP_NORM = 1.0
BETA_ONE = 0.5
BETA_TWO = 0.5
RATE = 0.01
BIAS_RATE = 0.03
DECAY = 0.1
EPSILON = 1e-08

MESH = pl.DeviceIdType.MESH
BF16 = jnp.bfloat16
F32 = jnp.float32
ROOT = math.sqrt(2.0 / math.pi)
CUBE = 0.044715
TAPS = 9
WIDE = 512


def gelu_parts(value):
    square = value * value
    th = jnp.tanh(ROOT * value * (1.0 + CUBE * square))
    half = 0.5 * (1.0 + th)
    slope = half + 0.5 * value * (1.0 - th * th) * (ROOT * (1.0 + 3.0 * CUBE * square))
    return value * half, slope


def flip_bits(index, mask):
    bit = 1
    while bit <= mask:
        if mask & bit:
            index = index + bit - 2 * bit * lax.rem(lax.div(index, bit), 2)
        bit *= 2
    return index


def adam_update(param, grad, first, second, rate, decay):
    first_new = BETA_ONE * first + (1.0 - BETA_ONE) * grad
    second_new = BETA_TWO * second + (1.0 - BETA_TWO) * grad * grad
    corrected = first_new * (1.0 / (1.0 - BETA_ONE**STEP))
    scaled = jnp.sqrt(second_new * (1.0 / (1.0 - BETA_TWO**STEP))) + EPSILON
    return (param - rate * (corrected / scaled + decay * param), first_new, second_new)


class Sizes:
    def __init__(self, mesh, frames_shape, weights_shape):
        self.dp = mesh.shape["dp"]
        self.tensor = mesh.shape["tensor"]
        self.items, self.height, self.width, self.out = frames_shape
        self.chan = self.out * self.tensor
        self.rows = weights_shape[1]
        self.own_in = self.rows // TAPS
        self.cols = TAPS * self.out
        self.major = self.dp // 2
        self.pairs = self.tensor // 2
        self.slots = self.dp // self.tensor
        self.spots = self.height * self.width
        self.real = self.spots * self.items
        self.span = -(-self.real // 16) * 16
        self.halo = (self.width + 1) * self.items
        self.pieces = next(n for n in (5, 4, 3, 2, 1) if self.span // 16 % n == 0)
        self.piece = self.span // self.pieces
        self.groups = ((0, self.pieces // 2), (self.pieces // 2, self.pieces))
        self.wire = BF16 if self.own_in % 16 == 0 else F32
        self.line = self.major == 4
        self.far_order = (2, 1, 3) if self.line else tuple(range(1, self.major))
        cut = (TAPS + 1) // 2 * self.out
        self.parts = (((0, cut), (cut, self.cols)),) * 2
        self.devices = self.dp * self.tensor
        self.shares = 2 if self.own_in % 32 == 0 else 1
        self.share = self.own_in // self.shares
        self.grant = (44 if self.wire == BF16 else 54) * 1024 * 1024


def body(
    sz,
    frames_ref,
    mask_ref,
    weights_ref,
    biases_ref,
    cot_ref,
    act4_out,
    act5_out,
    igrad_out,
    grads_out,
    stats_out,
    w_in,
    stage,
    cot,
    biases,
    mask,
    keep,
    w_all,
    frames,
    acts,
    spread,
    edges,
    slope4,
    act5,
    shifted,
    deltas,
    part_send,
    part_recv,
    part_own,
    cross_send,
    cross_recv,
    igrad,
    kgrad,
    near_send,
    near_recv,
    far_send,
    far_recv,
    relay_recv,
    shard,
    bias_sum,
    stats_all,
    local_sem,
    ready,
    wz_send,
    wz_recv,
    wf_send,
    wy_send,
    wy_recv,
    ax_send,
    ax_recv,
    as_send,
    as_recv,
    af_send,
    af_recv,
    rs_send,
    rs_recv,
    rx_send,
    rx_recv,
    gy_send,
    gy_recv,
    gz_send,
    gz_recv,
    gr_recv,
    st_send,
    st_recv,
):
    d = lax.axis_index("dp")
    t = lax.axis_index("tensor")
    major, minor = lax.div(d, 2), lax.rem(d, 2)
    near = (2 * major + 1 - minor, t)
    pair, side = lax.div(t, 2), lax.rem(t, 2)
    sibling = (d, 2 * pair + 1 - side)

    def far_slot(k):
        return 2 * flip_bits(major, k) + minor

    def near_slot(k):
        return 2 * flip_bits(major, k) + 1 - minor

    def far(k):
        return (far_slot(k), t)

    def cross_rank(k):
        return 2 * lax.rem(pair + k, sz.pairs) + side

    def cross_from(k):
        return 2 * lax.rem(pair + sz.pairs - k, sz.pairs) + side

    def remote(src, dst, send, recv, device):
        return pltpu.make_async_remote_copy(
            src_ref=src, dst_ref=dst, send_sem=send, recv_sem=recv, device_id=device, device_id_type=MESH
        )

    def same(block, send, recv, device):
        return remote(block, block, send, recv, device)

    all_pieces = range(sz.pieces)

    def rows_of(p):
        return pl.ds(pl.multiple_of(p * sz.piece, 16), sz.piece)

    far_steps = range(1, sz.major)
    cross_steps = range(1, sz.pairs)
    middle = jnp.logical_and(major > 0, major < sz.major - 1)
    far_steps = range(1, sz.major)
    cross_steps = range(1, sz.pairs)
    signal = functools.partial(pl.semaphore_signal, inc=1, device_id_type=MESH)

    barrier = pltpu.get_barrier_semaphore()
    if sz.line:
        pl.when(major > 0)(lambda: signal(barrier, device_id=(d - 2, t)))
        pl.when(major < sz.major - 1)(lambda: signal(barrier, device_id=(d + 2, t)))
        joined = jnp.where(middle, 2, 1) + 1 + sz.pairs
    else:
        for k in far_steps:
            signal(barrier, device_id=far(k))
        joined = sz.major + sz.pairs
    signal(barrier, device_id=near)
    for k in cross_steps:
        signal(barrier, device_id=(d, cross_rank(k)))
    signal(barrier, device_id=sibling)

    load_w = [pltpu.make_async_copy(weights_ref.at[l], w_in.at[l], local_sem.at[l]) for l in (0, 1)]
    load_frames = pltpu.make_async_copy(frames_ref, stage.at[0], local_sem.at[2])
    load_cot = pltpu.make_async_copy(cot_ref, stage.at[1], local_sem.at[3])
    load_biases = pltpu.make_async_copy(biases_ref, biases, local_sem.at[4])
    load_mask = pltpu.make_async_copy(mask_ref, mask, local_sem.at[5])
    for copy in (load_w[0], load_frames, load_w[1], load_cot, load_biases, load_mask):
        copy.start()

    def parts_of(l):
        return range(len(sz.parts[l]))

    def weight_block(l, slot, part):
        first, last = sz.parts[l][part]
        return w_all.at[l, slot, :, first:last]

    def weight_out(l, k, part):
        return same(weight_block(l, d, part), wz_send.at[l, k, part], wz_recv.at[l, k, part], far(k))

    def weight_relay(l, part):
        return same(weight_block(l, far_slot(2), part), wf_send.at[l, part], wz_recv.at[l, 3, part], far(1))

    def weight_over(l, k, part):
        return same(weight_block(l, far_slot(k), part), wy_send.at[l, k, part], wy_recv.at[l, k, part], near)

    def weights_over(l, k):
        for part in parts_of(l):
            weight_over(l, k, part).start()

    def weights_out(l):
        for k in sz.far_order:
            for part in parts_of(l):
                if sz.line and k == 3:
                    pl.when(middle)(weight_out(l, k, part).start)
                else:
                    weight_out(l, k, part).start()

    def weights_on(l, steps):
        for k in steps:
            for part in parts_of(l):
                block = weight_block(l, far_slot(k), part)
                same(block, wz_send.at[l, k, part], wz_recv.at[l, k, part], far(k)).wait_recv()
                if sz.line and k == 2:
                    pl.when(middle)(weight_relay(l, part).start)
                weight_over(l, k, part).start()

    def weights_here(l, part):
        for k in range(sz.major):
            block = weight_block(l, near_slot(k), part)
            same(block, wy_send.at[l, k, part], wy_recv.at[l, k, part], near).wait_recv()

    def weights_sent(l):
        for k in range(sz.major):
            for part in parts_of(l):
                weight_over(l, k, part).wait_send()
                if sz.line and k == 3:

                    @pl.when(middle)
                    def _():
                        weight_out(l, k, part).wait_send()
                        weight_relay(l, part).wait_send()

                elif k:
                    weight_out(l, k, part).wait_send()

    def round_weights(l):
        load_w[l].wait()
        for tap in range(TAPS):
            w_all[l, d, :, tap * sz.out : (tap + 1) * sz.out] = w_in[
                l, pl.ds(tap, sz.own_in, stride=TAPS), :
            ].astype(sz.wire)

    def gather_sends(g, maps, p, rows):
        own = maps.at[t, rows]
        out = [same(own, ax_send.at[g, p, k], ax_recv.at[g, p, k], (d, cross_rank(k))) for k in cross_steps]
        out.append(same(own, as_send.at[g, p], as_recv.at[g, p], sibling))
        return out

    def gather_forward(g, maps, p, rows, k):
        return same(maps.at[cross_from(k), rows], af_send.at[g, p, k], af_recv.at[g, p, k], sibling)

    def gather_pass_on(g, maps, p, rows):
        for k in cross_steps:
            same(maps.at[cross_from(k), rows], ax_send.at[g, p, k], ax_recv.at[g, p, k], sibling).wait_recv()
            gather_forward(g, maps, p, rows, k).start()

    def gather_here(g, maps, p, rows):
        same(maps.at[sibling[1], rows], as_send.at[g, p], as_recv.at[g, p], sibling).wait_recv()
        for k in cross_steps:
            rank = 2 * lax.rem(pair + sz.pairs - k, sz.pairs) + 1 - side
            same(maps.at[rank, rows], af_send.at[g, p, k], af_recv.at[g, p, k], sibling).wait_recv()

    def gather_sent(g, maps, p, rows):
        for copy in gather_sends(g, maps, p, rows):
            copy.wait_send()
        for k in cross_steps:
            gather_forward(g, maps, p, rows, k).wait_send()

    whole = pl.ds(0, sz.span)

    def product(l, part, maps, group):
        rows = slice(group[0] * sz.piece, group[1] * sz.piece)
        left = jnp.concatenate([maps[q, rows] for q in range(sz.tensor)], axis=1)
        first, last = sz.parts[l][part]
        for start in range(first, last, WIDE):
            stop = min(start + WIDE, last)
            right = w_all[l, :, :, start:stop].reshape(sz.chan, stop - start).astype(BF16)
            spread[sz.halo + rows.start : sz.halo + rows.stop, start:stop] = jnp.dot(
                left, right, preferred_element_type=F32
            )

    def own_bias(l):
        return biases[l : l + 1, pl.ds(pl.multiple_of(t * sz.out, sz.out), sz.out)]

    def shifted_sum(p):
        sums = []
        for b in range(3):
            total = None
            for a in range(3):
                shift = sz.items * (sz.width * (a - 1) + b - 1)
                tap = 3 * a + b
                rows = pl.ds(pl.multiple_of(p * sz.piece + sz.halo + shift, 8), sz.piece)
                term = spread[rows, tap * sz.out : (tap + 1) * sz.out]
                total = term if total is None else total + term
            sums.append(total)
        return sums[1] + sums[0] * edges[0, rows_of(p)] + sums[2] * edges[1, rows_of(p)]

    def note_delta(l, p, delta):
        bias_sum[l] += jnp.sum(delta.reshape(sz.piece // 8, 8, sz.out), axis=0)
        rows = pl.ds(pl.multiple_of(p * sz.piece + sz.halo, 8), sz.piece)
        shifted[0, rows] = delta * edges[0, rows_of(p)]
        shifted[1, rows] = delta
        shifted[2, rows] = delta * edges[1, rows_of(p)]

    def spread_delta(p):
        for a in range(3):
            for b in range(3):
                shift = sz.items * (sz.width * (a - 1) + b - 1)
                tap = 3 * a + b
                rows = pl.ds(pl.multiple_of(p * sz.piece + sz.halo - shift, 8), sz.piece)
                deltas[rows_of(p), tap * sz.out : (tap + 1) * sz.out] = shifted[b, rows].astype(BF16)

    def finish_four(first, last):
        @pl.loop(first, last)
        def _(p):
            act, slope = gelu_parts(shifted_sum(p) + own_bias(0))
            acts[t, rows_of(p)] = (act * edges[2, rows_of(p)]).astype(BF16)
            slope4[rows_of(p)] = slope * edges[2, rows_of(p)]
            for copy in gather_sends(1, acts, p, rows_of(p)):
                copy.start()

    def by_item(value):
        return (value.reshape(sz.piece // sz.items, sz.items, sz.out) * keep[...]).reshape(sz.piece, sz.out)

    def finish_five(first, last):
        @pl.loop(first, last)
        def _(p):
            act, slope = gelu_parts(shifted_sum(p) + own_bias(1))
            act5[rows_of(p)] = by_item(act).astype(BF16)
            delta = (by_item(cot[rows_of(p)].astype(F32)) * slope).astype(BF16).astype(F32)
            note_delta(1, p, delta)
            pl.when(p > 0)(lambda: spread_delta(p - 1))

    def part_copy(l, p):
        rows = rows_of(p)
        return remote(
            part_send.at[l, :, rows], part_recv.at[l, :, rows], rs_send.at[l, p], rs_recv.at[l, p], sibling
        )

    def cross_copy(l, p, k):
        rows = rows_of(p)
        return remote(
            cross_send.at[l, k, rows],
            cross_recv.at[l, k, rows],
            rx_send.at[l, p, k],
            rx_recv.at[l, p, k],
            (d, cross_rank(k)),
        )

    def back_product(l, group, which):
        blocks = [
            w_all[l, pl.ds((2 * j + which) * sz.slots, sz.slots)].reshape(sz.out, sz.cols) for j in range(sz.pairs)
        ]
        right = jnp.concatenate(blocks, axis=0).astype(BF16)
        left = deltas[group[0] * sz.piece : group[1] * sz.piece]
        out = lax.dot_general(left, right, (((1,), (1,)), ((), ())), preferred_element_type=F32)
        return [out[:, j * sz.out : (j + 1) * sz.out] for j in range(sz.pairs)]

    def back_to_sibling(l, group):
        rows = slice(group[0] * sz.piece, group[1] * sz.piece)
        for j, block in enumerate(back_product(l, group, 1 - side)):
            part_send[l, j, rows] = block.astype(BF16)
        for p in range(*group):
            part_copy(l, p).start()

    def back_own(l, group):
        rows = slice(group[0] * sz.piece, group[1] * sz.piece)
        for j, block in enumerate(back_product(l, group, side)):
            part_own[j, rows] = block

    def back_across(l, group):
        @pl.loop(*group)
        def _(p):
            part_copy(l, p).wait_recv()
            for k in cross_steps:
                j = lax.rem(pair + k, sz.pairs)
                total = part_own[j, rows_of(p)] + part_recv[l, j, rows_of(p)].astype(F32)
                cross_send[l, k, rows_of(p)] = total.astype(BF16)
                cross_copy(l, p, k).start()

    def back_products(l, first=None, between=None, second=None):
        nothing_else = lambda: None
        for group, meanwhile, then in zip(sz.groups, (first, second), (between, None)):
            back_to_sibling(l, group)
            (meanwhile or nothing_else)()
            back_own(l, group)
            back_across(l, group)
            (then or nothing_else)()

    def back_total(l, p):
        total = part_own[pair, rows_of(p)] + part_recv[l, pair, rows_of(p)].astype(F32)
        for k in cross_steps:
            cross_copy(l, p, k).wait_recv()
            total += cross_recv[l, k, rows_of(p)].astype(F32)
        return total

    shares = range(sz.shares)

    def share_of(h):
        return slice(h * sz.share, (h + 1) * sz.share)

    def near_copy(l, k, h):
        return remote(
            near_send.at[l, k, share_of(h)],
            near_recv.at[l, k, share_of(h)],
            gy_send.at[l, k, h],
            gy_recv.at[l, k, h],
            near,
        )

    def far_copy(l, k, h):
        return remote(
            far_send.at[l, k, share_of(h)],
            far_recv.at[l, k, share_of(h)],
            gz_send.at[l, k, h],
            gz_recv.at[l, k, h],
            far(k),
        )

    half = sz.tensor // 2
    far_half = [k for k in reversed(far_steps) if k >= sz.major // 2]
    near_half = [k for k in far_steps if k < sz.major // 2]

    def grads_product(l, maps, block, width, first, last):
        rows = slice(first * sz.piece, last * sz.piece)
        left = jnp.concatenate([maps[block + q, rows] for q in range(width)], axis=1)
        into = pl.ds(block * sz.slots, width * sz.slots)
        for start in range(0, sz.cols, WIDE):
            stop = min(start + WIDE, sz.cols)
            product = lax.dot_general(
                left, deltas[rows, start:stop], (((0,), (0,)), ((), ())), preferred_element_type=F32
            ).reshape(width * sz.slots, sz.own_in, stop - start)
            if first:
                product += kgrad[l, into, :, start:stop]
            kgrad[l, into, :, start:stop] = product

    def grads_block(l, maps, block, width, steps, first=0):
        grads_product(l, maps, block, width, first, sz.pieces)
        for k in steps:
            near_send[l, k] = kgrad[l, near_slot(k)].astype(sz.wire)
            for h in shares:
                near_copy(l, k, h).start()

    own_half = lax.div(major, sz.major // 2)

    def grads_half(l, maps, other):
        first = (1 - own_half if other else own_half) * half
        grads_block(l, maps, first, half, far_half if other else [*near_half, 0])

    def grads_place(l, maps, k, first=0):
        grads_block(l, maps, flip_bits(major, k), 1, [k], first)

    def relay_copy(l, h):
        rows = share_of(h)
        return remote(
            far_send.at[l, 3, rows], relay_recv.at[l, rows], gz_send.at[l, 3, h], gr_recv.at[l, h], far(1)
        )

    def grads_far(l, k, some=shares):
        for h in some:
            rows = share_of(h)
            near_copy(l, k, h).wait_recv()
            total = kgrad[l, far_slot(k), rows] + near_recv[l, k, rows].astype(F32)
            if sz.line and k == 2:

                @pl.when(middle)
                def _():
                    relay_copy(l, h).wait_recv()
                    far_send[l, k, rows] = (total + relay_recv[l, rows].astype(F32)).astype(sz.wire)

                @pl.when(jnp.logical_not(middle))
                def _():
                    far_send[l, k, rows] = total.astype(sz.wire)

            else:
                far_send[l, k, rows] = total.astype(sz.wire)
            if sz.line and k == 3:
                pl.when(middle)(far_copy(l, k, h).start)
                pl.when(jnp.logical_not(middle))(relay_copy(l, h).start)
            else:
                far_copy(l, k, h).start()

    def grads_sum(l):
        for h in shares:
            near_copy(l, 0, h).wait_recv()
            for k in far_steps:
                if sz.line and k == 3:
                    pl.when(middle)(far_copy(l, k, h).wait_recv)
                else:
                    far_copy(l, k, h).wait_recv()
        total = kgrad[l, d] + near_recv[l, 0].astype(F32)
        for k in far_steps:
            total += far_recv[l, k].astype(F32)
        shard[...] = total
        squares = jnp.sum((total * total).reshape(sz.own_in // 8, 8, sz.cols), axis=0)
        return sum(squares[:, tap * sz.out : (tap + 1) * sz.out] for tap in range(TAPS))

    def grads_out_rows(l):
        for tap in range(TAPS):
            grads_out[l, pl.ds(tap, sz.own_in, stride=TAPS), :] = shard[:, tap * sz.out : (tap + 1) * sz.out]

    round_weights(0)
    pl.semaphore_wait(barrier, joined)
    if sz.line:

        @pl.when(middle)
        def _():
            signal(ready, device_id=(d - 2, t))
            signal(ready, device_id=(d + 2, t))

    weights_over(0, 0)
    tail = sz.span - 16
    frames[t, tail:] = jnp.zeros((16, sz.out), BF16)
    load_frames.wait()
    frames[t, 0 : sz.real] = stage[0]
    for copy in gather_sends(0, frames, 0, whole):
        copy.start()
    round_weights(1)
    weights_over(1, 0)
    if sz.line:
        pl.semaphore_wait(ready, 1)
    weights_out(0)

    rest = sz.halo + sz.span
    for first in (0, rest):
        spread[first : first + sz.halo, :] = jnp.zeros((sz.halo, sz.cols), F32)
        shifted[:, first : first + sz.halo, :] = jnp.zeros((3, sz.halo, sz.out), F32)
    edges[...] = jnp.ones_like(edges)
    nothing = jnp.zeros((sz.items, sz.out), F32)
    for i in range(sz.height):
        for e, j in ((0, 0), (1, sz.width - 1)):
            first = (i * sz.width + j) * sz.items
            edges[e, first : first + sz.items, :] = nothing
    edges[2, sz.real :, :] = jnp.zeros((sz.span - sz.real, sz.out), F32)
    bias_sum[...] = jnp.zeros_like(bias_sum)
    if sz.line:

        @pl.when(jnp.logical_not(middle))
        def _():
            far_recv[:, 3] = jnp.zeros((2, sz.own_in, sz.cols), sz.wire)


    cot[tail:] = jnp.zeros((16, sz.out), BF16)
    load_cot.wait()
    cot[0 : sz.real] = stage[1]
    load_biases.wait()
    load_mask.wait()
    item = lax.broadcasted_iota(jnp.int32, (sz.items, sz.out), 0)
    kept = jnp.zeros((sz.items, sz.out), F32)
    for n in range(sz.items):
        kept = jnp.where(item == n, mask[n].astype(F32), kept)
    keep[...] = kept

    one, two = sz.groups
    weights_on(0, far_steps)
    weights_out(1)
    gather_pass_on(0, frames, 0, whole)
    gather_here(0, frames, 0, whole)
    weights_here(0, 0)
    product(0, 0, frames, one)
    product(0, 0, frames, two)
    weights_on(1, far_steps[:1])
    weights_here(0, 1)
    product(0, 1, frames, one)
    finish_four(0, one[1] - 1)
    weights_on(1, far_steps[1:2])
    product(0, 1, frames, two)
    finish_four(one[1] - 1, sz.pieces)

    for p in all_pieces[:1]:
        gather_pass_on(1, acts, p, rows_of(p))
    weights_on(1, far_steps[2:])
    for p in all_pieces[1:]:
        gather_pass_on(1, acts, p, rows_of(p))
    for p in range(*one):
        gather_here(1, acts, p, rows_of(p))
    weights_here(1, 0)
    product(1, 0, acts, one)
    weights_here(1, 1)
    product(1, 1, acts, one)
    finish_five(0, one[1] - 1)
    for p in range(*two):
        gather_here(1, acts, p, rows_of(p))
    product(1, 0, acts, two)
    product(1, 1, acts, two)
    finish_five(one[1] - 1, sz.pieces)
    spread_delta(sz.pieces - 1)
    if sz.line and sz.tensor == sz.major:
        back_products(1, lambda: grads_place(1, acts, 3), second=lambda: grads_place(1, acts, 2))
    else:
        grads_half(1, acts, True)
        back_products(1)
    grads_far(1, far_half[0], shares[:1])
    grads_half(1, acts, False)
    grads_far(1, far_half[0], shares[1:])

    def delta_four(first, last):
        @pl.loop(first, last)
        def _(p):
            note_delta(0, p, (back_total(1, p) * slope4[rows_of(p)]).astype(BF16).astype(F32))
            pl.when(p > 0)(lambda: spread_delta(p - 1))

    if sz.line and sz.tensor == sz.major and sz.pieces > 2:
        early = sz.pieces - 2
        delta_four(0, sz.pieces - 1)
        grads_far(1, 2)
        for k in (3, 2):
            grads_product(0, frames, flip_bits(major, k), 1, 0, early)
        delta_four(sz.pieces - 1, sz.pieces)
        spread_delta(sz.pieces - 1)
        grads_place(0, frames, 3, early)
        grads_place(0, frames, 2, early)
    else:
        delta_four(0, sz.pieces)
        spread_delta(sz.pieces - 1)
        grads_half(0, frames, True)
        for k in far_half[1:]:
            grads_far(1, k)
    for k in near_half:
        grads_far(1, k)
    grads_half(0, frames, False)
    back_products(
        0,
        between=lambda: grads_far(0, far_half[0], shares[:1]),
        second=lambda: grads_far(0, far_half[0], shares[1:]),
    )
    for k in (*far_half[1:], *near_half):
        grads_far(0, k)
    act4_out[...] = acts[t, 0 : sz.real]
    act5_out[...] = act5[0 : sz.real]
    squares = grads_sum(1)
    grads_out_rows(1)

    @pl.loop(0, sz.pieces)
    def _(p):
        igrad[rows_of(p)] = back_total(0, p)

    igrad_out[...] = igrad[0 : sz.real]

    me = d * sz.tensor + t
    for l in (0, 1):
        stats_all[me, l + 1 : l + 2, :] = jnp.sum(bias_sum[l], axis=0, keepdims=True)
    squares += grads_sum(0)
    stats_all[me, 0:1, :] = jnp.sum(squares, axis=0, keepdims=True)
    def stats_copy(a, b, mine):
        device = (flip_bits(d, a), flip_bits(t, b))
        slot = me if mine else device[0] * sz.tensor + device[1]
        k = a * sz.tensor + b
        return same(stats_all.at[slot, 0:3], st_send.at[k], st_recv.at[k], device)

    others = [(a, b) for a in reversed(range(sz.dp)) for b in reversed(range(sz.tensor)) if a or b]
    for a, b in others:
        stats_copy(a, b, True).start()

    grads_out_rows(0)
    for l in (0, 1):
        weights_sent(l)
        for h in shares:
            for k in far_steps:
                far_copy(l, k, h).wait_send()
            for k in range(sz.major):
                near_copy(l, k, h).wait_send()

        @pl.loop(0, sz.pieces)
        def _(p):
            part_copy(l, p).wait_send()
            for k in cross_steps:
                cross_copy(l, p, k).wait_send()

    gather_sent(0, frames, 0, whole)

    @pl.loop(0, sz.pieces)
    def _(p):
        gather_sent(1, acts, p, rows_of(p))

    for a, b in others:
        stats_copy(a, b, False).wait_recv()

    for q in range(sz.tensor):
        total = stats_all[q, 0:3]
        for slot in range(q + sz.tensor, sz.devices, sz.tensor):
            total += stats_all[slot, 0:3]
        stats_out[q, 0:3] = total

    for a, b in others:
        stats_copy(a, b, True).wait_send()


def train_step(sz, frames, item_mask, weights, biases, cotangent):
    sem = pltpu.SemaphoreType.DMA
    vmem = pltpu.VMEM
    maps = (sz.span, sz.out)
    block = (sz.own_in, sz.cols)
    shapes = [
        vmem((2, sz.rows, sz.out), F32),
        vmem((2, sz.real, sz.out), BF16),
        vmem(maps, BF16),
        vmem((2, sz.chan), F32),
        pltpu.SMEM((sz.items,), jnp.int32),
        vmem((sz.items, sz.out), F32),
        vmem((2, sz.dp, *block), sz.wire),
        vmem((sz.tensor, *maps), BF16),
        vmem((sz.tensor, *maps), BF16),
        vmem((sz.span + 2 * sz.halo, sz.cols), F32),
        vmem((3, *maps), F32),
        vmem(maps, F32),
        vmem(maps, BF16),
        vmem((3, sz.span + 2 * sz.halo, sz.out), F32),
        vmem((sz.span, sz.cols), BF16),
        vmem((2, sz.pairs, *maps), BF16),
        vmem((2, sz.pairs, *maps), BF16),
        vmem((sz.pairs, *maps), F32),
        vmem((2, sz.pairs, *maps), BF16),
        vmem((2, sz.pairs, *maps), BF16),
        vmem(maps, F32),
        vmem((2, sz.dp, *block), F32),
        vmem((2, sz.major, *block), sz.wire),
        vmem((2, sz.major, *block), sz.wire),
        vmem((2, sz.major, *block), sz.wire),
        vmem((2, sz.major, *block), sz.wire),
        vmem((2, *block), sz.wire),
        vmem(block, F32),
        vmem((2, 8, sz.out), F32),
        vmem((sz.devices, 8, sz.out), F32),
        sem((6,)),
        pltpu.SemaphoreType.REGULAR,
        sem((2, sz.major, 2)),
        sem((2, sz.major, 2)),
        sem((2, 2)),
        sem((2, sz.major, 2)),
        sem((2, sz.major, 2)),
        sem((2, sz.pieces, sz.pairs)),
        sem((2, sz.pieces, sz.pairs)),
        sem((2, sz.pieces)),
        sem((2, sz.pieces)),
        sem((2, sz.pieces, sz.pairs)),
        sem((2, sz.pieces, sz.pairs)),
        sem((2, sz.pieces)),
        sem((2, sz.pieces)),
        sem((2, sz.pieces, sz.pairs)),
        sem((2, sz.pieces, sz.pairs)),
        sem((2, sz.major, sz.shares)),
        sem((2, sz.major, sz.shares)),
        sem((2, sz.major, sz.shares)),
        sem((2, sz.major, sz.shares)),
        sem((2, sz.shares)),
        sem((sz.devices,)),
        sem((sz.devices,)),
    ]
    macs = 6 * sz.real * TAPS * sz.chan * sz.out
    rows = (sz.real, sz.out)
    return pl.pallas_call(
        functools.partial(body, sz),
        out_shape=[
            vmem(rows, BF16),
            vmem(rows, BF16),
            vmem(rows, F32),
            vmem((2, sz.rows, sz.out), F32),
            vmem((sz.tensor, 8, sz.out), F32),
        ],
        in_specs=[pl.BlockSpec(memory_space=pltpu.HBM)] * 5,
        out_specs=[pl.BlockSpec(memory_space=vmem)] * 5,
        scratch_shapes=shapes,
        compiler_params=pltpu.CompilerParams(
            collective_id=0, has_side_effects=True, vmem_limit_bytes=sz.grant
        ),
        cost_estimate=pl.CostEstimate(flops=2 * macs, bytes_accessed=6_000_000, transcendentals=0),
        name="train_step",
    )(*(pltpu.with_memory_space_constraint(x, pltpu.HBM) for x in (frames, item_mask, weights, biases, cotangent)))


def finish_body(
    sz,
    act4,
    act5,
    igrad,
    grads,
    stats,
    weights,
    first,
    second,
    biases_ref,
    bias_first_ref,
    bias_second_ref,
    act4_out,
    act5_out,
    igrad_out,
    norm_out,
    weights_out,
    first_out,
    second_out,
    biases_out,
    bias_first_out,
    bias_second_out,
    olds,
    news,
    in_sem,
    out_sem,
    move_sem,
):
    targets = (weights_out, first_out, second_out)
    parts = [(l, pl.ds(r * sz.rows // 2, sz.rows // 2)) for l in (0, 1) for r in (0, 1)]
    if sz.rows % 16:
        parts = [(l, pl.ds(0, sz.rows)) for l in (0, 1)]
    stores = [
        [pltpu.make_async_copy(news.at[l, i, r], ref.at[l, r], out_sem.at[p, i]) for i, ref in enumerate(targets)]
        for p, (l, r) in enumerate(parts)
    ]
    moves = [
        pltpu.make_async_copy(held, ref, move_sem.at[i])
        for i, (held, ref) in enumerate(((act4, act4_out), (act5, act5_out), (igrad, igrad_out)))
    ]
    loads = [
        pltpu.make_async_copy(ref, olds.at[i], in_sem.at[i])
        for i, ref in enumerate((biases_ref, bias_first_ref, bias_second_ref))
    ]
    for copy in (*loads, *moves):
        copy.start()
    bias_grad = jnp.concatenate([stats[q, 1:3, :] for q in range(sz.tensor)], axis=1)
    squares = jnp.sum(stats[:, 0, :], axis=(0, 1), keepdims=True) + jnp.sum(
        bias_grad * bias_grad, axis=(0, 1), keepdims=True
    )
    grad_norm = jnp.sqrt(squares)
    factor = jnp.minimum(1.0, CLIP_NORM / (grad_norm + 1e-06))
    norm_out[...] = grad_norm
    for p, (l, r) in enumerate(parts):
        news[l, 0, r], news[l, 1, r], news[l, 2, r] = adam_update(
            weights[l, r], grads[l, r] * factor, first[l, r], second[l, r], RATE, DECAY
        )
        for copy in stores[p]:
            copy.start()
    for copy in loads:
        copy.wait()
    biases_out[...], bias_first_out[...], bias_second_out[...] = adam_update(
        olds[0], bias_grad * factor, olds[1], olds[2], BIAS_RATE, 0.0
    )
    for copy in (*moves, *(copy for part in stores for copy in part)):
        copy.wait()


def finish(sz, act4, act5, igrad, grads, stats, weights, first, second, biases, bias_first, bias_second):
    inside = pl.BlockSpec(memory_space=pltpu.VMEM)
    outside = pl.BlockSpec(memory_space=pltpu.HBM)
    like = lambda x: jax.ShapeDtypeStruct(x.shape, x.dtype)
    sem = pltpu.SemaphoreType.DMA
    held = [pltpu.with_memory_space_constraint(x, pltpu.VMEM) for x in (act4, act5, igrad, grads, stats, weights, first, second)]
    given = [pltpu.with_memory_space_constraint(x, pltpu.HBM) for x in (biases, bias_first, bias_second)]
    return pl.pallas_call(
        functools.partial(finish_body, sz),
        out_shape=[
            like(act4),
            like(act5),
            like(igrad),
            jax.ShapeDtypeStruct((1, 1), F32),
            like(weights),
            like(first),
            like(second),
            like(biases),
            like(bias_first),
            like(bias_second),
        ],
        in_specs=[inside] * 8 + [outside] * 3,
        out_specs=[outside] * 3 + [inside] + [outside] * 3 + [inside] * 3,
        scratch_shapes=[
            pltpu.VMEM((3, *biases.shape), F32),
            pltpu.VMEM((2, 3, sz.rows, sz.out), F32),
            sem((3,)),
            sem((4, 3)),
            sem((3,)),
        ],
        compiler_params=pltpu.CompilerParams(vmem_limit_bytes=8 * 1024 * 1024),
        cost_estimate=pl.CostEstimate(flops=5_000_000, bytes_accessed=7_000_000, transcendentals=0),
        name="clip_and_adamw",
    )(*held, *given)


def on_device(
    mesh,
    frames,
    item_mask,
    weights,
    biases,
    cotangent,
    weight_first,
    weight_second,
    bias_first,
    bias_second,
):
    sz = Sizes(mesh, frames.shape, weights.shape)

    def flat(maps):
        return jnp.transpose(maps, (1, 2, 0, 3)).reshape(sz.real, sz.out)

    def square(rows):
        return jnp.transpose(rows.reshape(sz.height, sz.width, sz.items, sz.out), (2, 0, 1, 3))

    made = train_step(sz, flat(frames), item_mask, weights, biases, flat(cotangent))
    act_four, act_five, input_grad, grad_norm, *rest = finish(
        sz, *made, weights, weight_first, weight_second, biases, bias_first, bias_second
    )
    return (square(act_four), square(act_five), square(input_grad), grad_norm.reshape(()), *rest)


def solution(mesh):
    split = P("dp", None, None, "tensor")
    rows = P(None, "dp", "tensor")
    in_specs = (split, P("dp"), rows, P(), split, rows, rows, P(), P())
    out_specs = (split, split, split, P(), rows, rows, rows, P(), P(), P())
    return jax.shard_map(
        functools.partial(on_device, mesh), mesh=mesh, in_specs=in_specs, out_specs=out_specs, check_vma=False
    )
```
